32 devices in a mesh: dp: 8 (over y, x, core), fsdp: 4 (over z).
Axes of the slice: x: 2, y: 2, z: 4, core: 2. Of those that a mesh axis runs over, the one named last changes fastest.
Arguments:
- tokens: bfloat16 [2, 32, 256, 1536], P(None, ('dp', 'fsdp')), may hold values from -6 to 6
- w_query: bfloat16 [1536, 1536], P(('dp', 'fsdp')), may hold values from -0.3125 to 0.3125
- w_keyval: bfloat16 [1536, 512], P(('dp', 'fsdp')), may hold values from -0.15625 to 0.15625
- w_out: bfloat16 [1536, 1536], P(('dp', 'fsdp')), may hold values from -1.25 to 1.25
- w_gate: bfloat16 [1536, 4608], P(('dp', 'fsdp')), may hold values from -0.15625 to 0.15625
- w_up: bfloat16 [1536, 4608], P(('dp', 'fsdp')), may hold values from -0.15625 to 0.15625
- w_down: bfloat16 [4608, 1536], P(('dp', 'fsdp')), may hold values from -0.09375 to 0.09375
- gain_attn: bfloat16 [1536], P(('dp', 'fsdp')), may hold values from 0.5 to 1.5
- gain_ffn: bfloat16 [1536], P(('dp', 'fsdp')), may hold values from 0.5 to 1.5
- cotangent: bfloat16 [2, 32, 256, 1536], P(None, ('dp', 'fsdp')), may hold values from -6 to 6
- block_perm: int32 [2, 32], replicated, may hold values from 0 to 31, each once within a row
- extra_len: int32 [2, 4], replicated, may hold values from 1 to 3073, 4100 in all within a row
Outputs:
- block_out: bfloat16 [2, 32, 256, 1536], P(None, ('dp', 'fsdp'))
- grad_tokens: bfloat16 [2, 32, 256, 1536], P(None, ('dp', 'fsdp'))
- grad_query: float32 [1536, 1536], P(('dp', 'fsdp'))
- grad_keyval: float32 [1536, 512], P(('dp', 'fsdp'))
- grad_out: float32 [1536, 1536], P(('dp', 'fsdp'))
- grad_gate: float32 [1536, 4608], P(('dp', 'fsdp'))
- grad_up: float32 [1536, 4608], P(('dp', 'fsdp'))
- grad_down: float32 [4608, 1536], P(('dp', 'fsdp'))
- grad_gain_attn: float32 [1536], P(('dp', 'fsdp'))
- grad_gain_ffn: float32 [1536], P(('dp', 'fsdp'))
The draws below stay inside these ranges and needn't reach their ends.
Inputs may be any that keep to these rules, and one draw needn't show every extreme that they name: Each row of block_perm names every block of its micro-batch once. `extra_len`: each row sums to 8192 - 4 * (1023) and has an entry equal to 3073.
All inputs are finite; a program needn't handle non-finite values.
Results may differ from the reference program's by a relative error of at most 0.015.
The reference program's roundings to bfloat16 on the way count: a program that leaves them out, or rounds other values in their place, can miss the bound.
Values may be sent and summed in bfloat16 or wider, within the bound.
A program may use at most 320 MiB of HBM per device.

```python
import math
import jax
import jax.numpy as jnp
import numpy as np
from jax import lax

D = 1536
H = 6
HD = 256
FF = 4608
WIN = 1024
BLK = 256
MB = 2
NBLK = 32
TOK_MB = 8192
NSEQ = 4
LONGEST = 4096
NSRC = 4


def level_of(own_key, shape, pieces, smallest, largest):
    level = 1.0
    for position, parts in pieces:
        draws = jax.random.uniform(jax.random.fold_in(jax.random.fold_in(own_key, 6), position), (parts,), jnp.float32, smallest / len(pieces), largest / len(pieces))
        level = level * jnp.repeat(jnp.exp(draws), shape[position] // parts).reshape((-1,) + (1,) * (len(shape) - 1 - position))
    return level


def length_profile(count, total, limit, slope):
    weights = [(1 << 20) // math.isqrt(rank ** slope) + 1 for rank in range(2, count + 1)]
    spare, given = total - limit - (count - 1), [1] * (count - 1)
    while spare > 0:
        candidates = [i for i in range(count - 1) if given[i] < limit]
        pool, left = sum([weights[i] for i in candidates]), spare
        for i in candidates:
            more = min(limit - given[i], max(1, left * weights[i] // pool), spare)
            given[i] = given[i] + more
            spare = spare - more
    return np.array([limit] + given)


def uneven_parts(stream_key, count, total, limit, lean):
    if count == 2:
        one = jax.random.randint(stream_key, (), max(1, total - limit), min(limit, total - 1) + 1)
        return jnp.stack([one, total - one])
    sizes = jnp.asarray(length_profile(count, total, limit, lean), jnp.int32)
    couples = (count - 1) // 2
    donor, taker = sizes[1:1 + 2 * couples:2], sizes[2:2 + 2 * couples:2]
    room = jnp.minimum(donor - 1, limit - taker)
    shifted = jax.random.randint(jax.random.fold_in(stream_key, 1), (couples,), 0, 1 << 20) % (room + 1)
    sizes = sizes.at[1:1 + 2 * couples:2].set(donor - shifted).at[2:2 + 2 * couples:2].set(taker + shifted)
    return sizes[jax.random.permutation(jax.random.fold_in(stream_key, 2), count)]


def noise(key, shape, deviation, most, pieces=(), kind=jnp.bfloat16):
    level = level_of(key, shape, pieces, -0.22, 0.18) if pieces else 1.0
    array = jax.random.normal(key, shape, jnp.float32) * deviation * level
    return jnp.minimum(jnp.maximum(array, -most), most).astype(kind)


def setup_inputs(seed: int = 0) -> dict:
    seeds = jax.random.split(jax.random.key(seed), 13)
    return {
        "tokens": noise(seeds[0], (MB, NBLK, BLK, D), 1.0, 6.0, ((1, 32),)),
        "w_query": noise(seeds[1], (D, H * HD), (D // 4) ** -0.5, 0.3125, ((0, 32),)),
        "w_keyval": noise(seeds[2], (D, 2 * HD), D ** -0.5, 0.15625, ((0, 32),)),
        "w_out": noise(seeds[3], (H * HD, D), (max(1, H * HD // 64)) ** -0.5, 1.25, ((0, 32),)),
        "w_gate": noise(seeds[4], (D, FF), D ** -0.5, 0.15625, ((0, 32),)),
        "w_up": noise(seeds[5], (D, FF), D ** -0.5, 0.15625, ((0, 32),)),
        "w_down": noise(seeds[6], (FF, D), FF ** -0.5, 0.09375, ((0, 32),)),
        "gain_attn": jnp.clip(1.0 + 0.1 * jax.random.normal(seeds[7], (D,), jnp.float32), 0.5, 1.5).astype(jnp.bfloat16),
        "gain_ffn": jnp.clip(1.0 + 0.1 * jax.random.normal(seeds[8], (D,), jnp.float32), 0.5, 1.5).astype(jnp.bfloat16),
        "cotangent": noise(seeds[9], (MB, NBLK, BLK, D), 1.0, 6.0, ((1, 32),)),
        "block_perm": jax.vmap(lambda own: jax.random.permutation(own, NBLK))(jax.random.split(seeds[10], MB)).reshape((MB, NBLK)).astype(jnp.int32),
        "extra_len": jax.vmap(lambda own: uneven_parts(own, NSEQ, TOK_MB - NSEQ * (WIN - 1), LONGEST - WIN + 1, 2))(jax.random.split(seeds[11], MB)).reshape((MB, NSEQ)).astype(jnp.int32),
    }


@jax.custom_vjp
def low(v):
    return lax.optimization_barrier(v.astype(jnp.bfloat16)).astype(jnp.float32)

@jax.custom_vjp
def low_back(v):
    return v

def low_keep(v):
    return (low(v), None)

def low_pass(kept, grad):
    return (grad,)

def back_keep(v):
    return (v, None)

def back_low(kept, grad):
    return (low(grad),)
low.defvjp(low_keep, low_pass)
low_back.defvjp(back_keep, back_low)
EPS = 1e-06
HIGH = lax.Precision.HIGHEST

def norm_rows(value, gain):
    inverse = lax.rsqrt(lax.optimization_barrier(jnp.mean(value * value, axis=-1, keepdims=True)) + EPS)
    return value * inverse * gain

def sequence_of(positions, ends):
    return lax.optimization_barrier(jnp.sum((positions[:, None] >= ends[None, :]).astype(jnp.int32), axis=1))

def visible_mask(query_pos, key_pos, ends):
    same = sequence_of(query_pos, ends)[:, None] == sequence_of(key_pos, ends)[None, :]
    gap = query_pos[:, None] - key_pos[None, :]
    return same & (gap >= 0) & (gap < WIN) & (key_pos[None, :] >= 0)

def attend_block(query, keys, values, query_pos, key_pos, ends):
    scores = low_back(jnp.dot(query, keys.T, precision=HIGH))
    mask = jnp.repeat(visible_mask(query_pos, key_pos, ends), H, axis=0)
    masked = jnp.where(mask, scores, -1e+30)
    top = lax.optimization_barrier(jnp.max(masked, axis=1, keepdims=True))
    expd = jnp.exp(masked - top)
    probs = expd / lax.optimization_barrier(jnp.sum(expd, axis=1, keepdims=True))
    return jnp.dot(low(probs), values, precision=HIGH)

def forward(x, wq, wkv, wo, wg, wu, wd, g1, g2, ends):
    scale = HD ** (-0.5)
    n1 = low(norm_rows(x, g1))
    query = low(low_back(jnp.dot(n1, wq, precision=HIGH) * scale))
    keyval = low(low_back(jnp.dot(n1, wkv, precision=HIGH)))
    margin = NSRC * BLK
    padded = jnp.concatenate([jnp.zeros((margin, 2 * HD), jnp.float32), keyval], axis=0)
    nblocks = x.shape[0] // BLK

    def one_block(index):
        start = index * BLK
        qb = lax.dynamic_slice_in_dim(query, start, BLK, 0).reshape(BLK * H, HD)
        kvb = lax.dynamic_slice_in_dim(padded, start, (NSRC + 1) * BLK, 0)
        qpos = start + jnp.arange(BLK, dtype=jnp.int32)
        kpos = start - margin + jnp.arange((NSRC + 1) * BLK, dtype=jnp.int32)
        out = attend_block(qb, kvb[:, :HD], kvb[:, HD:], qpos, kpos, ends)
        return out.reshape(BLK, H * HD)
    att = lax.map(jax.checkpoint(one_block), jnp.arange(nblocks, dtype=jnp.int32))
    att = att.reshape(nblocks * BLK, H * HD)
    mixed = x + low_back(jnp.dot(low(low_back(att)), wo, precision=HIGH))
    n2 = low(norm_rows(mixed, g2))
    gate = low_back(jnp.dot(n2, wg, precision=HIGH))
    up = low_back(jnp.dot(n2, wu, precision=HIGH))
    hidden = low(jax.nn.gelu(gate, approximate=True) * up)
    return mixed + jnp.dot(hidden, wd, precision=HIGH)

def reference(tokens, w_query, w_keyval, w_out, w_gate, w_up, w_down, gain_attn, gain_ffn, cotangent, block_perm, extra_len):
    weights = tuple((w.astype(jnp.float32) for w in (w_query, w_keyval, w_out, w_gate, w_up, w_down, gain_attn, gain_ffn)))
    width = tokens.shape[-1]

    def per_batch(totals, batch):
        x_blocks, dy_blocks, perm_row, extra_row = batch
        ends = jnp.cumsum(extra_row + (WIN - 1)).astype(jnp.int32)
        x_orig = jnp.zeros(x_blocks.shape, jnp.float32).at[perm_row].set(x_blocks.astype(jnp.float32))
        dy_orig = jnp.zeros(dy_blocks.shape, jnp.float32).at[perm_row].set(dy_blocks.astype(jnp.float32))
        x_flat = x_orig.reshape(-1, width)
        dy_flat = dy_orig.reshape(-1, width)

        def apply(x, *ws):
            return forward(x, *ws, ends)
        out, pull = jax.vjp(apply, x_flat, *weights)
        grads = pull(dy_flat)
        out_blocks = out.reshape(x_blocks.shape)[perm_row].astype(jnp.bfloat16)
        dx_blocks = grads[0].reshape(x_blocks.shape)[perm_row].astype(jnp.bfloat16)
        totals = tuple((t + g for t, g in zip(totals, grads[1:])))
        return (totals, (out_blocks, dx_blocks))
    zeros = tuple((jnp.zeros(w.shape, jnp.float32) for w in weights))
    totals, (outs, dxs) = lax.scan(per_batch, zeros, (tokens, cotangent, block_perm, extra_len))
    return (outs, dxs, totals[0], totals[1], totals[2], totals[3], totals[4], totals[5], totals[6], totals[7])
```

```python
import functools
import math

import jax
import jax.numpy as jnp
from jax import lax
from jax.experimental import pallas as pl
from jax.experimental.pallas import tpu as pltpu
from jax.sharding import PartitionSpec as P

H = 6
HD = 256
WIN = 1024
BLK = 256


EPS = 1e-06
VMEM = 60 * 1024 * 1024


def for_sending(x):
    return jax.tree.map(lambda a: a.astype(jnp.bfloat16) if a.dtype == jnp.float32 else a, x)


def shifted(value, axis, steps):
    count = lax.axis_size(axis)
    leading, last = (max(0, -steps), min(count, count - steps))
    return lax.ppermute(value, axis, [(source, source + steps) for source in range(leading, last)])


def norm_rows(value, gain):
    inverse = lax.rsqrt(jnp.mean(value * value, axis=-1, keepdims=True) + EPS)
    return (value * inverse * gain, inverse)


def norm_back(value, inverse, gain, grad):
    scaled = grad * gain
    width = value.shape[-1]
    dvalue = (
        inverse * scaled
        - value * inverse**3 * jnp.sum(scaled * value, axis=-1, keepdims=True) / width
    )
    dgain = jnp.sum(grad * value * inverse, axis=0)
    return (dvalue, dgain)


def sequence_of(positions, ends):
    return jnp.sum((positions[:, None] >= ends[None, :]).astype(jnp.int32), axis=1)


def visible_mask(query_pos, key_pos, ends):
    same = sequence_of(query_pos, ends)[:, None] == sequence_of(key_pos, ends)[None, :]
    gap = query_pos[:, None] - key_pos[None, :]
    return same & (gap >= 0) & (gap < WIN) & (key_pos[None, :] >= 0)


def geglu(gate, up):
    return jax.nn.gelu(gate, approximate=True) * up


def move_keys(value, order, count):
    rows = value.shape[0]
    spread = lax.all_to_all(value, ("dp", "fsdp"), split_axis=1, concat_axis=0, tiled=True)
    pieces = spread.reshape(count, rows, spread.shape[1])
    placed = jnp.take(pieces, order, axis=0).reshape(count * rows, spread.shape[1])
    return lax.all_to_all(placed, ("dp", "fsdp"), split_axis=0, concat_axis=1, tiled=True)


def move_grads(value, order, count):
    rows = value.shape[0]
    spread = lax.all_to_all(
        for_sending(value), ("dp", "fsdp"), split_axis=1, concat_axis=0, tiled=True
    ).astype(value.dtype)
    pieces = spread.reshape(count, rows, spread.shape[1])
    placed = jnp.take(pieces, order, axis=0).reshape(count * rows, spread.shape[1])
    return lax.all_to_all(
        for_sending(placed), ("dp", "fsdp"), split_axis=0, concat_axis=1, tiled=True
    ).astype(placed.dtype)


def body(
    tokens,
    w_query,
    w_keyval,
    w_out,
    w_gate,
    w_up,
    w_down,
    gain_attn,
    gain_ffn,
    cotangent,
    block_perm,
    extra_len,
):
    count = lax.axis_size(("dp", "fsdp"))
    me = lax.axis_index(("dp", "fsdp"))
    batches = tokens.shape[0]
    sources = WIN // BLK + 1
    scale = HD ** (-0.5)
    shards = (w_query, w_keyval, w_out, w_gate, w_up, w_down, gain_attn, gain_ffn)
    device_ids = jnp.arange(count, dtype=jnp.int32)
    totals = None
    outputs = []
    input_grads = []
    for batch in range(batches):
        full = (
            lax.all_gather(shards[0], ("dp", "fsdp"), axis=0, tiled=True),
            lax.all_gather(shards[1], ("dp", "fsdp"), axis=0, tiled=True),
            lax.all_gather(shards[2], ("dp", "fsdp"), axis=0, tiled=True),
            lax.all_gather(shards[3], ("dp", "fsdp"), axis=0, tiled=True),
            lax.all_gather(shards[4], ("dp", "fsdp"), axis=0, tiled=True),
            lax.all_gather(shards[5], ("dp", "fsdp"), axis=0, tiled=True),
            lax.all_gather(shards[6], ("dp", "fsdp"), axis=0, tiled=True),
            lax.all_gather(shards[7], ("dp", "fsdp"), axis=0, tiled=True),
        )
        wq, wkv, wo, wg, wu, wd, g1b, g2b = full
        g1 = g1b.astype(jnp.float32)
        g2 = g2b.astype(jnp.float32)
        perm_row = block_perm[batch]
        ends = jnp.cumsum(extra_len[batch] + (WIN - 1))
        mine = lax.dynamic_slice_in_dim(perm_row, me, 1)[0]
        holder = jnp.sum(
            jnp.where(perm_row[None, :] == device_ids[:, None], device_ids[None, :], 0), axis=1
        )
        query_pos = mine * BLK + jnp.arange(BLK, dtype=jnp.int32)
        key_pos = (mine - (sources - 1)) * BLK + jnp.arange(sources * BLK, dtype=jnp.int32)
        mask = jnp.repeat(visible_mask(query_pos, key_pos, ends), H, axis=0)
        x = tokens[batch, 0].astype(jnp.float32)
        n1, r1 = norm_rows(x, g1)
        n1b = n1.astype(jnp.bfloat16)
        query = (jnp.dot(n1b, wq, preferred_element_type=jnp.float32) * scale).astype(jnp.bfloat16)
        query_rows = query.reshape(BLK * H, HD)
        keyval = jnp.dot(n1b, wkv, preferred_element_type=jnp.float32).astype(jnp.bfloat16)
        ordered = move_keys(keyval, holder, count)
        window = [ordered] * sources
        for back in range(1, sources):
            window[sources - 1 - back] = shifted(ordered, ("dp", "fsdp"), back)
        picked = move_keys(jnp.concatenate(window, axis=0), perm_row, count)
        keys_src = picked[:, :HD]
        values_src = picked[:, HD:]
        scores = jnp.einsum("qd,kd->qk", query_rows, keys_src, preferred_element_type=jnp.float32)
        masked = jnp.where(mask, scores, -1e30)
        top = jnp.max(masked, axis=1, keepdims=True)
        expd = jnp.exp(masked - top)
        rowsum = jnp.sum(expd, axis=1, keepdims=True)
        lse = top + jnp.log(rowsum)
        probs_low = (expd / rowsum).astype(jnp.bfloat16)
        att = jnp.dot(probs_low, values_src, preferred_element_type=jnp.float32)
        att_low = att.reshape(BLK, H * HD).astype(jnp.bfloat16)
        mixed = x + jnp.dot(att_low, wo, preferred_element_type=jnp.float32)
        n2, r2 = norm_rows(mixed, g2)
        n2b = n2.astype(jnp.bfloat16)
        gate = jnp.dot(n2b, wg, preferred_element_type=jnp.float32)
        up = jnp.dot(n2b, wu, preferred_element_type=jnp.float32)
        hidden = geglu(gate, up).astype(jnp.bfloat16)
        outputs.append(
            (mixed + jnp.dot(hidden, wd, preferred_element_type=jnp.float32)).astype(jnp.bfloat16)
        )
        wq, wkv, wo, wg, wu, wd, g1b, g2b = (
            lax.all_gather(shards[0], ("dp", "fsdp"), axis=0, tiled=True),
            lax.all_gather(shards[1], ("dp", "fsdp"), axis=0, tiled=True),
            lax.all_gather(shards[2], ("dp", "fsdp"), axis=0, tiled=True),
            lax.all_gather(shards[3], ("dp", "fsdp"), axis=0, tiled=True),
            lax.all_gather(shards[4], ("dp", "fsdp"), axis=0, tiled=True),
            lax.all_gather(shards[5], ("dp", "fsdp"), axis=0, tiled=True),
            lax.all_gather(shards[6], ("dp", "fsdp"), axis=0, tiled=True),
            lax.all_gather(shards[7], ("dp", "fsdp"), axis=0, tiled=True),
        )
        dy = cotangent[batch, 0]
        d_down = jnp.einsum("tf,td->fd", hidden, dy, preferred_element_type=jnp.float32)
        d_hidden = jnp.einsum("td,fd->tf", dy, wd, preferred_element_type=jnp.float32)
        _, geglu_pull = jax.vjp(geglu, gate, up)
        d_gate, d_up = geglu_pull(d_hidden)
        d_gate_low = d_gate.astype(jnp.bfloat16)
        d_up_low = d_up.astype(jnp.bfloat16)
        d_wgate = jnp.einsum("td,tf->df", n2b, d_gate_low, preferred_element_type=jnp.float32)
        d_wup = jnp.einsum("td,tf->df", n2b, d_up_low, preferred_element_type=jnp.float32)
        d_n2 = jnp.einsum("tf,df->td", d_gate_low, wg, preferred_element_type=jnp.float32)
        d_n2 = d_n2 + jnp.einsum("tf,df->td", d_up_low, wu, preferred_element_type=jnp.float32)
        d_mixed_norm, d_g2 = norm_back(mixed, r2, g2, d_n2)
        d_mixed = dy.astype(jnp.float32) + d_mixed_norm
        d_branch = d_mixed.astype(jnp.bfloat16)
        d_wout = jnp.einsum("ta,td->ad", att_low, d_branch, preferred_element_type=jnp.float32)
        d_att = jnp.einsum("td,ad->ta", d_branch, wo, preferred_element_type=jnp.float32)
        d_att_rows = d_att.astype(jnp.bfloat16).reshape(BLK * H, HD)
        again = jnp.einsum("qd,kd->qk", query_rows, keys_src, preferred_element_type=jnp.float32)
        probs = jnp.exp(jnp.where(mask, again, -1e30) - lse)
        d_probs = jnp.einsum(
            "qd,kd->qk", d_att_rows, values_src, preferred_element_type=jnp.float32
        )
        delta = jnp.sum(probs * d_probs, axis=1, keepdims=True)
        d_scores = (probs * (d_probs - delta)).astype(jnp.bfloat16)
        d_query = jnp.dot(d_scores, keys_src, preferred_element_type=jnp.float32).astype(
            jnp.bfloat16
        )
        d_query = d_query.reshape(BLK, H * HD)
        d_keys = jnp.einsum("qk,qd->kd", d_scores, query_rows, preferred_element_type=jnp.float32)
        d_values = jnp.einsum(
            "qk,qd->kd", probs.astype(jnp.bfloat16), d_att_rows, preferred_element_type=jnp.float32
        )
        d_keyval_flat = jnp.concatenate([d_keys, d_values], axis=1)
        ordered_grads = move_grads(d_keyval_flat, holder, count).reshape(sources, BLK, 2 * HD)
        summed = ordered_grads[sources - 1]
        for back in range(1, sources):
            summed = summed + shifted(
                ordered_grads[sources - 1 - back].astype(jnp.bfloat16), ("dp", "fsdp"), -back
            ).astype(jnp.float32)
        d_keyval = move_grads(summed, perm_row, count).astype(jnp.bfloat16)
        d_wquery = jnp.einsum("td,ta->da", n1b, d_query, preferred_element_type=jnp.float32) * scale
        d_wkeyval = jnp.einsum("td,tc->dc", n1b, d_keyval, preferred_element_type=jnp.float32)
        d_n1 = jnp.einsum("ta,da->td", d_query, wq, preferred_element_type=jnp.float32) * scale
        d_n1 = d_n1 + jnp.einsum("tc,dc->td", d_keyval, wkv, preferred_element_type=jnp.float32)
        d_x_norm, d_g1 = norm_back(x, r1, g1, d_n1)
        input_grads.append((d_mixed + d_x_norm).astype(jnp.bfloat16))
        local = (d_wquery, d_wkeyval, d_wout, d_wgate, d_wup, d_down, d_g1, d_g2)
        totals = local if totals is None else tuple((a + b for a, b in zip(totals, local)))
    totals = lax.psum_scatter(totals, ("dp", "fsdp"), scatter_dimension=0, tiled=True)
    block_out = jnp.stack(outputs)[:, None]
    grad_tokens = jnp.stack(input_grads)[:, None]
    return (
        block_out,
        grad_tokens,
        totals[0],
        totals[1],
        totals[2],
        totals[3],
        totals[4],
        totals[5],
        totals[6],
        totals[7],
    )


MESH = pl.DeviceIdType.MESH

class Place:
    def __init__(self, grid):
        self.A, self.B, self.C, self.Z = grid
        dp = lax.axis_index("dp")
        self.z = lax.axis_index("fsdp")
        self.c = dp % 2
        self.x = (dp // 2) % 2
        self.y = dp // 4
    def dev(self, y=None, x=None, c=None, z=None):
        y = self.y if y is None else y
        x = self.x if x is None else x
        c = self.c if c is None else c
        z = self.z if z is None else z
        return ((y * 2 + x) * 2 + c, z)

def barrier(p):
    sem = pltpu.get_barrier_semaphore()
    peers = [p.dev(c=1 - p.c), p.dev(x=1 - p.x), p.dev(y=1 - p.y)] + [p.dev(z=(p.z + i) % p.Z) for i in range(1, p.Z)]
    for q in peers:
        pl.semaphore_signal(sem, inc=1, device_id=q, device_id_type=MESH)
    pl.semaphore_wait(sem, len(peers))

class Gather:
    COPIES = 12
    def __init__(self, p, src, dst, rows, cols, send, recv, local):
        self.p, self.dst, self.send, self.recv, self.local = p, dst, send, recv, local
        self.src = src.at[pl.ds(*rows), pl.ds(*cols)]
        self.r = pl.ds(*rows)
        self.all = pl.ds(*cols)
        half = (cols[1] // 256) * 128 if cols[1] > 128 else 128
        half = cols[1] - half if cols[1] - half >= half else half
        self.h = [pl.ds(cols[0], half), pl.ds(cols[0] + half, cols[1] - half)] if cols[1] > 128 else None
    def copy(self, k, src, dst, dev):
        return pltpu.make_async_remote_copy(src, dst, self.send.at[k], self.recv.at[k], device_id=dev, device_id_type=MESH)
    def own(self):
        p = self.p
        return pltpu.make_async_copy(self.src, self.dst.at[p.y, p.x, p.c, p.z, self.r, self.all], self.local)
    def zs(self):
        p = self.p
        out = []
        for i in range(1, p.Z):
            out.append((self.copy(i - 1, self.src, self.dst.at[p.y, p.x, p.c, p.z, self.r, self.all], p.dev(z=(p.z + i) % p.Z)),
                        self.dst.at[p.y, p.x, p.c, (p.z + p.Z - i) % p.Z, self.r, self.all]))
        return [a for a, _ in out]
    def same(self, k, ref, dev):
        return self.copy(k, ref, ref, dev)
    def p1(self):
        p, d = self.p, self.dst
        return [self.same(3, d.at[p.y, p.x, p.c, :, self.r, self.h[0]], p.dev(x=1 - p.x)),
                self.same(4, d.at[p.y, p.x, p.c, :, self.r, self.h[1]], p.dev(y=1 - p.y))]
    def p2(self):
        p, d = self.p, self.dst
        return [self.same(5, d.at[p.y, :, p.c, :, self.r, self.h[0]], p.dev(y=1 - p.y)),
                self.same(6, d.at[:, p.x, p.c, :, self.r, self.h[1]], p.dev(x=1 - p.x))]
    def c0(self):
        p, d = self.p, self.dst
        return [self.same(7, d.at[p.y, p.x, p.c, :, self.r, self.all], p.dev(c=1 - p.c))]
    def c1(self):
        p, d = self.p, self.dst
        o = p.dev(c=1 - p.c)
        return [self.same(8, d.at[p.y, 1 - p.x, p.c, :, self.r, self.h[0]], o),
                self.same(9, d.at[1 - p.y, p.x, p.c, :, self.r, self.h[1]], o)]
    def c2(self):
        p, d = self.p, self.dst
        o = p.dev(c=1 - p.c)
        return [self.same(10, d.at[1 - p.y, :, p.c, :, self.r, self.h[0]], o),
                self.same(11, d.at[:, 1 - p.x, p.c, :, self.r, self.h[1]], o)]

def start(cs):
    for c in cs: c.start()
def wait_recv(cs):
    for c in cs: c.wait_recv()
def wait_send(cs):
    for c in cs: c.wait_send()

def gather_kernel(grid, units, nin, *refs):
    ins, outs = refs[:nin], refs[nin:2 * nin]
    send, recv, local = refs[2 * nin:]
    p = Place(grid)
    barrier(p)
    U = len(units)
    gs = [Gather(p, ins[i], outs[i], rows, cols, send.at[u], recv.at[u], local.at[u]) for u, (i, rows, cols) in enumerate(units)]
    for s in range(U + 4):
        if s < U:
            gs[s].own().start(); start(gs[s].zs())
        if 0 <= s - 1 < U:
            g = gs[s - 1]; g.own().wait(); wait_recv(g.zs()); start(g.p1()); start(g.c0())
        if 0 <= s - 2 < U:
            g = gs[s - 2]; wait_recv(g.p1()); start(g.p2()); start(g.c1())
        if 0 <= s - 3 < U:
            g = gs[s - 3]; wait_recv(g.p2()); start(g.c2())
        if 0 <= s - 4 < U:
            g = gs[s - 4]
            wait_recv(g.c0() + g.c1() + g.c2())
            wait_send(g.zs() + g.p1() + g.p2() + g.c0() + g.c1() + g.c2())

def gather(grid, shards, units, collective_id):
    n = len(shards)
    outs = pl.pallas_call(
        functools.partial(gather_kernel, grid, units, n),
        out_shape=[jax.ShapeDtypeStruct(tuple(grid) + s.shape, s.dtype) for s in shards],
        in_specs=[pl.BlockSpec(memory_space=pl.ANY)] * n,
        out_specs=[pl.BlockSpec(memory_space=pl.ANY)] * n,
        scratch_shapes=[pltpu.SemaphoreType.DMA((len(units), 12)), pltpu.SemaphoreType.DMA((len(units), 12)), pltpu.SemaphoreType.DMA((len(units),))],
        compiler_params=pltpu.CompilerParams(collective_id=collective_id, has_side_effects=True),
        name="gather",
    )(*shards)
    return [o.reshape(-1, s.shape[-1]) for o, s in zip(outs, shards)]

class Scatter:
    def __init__(self, p, u, slot, src, out, rows, cols, bufs, sems):
        self.p, self.u, self.slot = p, u, slot
        self.rb0, self.rb1, self.rb2, self.rb3, self.own, self.fin = bufs
        self.send, self.recv, self.lsem = sems
        self.src, self.out = src, out
        self.r, self.cols = pl.ds(*rows), pl.ds(*cols)
        w = cols[1]
        half = w - (w // 256) * 128
        self.w, self.h = w, [pl.ds(0, half), pl.ds(half, w - half)]
        self.hs = [half, w - half]
        self.R = rows[1]
        self.rows, self.colsl = rows, cols
        self.all = pl.ds(0, w)
        self.P = self.own.at[slot]
    def copy(self, k, src, dst, dev):
        return pltpu.make_async_remote_copy(src, dst, self.send.at[self.u, k], self.recv.at[self.u, k], device_id=dev, device_id_type=MESH)
    def r0(self):
        p = self.p
        return [self.copy(0, self.src.at[:, :, 1 - p.c, :, self.r, self.cols], self.rb0.at[self.u, :, :, :, :, self.all], p.dev(c=1 - p.c))]
    def load_own(self):
        p = self.p
        return pltpu.make_async_copy(self.src.at[:, :, p.c, :, self.r, self.cols], self.P.at[..., self.all], self.lsem.at[self.u, 0])
    def load_r0(self, tmp):
        return pltpu.make_async_copy(self.rb0.at[self.u, :, :, :, :, self.all], tmp.at[..., self.all], self.lsem.at[self.u, 1])
    def add0(self, tmp):
        P, w, Z = self.P, self.w, self.p.Z
        @pl.loop(0, P.shape[0] * P.shape[1] * Z)
        def _(i):
            a, b, d = i // (P.shape[1] * Z), (i // Z) % P.shape[1], i % Z
            P[a, b, d, :, pl.ds(0, w)] = (P[a, b, d, :, pl.ds(0, w)].astype(jnp.float32) + tmp[a, b, d, :, pl.ds(0, w)].astype(jnp.float32)).astype(jnp.bfloat16)
    def r1(self):
        p, P = self.p, self.P
        return [self.copy(1, P.at[1 - p.y, :, :, :, self.h[0]], self.rb1.at[self.u, 0, :, :, :, pl.ds(0, self.hs[0])], p.dev(y=1 - p.y)),
                self.copy(2, P.at[:, 1 - p.x, :, :, self.h[1]], self.rb1.at[self.u, 1, :, :, :, pl.ds(0, self.hs[1])], p.dev(x=1 - p.x))]
    def add1(self):
        p, P, Z = self.p, self.P, self.p.Z
        @pl.loop(0, 2 * Z)
        def _(i):
            b, d = i // Z, i % Z
            P[p.y, b, d, :, self.h[0]] = (P[p.y, b, d, :, self.h[0]].astype(jnp.float32) + self.rb1[self.u, 0, b, d, :, pl.ds(0, self.hs[0])].astype(jnp.float32)).astype(jnp.bfloat16)
            P[b, p.x, d, :, self.h[1]] = (P[b, p.x, d, :, self.h[1]].astype(jnp.float32) + self.rb1[self.u, 1, b, d, :, pl.ds(0, self.hs[1])].astype(jnp.float32)).astype(jnp.bfloat16)
    def r2(self):
        p, P = self.p, self.P
        return [self.copy(3, P.at[p.y, 1 - p.x, :, :, self.h[0]], self.rb2.at[self.u, :, :, self.h[0]], p.dev(x=1 - p.x)),
                self.copy(4, P.at[1 - p.y, p.x, :, :, self.h[1]], self.rb2.at[self.u, :, :, self.h[1]], p.dev(y=1 - p.y))]
    def add2(self):
        p, P, Z = self.p, self.P, self.p.Z
        @pl.loop(0, Z)
        def _(d):
            P[p.y, p.x, d, :, self.all] = (P[p.y, p.x, d, :, self.all].astype(jnp.float32) + self.rb2[self.u, d, :, self.all].astype(jnp.float32)).astype(jnp.bfloat16)
    def r3(self):
        p, P = self.p, self.P
        return [self.copy(4 + i, P.at[p.y, p.x, (p.z + i) % p.Z, :, self.all], self.rb3.at[self.u, i - 1, :, self.all], p.dev(z=(p.z + i) % p.Z)) for i in range(1, p.Z)]
    def add3(self, f):
        p, P = self.p, self.P
        s = P[p.y, p.x, p.z, :, self.all].astype(jnp.float32)
        for i in range(p.Z - 1):
            s = s + self.rb3[self.u, i, :, self.all].astype(jnp.float32)
        self.fin[f, :, self.all] = s
    def store(self, f):
        return pltpu.make_async_copy(self.fin.at[f, :, self.all], self.out.at[pl.ds(*self.rows), self.cols], self.lsem.at[self.u, 2])

def scatter_kernel(grid, units, nin, *refs):
    ins, outs = refs[:nin], refs[nin:2 * nin]
    rb0 = refs[2 * nin]
    rb1, rb2, rb3, own, tmp, fin, send, recv, lsem = refs[2 * nin + 1:]
    p = Place(grid)
    barrier(p)
    U, NS = len(units), own.shape[0]
    gs = [Scatter(p, u, u % NS, ins[i], outs[i], rows, cols, (rb0, rb1, rb2, rb3, own, fin), (send, recv, lsem)) for u, (i, rows, cols) in enumerate(units)]
    for s in range(U + 5):
        if s < U:
            g = gs[s]
            start(g.r0())
            if s >= NS:
                pass
            g.load_own().start()
        if 0 <= s - 1 < U:
            g = gs[s - 1]; t = tmp
            wait_recv(g.r0()); g.load_r0(t).start(); g.load_own().wait(); g.load_r0(t).wait(); g.add0(t); start(g.r1())
        if 0 <= s - 2 < U:
            g = gs[s - 2]; wait_recv(g.r1()); wait_send(g.r1()); g.add1(); start(g.r2())
        if 0 <= s - 3 < U:
            g = gs[s - 3]; wait_recv(g.r2()); wait_send(g.r2()); g.add2(); start(g.r3())
        if 0 <= s - 4 < U:
            g = gs[s - 4]; wait_recv(g.r3()); wait_send(g.r0() + g.r3())
            f = (s - 4) % 2
            if s - 6 >= 0:
                gs[s - 6].store(f).wait()
            g.add3(f); g.store(f).start()
    for u in range(max(0, U - 2), U):
        gs[u].store(u % 2).wait()

def scatter(grid, fulls, units, collective_id):
    n = len(fulls)
    A, B, C, Z = grid
    ndev = A * B * C * Z
    U = len(units)
    shards = [(f.shape[0] // ndev, f.shape[1]) for f in fulls]
    W = max(c[1] for _, _, c in units)
    R = units[0][1][1]
    NS = 5
    outs = pl.pallas_call(
        functools.partial(scatter_kernel, grid, units, n),
        out_shape=[jax.ShapeDtypeStruct(s, jnp.float32) for s in shards] + [jax.ShapeDtypeStruct((U, A, B, Z, R, W), jnp.bfloat16)],
        in_specs=[pl.BlockSpec(memory_space=pl.ANY)] * n,
        out_specs=[pl.BlockSpec(memory_space=pl.ANY)] * (n + 1),
        scratch_shapes=[
            pltpu.VMEM((U, 2, 2, Z, R, W - (W // 256) * 128), jnp.bfloat16),
            pltpu.VMEM((U, Z, R, W), jnp.bfloat16),
            pltpu.VMEM((U, Z - 1, R, W), jnp.bfloat16),
            pltpu.VMEM((NS, A, B, Z, R, W), jnp.bfloat16),
            pltpu.VMEM((A, B, Z, R, W), jnp.bfloat16),
            pltpu.VMEM((2, R, W), jnp.float32),
            pltpu.SemaphoreType.DMA((U, 8)), pltpu.SemaphoreType.DMA((U, 8)), pltpu.SemaphoreType.DMA((U, 3))],
        compiler_params=pltpu.CompilerParams(collective_id=collective_id, has_side_effects=True, vmem_limit_bytes=60 * 1024 * 1024),
        name="scatter",
    )(*[f.reshape(tuple(grid) + (s[0], s[1])) for f, s in zip(fulls, shards)])
    return outs[:n]


def window_mask(start, ends, nseq, m, queries, keys):
    qpos = start + lax.broadcasted_iota(jnp.int32, (queries, 1), 0)
    first = jnp.maximum(qpos - (WIN - 1), 0)
    for k in range(nseq):
        end = ends[m, k]
        first = jnp.maximum(first, jnp.where(qpos >= end, end, 0))
    kpos = start - (keys - queries) + lax.broadcasted_iota(jnp.int32, (1, keys), 1)
    return (kpos >= first) & (kpos <= qpos)


def softmax_rows(q, k, mask):
    scores = lax.dot_general(q, k, (((1,), (1,)), ((), ())), preferred_element_type=jnp.float32)
    masked = jnp.where(mask, scores, -1e30)
    expd = jnp.exp(masked - jnp.max(masked, axis=1, keepdims=True))
    return expd * (1.0 / jnp.sum(expd, axis=1, keepdims=True))


def attend_kernel(nseq, start, ends, q_ref, kv_ref, o_ref):
    m = pl.program_id(0)
    mask = window_mask(start[m], ends, nseq, m, q_ref.shape[0], kv_ref.shape[1])
    p = softmax_rows(q_ref[...], kv_ref[0, :, :HD], mask)
    o_ref[...] = jnp.dot(p.astype(jnp.bfloat16), kv_ref[0, :, HD:], preferred_element_type=jnp.float32).astype(jnp.bfloat16)


def attend(q, window, start, ends):
    batches, keys, _ = window.shape
    return pl.pallas_call(
        functools.partial(attend_kernel, ends.shape[1]),
        out_shape=jax.ShapeDtypeStruct(q.shape, jnp.bfloat16),
        grid_spec=pltpu.PrefetchScalarGridSpec(
            num_scalar_prefetch=2,
            grid=(batches, H),
            in_specs=[
                pl.BlockSpec((BLK, HD), lambda m, h, *_: (m, h)),
                pl.BlockSpec((1, keys, 2 * HD), lambda m, h, *_: (m, 0, 0)),
            ],
            out_specs=pl.BlockSpec((BLK, HD), lambda m, h, *_: (m, h)),
        ),
        compiler_params=pltpu.CompilerParams(vmem_limit_bytes=VMEM),
        name="attend",
    )(start, ends, q, window)


def attend_back_kernel(nseq, start, ends, q_ref, kv_ref, d_ref, dq_ref, dkv_ref, dkv):
    m, h = pl.program_id(0), pl.program_id(1)
    mask = window_mask(start[m], ends, nseq, m, q_ref.shape[0], kv_ref.shape[1])
    q, k, v, d = q_ref[...], kv_ref[0, :, :HD], kv_ref[0, :, HD:], d_ref[...]
    p = softmax_rows(q, k, mask)
    dp = lax.dot_general(d, v, (((1,), (1,)), ((), ())), preferred_element_type=jnp.float32)
    ds = (p * (dp - jnp.sum(p * dp, axis=1, keepdims=True))).astype(jnp.bfloat16)
    dq_ref[...] = jnp.dot(ds, k, preferred_element_type=jnp.float32).astype(jnp.bfloat16)
    dk = lax.dot_general(ds, q, (((0,), (0,)), ((), ())), preferred_element_type=jnp.float32)
    dv = lax.dot_general(p.astype(jnp.bfloat16), d, (((0,), (0,)), ((), ())), preferred_element_type=jnp.float32)

    @pl.when(h == 0)
    def _():
        dkv[:, :HD] = dk
        dkv[:, HD:] = dv

    @pl.when(h > 0)
    def _():
        dkv[:, :HD] += dk
        dkv[:, HD:] += dv

    @pl.when(h == pl.num_programs(1) - 1)
    def _():
        dkv_ref[0] = dkv[...].astype(jnp.bfloat16)


def attend_back(q, window, datt, start, ends):
    batches, keys, _ = window.shape
    return pl.pallas_call(
        functools.partial(attend_back_kernel, ends.shape[1]),
        out_shape=[jax.ShapeDtypeStruct(q.shape, jnp.bfloat16), jax.ShapeDtypeStruct(window.shape, jnp.bfloat16)],
        grid_spec=pltpu.PrefetchScalarGridSpec(
            num_scalar_prefetch=2,
            grid=(batches, H),
            in_specs=[
                pl.BlockSpec((BLK, HD), lambda m, h, *_: (m, h)),
                pl.BlockSpec((1, keys, 2 * HD), lambda m, h, *_: (m, 0, 0)),
                pl.BlockSpec((BLK, HD), lambda m, h, *_: (m, h)),
            ],
            out_specs=[
                pl.BlockSpec((BLK, HD), lambda m, h, *_: (m, h)),
                pl.BlockSpec((1, keys, 2 * HD), lambda m, h, *_: (m, 0, 0)),
            ],
            scratch_shapes=[pltpu.VMEM((keys, 2 * HD), jnp.float32)],
        ),
        compiler_params=pltpu.CompilerParams(vmem_limit_bytes=VMEM),
        name="attend_back",
    )(start, ends, q, window, datt)


def geglu_parts(gate):
    c = math.sqrt(2.0 / math.pi)
    square = gate * gate
    t = jnp.tanh(c * gate * (1.0 + 0.044715 * square))
    half = 0.5 * (1.0 + t)
    value = gate * half
    slope = half + 0.5 * gate * (1.0 - t * t) * c * (1.0 + 3 * 0.044715 * square)
    return value, slope


def ffn_kernel(n2_ref, n2t_ref, dy_ref, wg_ref, wu_ref, wd_ref, out_ref, dn2_ref, dwg_ref, dwu_ref, dwd_ref):
    n2, dy = n2_ref[...], dy_ref[...]
    wg, wu, wd = wg_ref[...], wu_ref[...], wd_ref[...]
    f32 = jnp.float32
    gate = jnp.dot(n2, wg, preferred_element_type=f32)
    up = jnp.dot(n2, wu, preferred_element_type=f32)
    value, slope = geglu_parts(gate)
    hidden = (value * up).astype(jnp.bfloat16)
    dh = lax.dot_general(dy, wd, (((1,), (1,)), ((), ())), preferred_element_type=f32)
    dgate = (dh * up * slope).astype(jnp.bfloat16)
    dup = (dh * value).astype(jnp.bfloat16)
    out = jnp.dot(hidden, wd, preferred_element_type=f32)
    dn2 = lax.dot_general(dgate, wg, (((1,), (1,)), ((), ())), preferred_element_type=f32)
    dn2 += lax.dot_general(dup, wu, (((1,), (1,)), ((), ())), preferred_element_type=f32)
    dwd_ref[...] = lax.dot_general(hidden, dy, (((0,), (0,)), ((), ())), preferred_element_type=f32).astype(jnp.bfloat16)
    dwg_ref[...] = jnp.dot(n2t_ref[...], dgate, preferred_element_type=f32).astype(jnp.bfloat16)
    dwu_ref[...] = jnp.dot(n2t_ref[...], dup, preferred_element_type=f32).astype(jnp.bfloat16)

    @pl.when(pl.program_id(0) == 0)
    def _():
        out_ref[...] = out
        dn2_ref[...] = dn2

    @pl.when(pl.program_id(0) > 0)
    def _():
        out_ref[...] += out
        dn2_ref[...] += dn2


def ffn(n2, dy, wg, wu, wd, tile):
    tok, width = n2.shape
    hidden = wg.shape[1]
    whole = pl.BlockSpec((tok, width), lambda i: (0, 0))
    cols = pl.BlockSpec((width, tile), lambda i: (0, i))
    rows = pl.BlockSpec((tile, width), lambda i: (i, 0))
    return pl.pallas_call(
        ffn_kernel,
        grid=(hidden // tile,),
        in_specs=[whole, pl.BlockSpec((width, tok), lambda i: (0, 0)), whole, cols, cols, rows],
        out_specs=[whole, whole, cols, cols, rows],
        out_shape=[jax.ShapeDtypeStruct((tok, width), jnp.float32)] * 2
        + [jax.ShapeDtypeStruct(wg.shape, jnp.bfloat16), jax.ShapeDtypeStruct(wu.shape, jnp.bfloat16), jax.ShapeDtypeStruct(wd.shape, jnp.bfloat16)],
        compiler_params=pltpu.CompilerParams(vmem_limit_bytes=VMEM),
        name="ffn",
    )(n2, n2.T, dy, wg, wu, wd)

def place_of(perm):
    return jnp.argsort(perm, axis=1).astype(jnp.int32)


def windows_of(kv, perm, sources):
    axes = ("dp", "fsdp")
    batches, rows, cols = kv.shape
    count = perm.shape[1]
    part = rows // count
    pieces = kv.reshape(batches, count, part, cols).transpose(1, 0, 2, 3)
    spread = lax.all_to_all(pieces, axes, split_axis=0, concat_axis=0, tiled=True)
    holder = place_of(perm)
    block = perm[:, :, None] - (sources - 1) + jnp.arange(sources, dtype=jnp.int32)
    source = jnp.take_along_axis(holder[:, None, :], jnp.maximum(block, 0), axis=2)
    index = (source * batches + jnp.arange(batches, dtype=jnp.int32)[:, None, None]).transpose(1, 0, 2).reshape(-1)
    picked = jnp.take(spread.reshape(count * batches, part, cols), index, axis=0).reshape(count, batches * sources, part, cols)
    arrived = lax.all_to_all(picked, axes, split_axis=0, concat_axis=0, tiled=True)
    return arrived.transpose(1, 0, 2, 3).reshape(batches, sources * rows, cols)


def window_sums(grads, perm, sources):
    axes = ("dp", "fsdp")
    batches, wide, cols = grads.shape
    rows = wide // sources
    count = perm.shape[1]
    part = rows // count
    pieces = grads.reshape(batches * sources, count, part, cols).transpose(1, 0, 2, 3)
    spread = lax.all_to_all(pieces, axes, split_axis=0, concat_axis=0, tiled=True)
    holder = place_of(perm)
    block = perm[:, :, None] + (sources - 1) - jnp.arange(sources, dtype=jnp.int32)
    reader = jnp.take_along_axis(holder[:, None, :], jnp.minimum(block, count - 1), axis=2)
    slot = jnp.arange(batches, dtype=jnp.int32)[:, None, None] * sources + jnp.arange(sources, dtype=jnp.int32)
    index = (reader * (batches * sources) + slot).transpose(1, 0, 2)
    picked = jnp.take(spread.reshape(count * batches * sources, part, cols), index.reshape(-1), axis=0)
    picked = picked.reshape(count, batches, sources, part, cols).astype(jnp.float32)
    valid = (block < count).transpose(1, 0, 2)[..., None, None]
    summed = jnp.sum(jnp.where(valid, picked, 0.0), axis=2).astype(jnp.bfloat16)
    arrived = lax.all_to_all(summed, axes, split_axis=0, concat_axis=0, tiled=True)
    return arrived.transpose(1, 0, 2, 3).reshape(batches, rows, cols)


def fast_body(grid, tokens, w_query, w_keyval, w_out, w_gate, w_up, w_down, gain_attn, gain_ffn, cotangent, block_perm, extra_len):
    f32, bf16 = jnp.float32, jnp.bfloat16
    batches, _, rows, width = tokens.shape
    tok = batches * rows
    me = lax.axis_index(("dp", "fsdp"))
    sources = WIN // BLK + 1
    scale = HD ** (-0.5)
    kvw = w_keyval.shape[1]
    gains = jnp.stack([gain_attn, gain_ffn], axis=1)
    small = jnp.concatenate([w_keyval, jnp.pad(gains, ((0, 0), (0, 126)))], axis=1)
    shards = [small, w_query, w_out, w_gate, w_up, w_down]
    units = units_of(shards, width)
    small, wq, wo, wg, wu, wd = gather(grid, shards, units, 0)
    wkv = small[:, :kvw]
    g1, g2 = small[:, kvw].astype(f32), small[:, kvw + 1].astype(f32)

    x = tokens.reshape(tok, width).astype(f32)
    dy = cotangent.reshape(tok, width)
    n1, r1 = norm_rows(x, g1)
    n1b = n1.astype(bf16)
    query = (jnp.dot(n1b, wq, preferred_element_type=f32) * scale).astype(bf16)
    keyval = jnp.dot(n1b, wkv, preferred_element_type=f32).astype(bf16)
    window = windows_of(keyval.reshape(batches, rows, kvw), block_perm, sources)
    start = lax.dynamic_slice_in_dim(block_perm, me, 1, axis=1)[:, 0] * BLK
    ends = jnp.cumsum(extra_len + (WIN - 1), axis=1).astype(jnp.int32)
    att = attend(query, window, start, ends)
    mixed = x + jnp.dot(att, wo, preferred_element_type=f32)
    n2, r2 = norm_rows(mixed, g2)
    out, d_n2, d_wgate, d_wup, d_down = ffn(n2.astype(bf16), dy, wg, wu, wd, 512)
    block_out = (mixed + out).astype(bf16)
    d_mixed_norm, d_g2 = norm_back(mixed, r2, g2, d_n2)
    d_mixed = dy.astype(f32) + d_mixed_norm
    d_branch = d_mixed.astype(bf16)
    d_wout = jnp.einsum("ta,td->ad", att, d_branch, preferred_element_type=f32).astype(bf16)
    d_att = jnp.einsum("td,ad->ta", d_branch, wo, preferred_element_type=f32).astype(bf16)
    d_query, d_window = attend_back(query, window, d_att, start, ends)
    d_keyval = window_sums(d_window, block_perm, sources).reshape(tok, kvw)
    d_wquery = (jnp.einsum("td,ta->da", n1b, d_query, preferred_element_type=f32) * scale).astype(bf16)
    d_wkeyval = jnp.einsum("td,tc->dc", n1b, d_keyval, preferred_element_type=f32)
    d_n1 = jnp.einsum("ta,da->td", d_query, wq, preferred_element_type=f32) * scale
    d_n1 = d_n1 + jnp.einsum("tc,dc->td", d_keyval, wkv, preferred_element_type=f32)
    d_x_norm, d_g1 = norm_back(x, r1, g1, d_n1)
    grad_tokens = (d_mixed + d_x_norm).astype(bf16)
    d_gains = jnp.pad(jnp.stack([d_g1, d_g2], axis=1), ((0, 0), (0, 126)))
    d_small = jnp.concatenate([d_wkeyval, d_gains], axis=1).astype(bf16)
    small, dq, do, dg, du, dd = scatter(grid, [d_small, d_wquery, d_wout, d_wgate, d_wup, d_down], units, 1)
    return (
        block_out.reshape(tokens.shape),
        grad_tokens.reshape(tokens.shape),
        dq,
        small[:, :kvw],
        do,
        dg,
        du,
        dd,
        small[:, kvw],
        small[:, kvw + 1],
    )


def units_of(shards, width):
    rows = min(s.shape[0] for s in shards)
    units = []
    for i, s in enumerate(shards):
        for r in range(0, s.shape[0], rows):
            for c in range(0, s.shape[1], width):
                units.append((i, (r, rows), (c, min(width, s.shape[1] - c))))
    return units


def solution(mesh):
    count = mesh.shape["dp"] * mesh.shape["fsdp"]
    grid = (2, 2, 2, mesh.shape["fsdp"])
    whole_tiles = mesh.shape["dp"] == 8 and 1536 % (16 * count) == 0
    run = functools.partial(fast_body, grid) if whole_tiles else body
    placed = (
        P(None, ("dp", "fsdp"), None, None),
        P(("dp", "fsdp"), None),
        P(("dp", "fsdp"), None),
        P(("dp", "fsdp"), None),
        P(("dp", "fsdp"), None),
        P(("dp", "fsdp"), None),
        P(("dp", "fsdp"), None),
        P(("dp", "fsdp")),
        P(("dp", "fsdp")),
        P(None, ("dp", "fsdp"), None, None),
        P(),
        P(),
    )
    return jax.shard_map(
        run,
        mesh=mesh,
        in_specs=placed,
        out_specs=(
            P(None, ("dp", "fsdp"), None, None),
            P(None, ("dp", "fsdp"), None, None),
            P(("dp", "fsdp"), None),
            P(("dp", "fsdp"), None),
            P(("dp", "fsdp"), None),
            P(("dp", "fsdp"), None),
            P(("dp", "fsdp"), None),
            P(("dp", "fsdp"), None),
            P(("dp", "fsdp")),
            P(("dp", "fsdp")),
        ),
        check_vma=False,
    )
```

```python
import functools
import math

import jax
import jax.numpy as jnp
from jax import lax
from jax.experimental import pallas as pl
from jax.experimental.pallas import tpu as pltpu
from jax.sharding import PartitionSpec as P

H = 6
HD = 256
WIN = 1024
BLK = 256


EPS = 1e-06
VMEM = 60 * 1024 * 1024


def for_sending(x):
    return jax.tree.map(lambda a: a.astype(jnp.bfloat16) if a.dtype == jnp.float32 else a, x)


def shifted(value, axis, steps):
    count = lax.axis_size(axis)
    leading, last = (max(0, -steps), min(count, count - steps))
    return lax.ppermute(value, axis, [(source, source + steps) for source in range(leading, last)])


def norm_rows(value, gain):
    inverse = lax.rsqrt(jnp.mean(value * value, axis=-1, keepdims=True) + EPS)
    return (value * inverse * gain, inverse)


def norm_back(value, inverse, gain, grad):
    scaled = grad * gain
    width = value.shape[-1]
    dvalue = (
        inverse * scaled
        - value * inverse**3 * jnp.sum(scaled * value, axis=-1, keepdims=True) / width
    )
    dgain = jnp.sum(grad * value * inverse, axis=0)
    return (dvalue, dgain)


def sequence_of(positions, ends):
    return jnp.sum((positions[:, None] >= ends[None, :]).astype(jnp.int32), axis=1)


def visible_mask(query_pos, key_pos, ends):
    same = sequence_of(query_pos, ends)[:, None] == sequence_of(key_pos, ends)[None, :]
    gap = query_pos[:, None] - key_pos[None, :]
    return same & (gap >= 0) & (gap < WIN) & (key_pos[None, :] >= 0)


def geglu(gate, up):
    return jax.nn.gelu(gate, approximate=True) * up


def move_keys(value, order, count):
    rows = value.shape[0]
    spread = lax.all_to_all(value, ("dp", "fsdp"), split_axis=1, concat_axis=0, tiled=True)
    pieces = spread.reshape(count, rows, spread.shape[1])
    placed = jnp.take(pieces, order, axis=0).reshape(count * rows, spread.shape[1])
    return lax.all_to_all(placed, ("dp", "fsdp"), split_axis=0, concat_axis=1, tiled=True)


def move_grads(value, order, count):
    rows = value.shape[0]
    spread = lax.all_to_all(
        for_sending(value), ("dp", "fsdp"), split_axis=1, concat_axis=0, tiled=True
    ).astype(value.dtype)
    pieces = spread.reshape(count, rows, spread.shape[1])
    placed = jnp.take(pieces, order, axis=0).reshape(count * rows, spread.shape[1])
    return lax.all_to_all(
        for_sending(placed), ("dp", "fsdp"), split_axis=0, concat_axis=1, tiled=True
    ).astype(placed.dtype)


def body(
    tokens,
    w_query,
    w_keyval,
    w_out,
    w_gate,
    w_up,
    w_down,
    gain_attn,
    gain_ffn,
    cotangent,
    block_perm,
    extra_len,
):
    count = lax.axis_size(("dp", "fsdp"))
    me = lax.axis_index(("dp", "fsdp"))
    batches = tokens.shape[0]
    sources = WIN // BLK + 1
    scale = HD ** (-0.5)
    shards = (w_query, w_keyval, w_out, w_gate, w_up, w_down, gain_attn, gain_ffn)
    device_ids = jnp.arange(count, dtype=jnp.int32)
    totals = None
    outputs = []
    input_grads = []
    for batch in range(batches):
        full = (
            lax.all_gather(shards[0], ("dp", "fsdp"), axis=0, tiled=True),
            lax.all_gather(shards[1], ("dp", "fsdp"), axis=0, tiled=True),
            lax.all_gather(shards[2], ("dp", "fsdp"), axis=0, tiled=True),
            lax.all_gather(shards[3], ("dp", "fsdp"), axis=0, tiled=True),
            lax.all_gather(shards[4], ("dp", "fsdp"), axis=0, tiled=True),
            lax.all_gather(shards[5], ("dp", "fsdp"), axis=0, tiled=True),
            lax.all_gather(shards[6], ("dp", "fsdp"), axis=0, tiled=True),
            lax.all_gather(shards[7], ("dp", "fsdp"), axis=0, tiled=True),
        )
        wq, wkv, wo, wg, wu, wd, g1b, g2b = full
        g1 = g1b.astype(jnp.float32)
        g2 = g2b.astype(jnp.float32)
        perm_row = block_perm[batch]
        ends = jnp.cumsum(extra_len[batch] + (WIN - 1))
        mine = lax.dynamic_slice_in_dim(perm_row, me, 1)[0]
        holder = jnp.sum(
            jnp.where(perm_row[None, :] == device_ids[:, None], device_ids[None, :], 0), axis=1
        )
        query_pos = mine * BLK + jnp.arange(BLK, dtype=jnp.int32)
        key_pos = (mine - (sources - 1)) * BLK + jnp.arange(sources * BLK, dtype=jnp.int32)
        mask = jnp.repeat(visible_mask(query_pos, key_pos, ends), H, axis=0)
        x = tokens[batch, 0].astype(jnp.float32)
        n1, r1 = norm_rows(x, g1)
        n1b = n1.astype(jnp.bfloat16)
        query = (jnp.dot(n1b, wq, preferred_element_type=jnp.float32) * scale).astype(jnp.bfloat16)
        query_rows = query.reshape(BLK * H, HD)
        keyval = jnp.dot(n1b, wkv, preferred_element_type=jnp.float32).astype(jnp.bfloat16)
        ordered = move_keys(keyval, holder, count)
        window = [ordered] * sources
        for back in range(1, sources):
            window[sources - 1 - back] = shifted(ordered, ("dp", "fsdp"), back)
        picked = move_keys(jnp.concatenate(window, axis=0), perm_row, count)
        keys_src = picked[:, :HD]
        values_src = picked[:, HD:]
        scores = jnp.einsum("qd,kd->qk", query_rows, keys_src, preferred_element_type=jnp.float32)
        masked = jnp.where(mask, scores, -1e30)
        top = jnp.max(masked, axis=1, keepdims=True)
        expd = jnp.exp(masked - top)
        rowsum = jnp.sum(expd, axis=1, keepdims=True)
        lse = top + jnp.log(rowsum)
        probs_low = (expd / rowsum).astype(jnp.bfloat16)
        att = jnp.dot(probs_low, values_src, preferred_element_type=jnp.float32)
        att_low = att.reshape(BLK, H * HD).astype(jnp.bfloat16)
        mixed = x + jnp.dot(att_low, wo, preferred_element_type=jnp.float32)
        n2, r2 = norm_rows(mixed, g2)
        n2b = n2.astype(jnp.bfloat16)
        gate = jnp.dot(n2b, wg, preferred_element_type=jnp.float32)
        up = jnp.dot(n2b, wu, preferred_element_type=jnp.float32)
        hidden = geglu(gate, up).astype(jnp.bfloat16)
        outputs.append(
            (mixed + jnp.dot(hidden, wd, preferred_element_type=jnp.float32)).astype(jnp.bfloat16)
        )
        wq, wkv, wo, wg, wu, wd, g1b, g2b = (
            lax.all_gather(shards[0], ("dp", "fsdp"), axis=0, tiled=True),
            lax.all_gather(shards[1], ("dp", "fsdp"), axis=0, tiled=True),
            lax.all_gather(shards[2], ("dp", "fsdp"), axis=0, tiled=True),
            lax.all_gather(shards[3], ("dp", "fsdp"), axis=0, tiled=True),
            lax.all_gather(shards[4], ("dp", "fsdp"), axis=0, tiled=True),
            lax.all_gather(shards[5], ("dp", "fsdp"), axis=0, tiled=True),
            lax.all_gather(shards[6], ("dp", "fsdp"), axis=0, tiled=True),
            lax.all_gather(shards[7], ("dp", "fsdp"), axis=0, tiled=True),
        )
        dy = cotangent[batch, 0]
        d_down = jnp.einsum("tf,td->fd", hidden, dy, preferred_element_type=jnp.float32)
        d_hidden = jnp.einsum("td,fd->tf", dy, wd, preferred_element_type=jnp.float32)
        _, geglu_pull = jax.vjp(geglu, gate, up)
        d_gate, d_up = geglu_pull(d_hidden)
        d_gate_low = d_gate.astype(jnp.bfloat16)
        d_up_low = d_up.astype(jnp.bfloat16)
        d_wgate = jnp.einsum("td,tf->df", n2b, d_gate_low, preferred_element_type=jnp.float32)
        d_wup = jnp.einsum("td,tf->df", n2b, d_up_low, preferred_element_type=jnp.float32)
        d_n2 = jnp.einsum("tf,df->td", d_gate_low, wg, preferred_element_type=jnp.float32)
        d_n2 = d_n2 + jnp.einsum("tf,df->td", d_up_low, wu, preferred_element_type=jnp.float32)
        d_mixed_norm, d_g2 = norm_back(mixed, r2, g2, d_n2)
        d_mixed = dy.astype(jnp.float32) + d_mixed_norm
        d_branch = d_mixed.astype(jnp.bfloat16)
        d_wout = jnp.einsum("ta,td->ad", att_low, d_branch, preferred_element_type=jnp.float32)
        d_att = jnp.einsum("td,ad->ta", d_branch, wo, preferred_element_type=jnp.float32)
        d_att_rows = d_att.astype(jnp.bfloat16).reshape(BLK * H, HD)
        again = jnp.einsum("qd,kd->qk", query_rows, keys_src, preferred_element_type=jnp.float32)
        probs = jnp.exp(jnp.where(mask, again, -1e30) - lse)
        d_probs = jnp.einsum(
            "qd,kd->qk", d_att_rows, values_src, preferred_element_type=jnp.float32
        )
        delta = jnp.sum(probs * d_probs, axis=1, keepdims=True)
        d_scores = (probs * (d_probs - delta)).astype(jnp.bfloat16)
        d_query = jnp.dot(d_scores, keys_src, preferred_element_type=jnp.float32).astype(
            jnp.bfloat16
        )
        d_query = d_query.reshape(BLK, H * HD)
        d_keys = jnp.einsum("qk,qd->kd", d_scores, query_rows, preferred_element_type=jnp.float32)
        d_values = jnp.einsum(
            "qk,qd->kd", probs.astype(jnp.bfloat16), d_att_rows, preferred_element_type=jnp.float32
        )
        d_keyval_flat = jnp.concatenate([d_keys, d_values], axis=1)
        ordered_grads = move_grads(d_keyval_flat, holder, count).reshape(sources, BLK, 2 * HD)
        summed = ordered_grads[sources - 1]
        for back in range(1, sources):
            summed = summed + shifted(
                ordered_grads[sources - 1 - back].astype(jnp.bfloat16), ("dp", "fsdp"), -back
            ).astype(jnp.float32)
        d_keyval = move_grads(summed, perm_row, count).astype(jnp.bfloat16)
        d_wquery = jnp.einsum("td,ta->da", n1b, d_query, preferred_element_type=jnp.float32) * scale
        d_wkeyval = jnp.einsum("td,tc->dc", n1b, d_keyval, preferred_element_type=jnp.float32)
        d_n1 = jnp.einsum("ta,da->td", d_query, wq, preferred_element_type=jnp.float32) * scale
        d_n1 = d_n1 + jnp.einsum("tc,dc->td", d_keyval, wkv, preferred_element_type=jnp.float32)
        d_x_norm, d_g1 = norm_back(x, r1, g1, d_n1)
        input_grads.append((d_mixed + d_x_norm).astype(jnp.bfloat16))
        local = (d_wquery, d_wkeyval, d_wout, d_wgate, d_wup, d_down, d_g1, d_g2)
        totals = local if totals is None else tuple((a + b for a, b in zip(totals, local)))
    totals = lax.psum_scatter(totals, ("dp", "fsdp"), scatter_dimension=0, tiled=True)
    block_out = jnp.stack(outputs)[:, None]
    grad_tokens = jnp.stack(input_grads)[:, None]
    return (
        block_out,
        grad_tokens,
        totals[0],
        totals[1],
        totals[2],
        totals[3],
        totals[4],
        totals[5],
        totals[6],
        totals[7],
    )


MESH = pl.DeviceIdType.MESH

class Place:
    def __init__(self, grid):
        self.A, self.B, self.C, self.Z = grid
        dp = lax.axis_index("dp")
        self.z = lax.axis_index("fsdp")
        self.c = dp % 2
        self.x = (dp // 2) % 2
        self.y = dp // 4
    def dev(self, y=None, x=None, c=None, z=None):
        y = self.y if y is None else y
        x = self.x if x is None else x
        c = self.c if c is None else c
        z = self.z if z is None else z
        return ((y * 2 + x) * 2 + c, z)

def barrier(p):
    sem = pltpu.get_barrier_semaphore()
    peers = [p.dev(c=1 - p.c), p.dev(x=1 - p.x), p.dev(y=1 - p.y)] + [p.dev(z=(p.z + i) % p.Z) for i in range(1, p.Z)]
    for q in peers:
        pl.semaphore_signal(sem, inc=1, device_id=q, device_id_type=MESH)
    pl.semaphore_wait(sem, len(peers))

class Gather:
    COPIES = 12
    def __init__(self, p, src, dst, rows, cols, send, recv, local):
        self.p, self.dst, self.send, self.recv, self.local = p, dst, send, recv, local
        self.src = src.at[pl.ds(*rows), pl.ds(*cols)]
        self.r = pl.ds(*rows)
        self.all = pl.ds(*cols)
        half = (cols[1] // 256) * 128 if cols[1] > 128 else 128
        half = cols[1] - half if cols[1] - half >= half else half
        self.h = [pl.ds(cols[0], half), pl.ds(cols[0] + half, cols[1] - half)] if cols[1] > 128 else None
    def copy(self, k, src, dst, dev):
        return pltpu.make_async_remote_copy(src, dst, self.send.at[k], self.recv.at[k], device_id=dev, device_id_type=MESH)
    def own(self):
        p = self.p
        return pltpu.make_async_copy(self.src, self.dst.at[p.y, p.x, p.c, p.z, self.r, self.all], self.local)
    def zs(self):
        p = self.p
        out = []
        for i in range(1, p.Z):
            out.append((self.copy(i - 1, self.src, self.dst.at[p.y, p.x, p.c, p.z, self.r, self.all], p.dev(z=(p.z + i) % p.Z)),
                        self.dst.at[p.y, p.x, p.c, (p.z + p.Z - i) % p.Z, self.r, self.all]))
        return [a for a, _ in out]
    def same(self, k, ref, dev):
        return self.copy(k, ref, ref, dev)
    def p1(self):
        p, d = self.p, self.dst
        return [self.same(3, d.at[p.y, p.x, p.c, :, self.r, self.h[0]], p.dev(x=1 - p.x)),
                self.same(4, d.at[p.y, p.x, p.c, :, self.r, self.h[1]], p.dev(y=1 - p.y))]
    def p2(self):
        p, d = self.p, self.dst
        return [self.same(5, d.at[p.y, :, p.c, :, self.r, self.h[0]], p.dev(y=1 - p.y)),
                self.same(6, d.at[:, p.x, p.c, :, self.r, self.h[1]], p.dev(x=1 - p.x))]
    def c0(self):
        p, d = self.p, self.dst
        return [self.same(7, d.at[p.y, p.x, p.c, :, self.r, self.all], p.dev(c=1 - p.c))]
    def c1(self):
        p, d = self.p, self.dst
        o = p.dev(c=1 - p.c)
        return [self.same(8, d.at[p.y, 1 - p.x, p.c, :, self.r, self.h[0]], o),
                self.same(9, d.at[1 - p.y, p.x, p.c, :, self.r, self.h[1]], o)]
    def c2(self):
        p, d = self.p, self.dst
        o = p.dev(c=1 - p.c)
        return [self.same(10, d.at[1 - p.y, :, p.c, :, self.r, self.h[0]], o),
                self.same(11, d.at[:, 1 - p.x, p.c, :, self.r, self.h[1]], o)]

def start(cs):
    for c in cs: c.start()
def wait_recv(cs):
    for c in cs: c.wait_recv()
def wait_send(cs):
    for c in cs: c.wait_send()

def gather_kernel(grid, units, nin, *refs):
    ins, outs = refs[:nin], refs[nin:2 * nin]
    send, recv, local = refs[2 * nin:]
    p = Place(grid)
    barrier(p)
    U = len(units)
    gs = [Gather(p, ins[i], outs[i], rows, cols, send.at[u], recv.at[u], local.at[u]) for u, (i, rows, cols) in enumerate(units)]
    for s in range(U + 4):
        if s < U:
            gs[s].own().start(); start(gs[s].zs())
        if 0 <= s - 1 < U:
            g = gs[s - 1]; g.own().wait(); wait_recv(g.zs()); start(g.p1()); start(g.c0())
        if 0 <= s - 2 < U:
            g = gs[s - 2]; wait_recv(g.p1()); start(g.p2()); start(g.c1())
        if 0 <= s - 3 < U:
            g = gs[s - 3]; wait_recv(g.p2()); start(g.c2())
        if 0 <= s - 4 < U:
            g = gs[s - 4]
            wait_recv(g.c0() + g.c1() + g.c2())
            wait_send(g.zs() + g.p1() + g.p2() + g.c0() + g.c1() + g.c2())

def gather(grid, shards, units, collective_id):
    n = len(shards)
    outs = pl.pallas_call(
        functools.partial(gather_kernel, grid, units, n),
        out_shape=[jax.ShapeDtypeStruct(tuple(grid) + s.shape, s.dtype) for s in shards],
        in_specs=[pl.BlockSpec(memory_space=pl.ANY)] * n,
        out_specs=[pl.BlockSpec(memory_space=pl.ANY)] * n,
        scratch_shapes=[pltpu.SemaphoreType.DMA((len(units), 12)), pltpu.SemaphoreType.DMA((len(units), 12)), pltpu.SemaphoreType.DMA((len(units),))],
        compiler_params=pltpu.CompilerParams(collective_id=collective_id, has_side_effects=True),
        name="gather",
    )(*shards)
    return [o.reshape(-1, s.shape[-1]) for o, s in zip(outs, shards)]

class Scatter:
    def __init__(self, p, u, slot, src, out, rows, cols, bufs, sems):
        self.p, self.u, self.slot = p, u, slot
        self.rb0, self.rb1, self.rb2, self.rb3, self.own, self.fin = bufs
        self.send, self.recv, self.lsem = sems
        self.src, self.out = src, out
        self.r, self.cols = pl.ds(*rows), pl.ds(*cols)
        w = cols[1]
        half = w - (w // 256) * 128
        self.w, self.h = w, [pl.ds(0, half), pl.ds(half, w - half)]
        self.hs = [half, w - half]
        self.R = rows[1]
        self.rows, self.colsl = rows, cols
        self.all = pl.ds(0, w)
        self.P = self.own.at[slot]
    def copy(self, k, src, dst, dev):
        return pltpu.make_async_remote_copy(src, dst, self.send.at[self.u, k], self.recv.at[self.u, k], device_id=dev, device_id_type=MESH)
    def r0(self):
        p = self.p
        return [self.copy(0, self.src.at[:, :, 1 - p.c, :, self.r, self.cols], self.rb0.at[self.u, :, :, :, :, self.all], p.dev(c=1 - p.c))]
    def load_own(self):
        p = self.p
        return pltpu.make_async_copy(self.src.at[:, :, p.c, :, self.r, self.cols], self.P.at[..., self.all], self.lsem.at[self.u, 0])
    def load_r0(self, tmp):
        return pltpu.make_async_copy(self.rb0.at[self.u, :, :, :, :, self.all], tmp.at[..., self.all], self.lsem.at[self.u, 1])
    def add0(self, tmp):
        P, w, Z = self.P, self.w, self.p.Z
        @pl.loop(0, P.shape[0] * P.shape[1] * Z)
        def _(i):
            a, b, d = i // (P.shape[1] * Z), (i // Z) % P.shape[1], i % Z
            P[a, b, d, :, pl.ds(0, w)] = (P[a, b, d, :, pl.ds(0, w)].astype(jnp.float32) + tmp[a, b, d, :, pl.ds(0, w)].astype(jnp.float32)).astype(jnp.bfloat16)
    def r1(self):
        p, P = self.p, self.P
        return [self.copy(1, P.at[1 - p.y, :, :, :, self.h[0]], self.rb1.at[self.u, 0, :, :, :, pl.ds(0, self.hs[0])], p.dev(y=1 - p.y)),
                self.copy(2, P.at[:, 1 - p.x, :, :, self.h[1]], self.rb1.at[self.u, 1, :, :, :, pl.ds(0, self.hs[1])], p.dev(x=1 - p.x))]
    def add1(self):
        p, P, Z = self.p, self.P, self.p.Z
        @pl.loop(0, 2 * Z)
        def _(i):
            b, d = i // Z, i % Z
            P[p.y, b, d, :, self.h[0]] = (P[p.y, b, d, :, self.h[0]].astype(jnp.float32) + self.rb1[self.u, 0, b, d, :, pl.ds(0, self.hs[0])].astype(jnp.float32)).astype(jnp.bfloat16)
            P[b, p.x, d, :, self.h[1]] = (P[b, p.x, d, :, self.h[1]].astype(jnp.float32) + self.rb1[self.u, 1, b, d, :, pl.ds(0, self.hs[1])].astype(jnp.float32)).astype(jnp.bfloat16)
    def r2(self):
        p, P = self.p, self.P
        return [self.copy(3, P.at[p.y, 1 - p.x, :, :, self.h[0]], self.rb2.at[self.u, :, :, self.h[0]], p.dev(x=1 - p.x)),
                self.copy(4, P.at[1 - p.y, p.x, :, :, self.h[1]], self.rb2.at[self.u, :, :, self.h[1]], p.dev(y=1 - p.y))]
    def add2(self):
        p, P, Z = self.p, self.P, self.p.Z
        @pl.loop(0, Z)
        def _(d):
            P[p.y, p.x, d, :, self.all] = (P[p.y, p.x, d, :, self.all].astype(jnp.float32) + self.rb2[self.u, d, :, self.all].astype(jnp.float32)).astype(jnp.bfloat16)
    def r3(self):
        p, P = self.p, self.P
        return [self.copy(4 + i, P.at[p.y, p.x, (p.z + i) % p.Z, :, self.all], self.rb3.at[self.u, i - 1, :, self.all], p.dev(z=(p.z + i) % p.Z)) for i in range(1, p.Z)]
    def add3(self, f):
        p, P = self.p, self.P
        s = P[p.y, p.x, p.z, :, self.all].astype(jnp.float32)
        for i in range(p.Z - 1):
            s = s + self.rb3[self.u, i, :, self.all].astype(jnp.float32)
        self.fin[f, :, self.all] = s
    def store(self, f):
        return pltpu.make_async_copy(self.fin.at[f, :, self.all], self.out.at[pl.ds(*self.rows), self.cols], self.lsem.at[self.u, 2])

def scatter_kernel(grid, units, nin, *refs):
    ins, outs = refs[:nin], refs[nin:2 * nin]
    rb0 = refs[2 * nin]
    rb1, rb2, rb3, own, tmp, fin, send, recv, lsem = refs[2 * nin + 1:]
    p = Place(grid)
    barrier(p)
    U, NS = len(units), own.shape[0]
    gs = [Scatter(p, u, u % NS, ins[i], outs[i], rows, cols, (rb0, rb1, rb2, rb3, own, fin), (send, recv, lsem)) for u, (i, rows, cols) in enumerate(units)]
    for s in range(U + 5):
        if s < U:
            g = gs[s]
            start(g.r0())
            if s >= NS:
                pass
            g.load_own().start()
        if 0 <= s - 1 < U:
            g = gs[s - 1]; t = tmp
            wait_recv(g.r0()); g.load_r0(t).start(); g.load_own().wait(); g.load_r0(t).wait(); g.add0(t); start(g.r1())
        if 0 <= s - 2 < U:
            g = gs[s - 2]; wait_recv(g.r1()); wait_send(g.r1()); g.add1(); start(g.r2())
        if 0 <= s - 3 < U:
            g = gs[s - 3]; wait_recv(g.r2()); wait_send(g.r2()); g.add2(); start(g.r3())
        if 0 <= s - 4 < U:
            g = gs[s - 4]; wait_recv(g.r3()); wait_send(g.r0() + g.r3())
            f = (s - 4) % 2
            if s - 6 >= 0:
                gs[s - 6].store(f).wait()
            g.add3(f); g.store(f).start()
    for u in range(max(0, U - 2), U):
        gs[u].store(u % 2).wait()

def scatter(grid, fulls, units, collective_id):
    n = len(fulls)
    A, B, C, Z = grid
    ndev = A * B * C * Z
    U = len(units)
    shards = [(f.shape[0] // ndev, f.shape[1]) for f in fulls]
    W = max(c[1] for _, _, c in units)
    R = units[0][1][1]
    NS = 5
    outs = pl.pallas_call(
        functools.partial(scatter_kernel, grid, units, n),
        out_shape=[jax.ShapeDtypeStruct(s, jnp.float32) for s in shards] + [jax.ShapeDtypeStruct((U, A, B, Z, R, W), jnp.bfloat16)],
        in_specs=[pl.BlockSpec(memory_space=pl.ANY)] * n,
        out_specs=[pl.BlockSpec(memory_space=pl.ANY)] * (n + 1),
        scratch_shapes=[
            pltpu.VMEM((U, 2, 2, Z, R, W - (W // 256) * 128), jnp.bfloat16),
            pltpu.VMEM((U, Z, R, W), jnp.bfloat16),
            pltpu.VMEM((U, Z - 1, R, W), jnp.bfloat16),
            pltpu.VMEM((NS, A, B, Z, R, W), jnp.bfloat16),
            pltpu.VMEM((A, B, Z, R, W), jnp.bfloat16),
            pltpu.VMEM((2, R, W), jnp.float32),
            pltpu.SemaphoreType.DMA((U, 8)), pltpu.SemaphoreType.DMA((U, 8)), pltpu.SemaphoreType.DMA((U, 3))],
        compiler_params=pltpu.CompilerParams(collective_id=collective_id, has_side_effects=True, vmem_limit_bytes=60 * 1024 * 1024),
        name="scatter",
    )(*[f.reshape(tuple(grid) + (s[0], s[1])) for f, s in zip(fulls, shards)])
    return outs[:n]


def window_mask(start, ends, nseq, m, queries, keys):
    qpos = start + lax.broadcasted_iota(jnp.int32, (queries, 1), 0)
    first = jnp.maximum(qpos - (WIN - 1), 0)
    for k in range(nseq):
        end = ends[m, k]
        first = jnp.maximum(first, jnp.where(qpos >= end, end, 0))
    kpos = start - (keys - queries) + lax.broadcasted_iota(jnp.int32, (1, keys), 1)
    return (kpos >= first) & (kpos <= qpos)


def softmax_rows(q, k, mask):
    scores = lax.dot_general(q, k, (((1,), (1,)), ((), ())), preferred_element_type=jnp.float32)
    masked = jnp.where(mask, scores, -1e30)
    expd = jnp.exp(masked - jnp.max(masked, axis=1, keepdims=True))
    return expd * (1.0 / jnp.sum(expd, axis=1, keepdims=True))


def attend_kernel(nseq, start, ends, q_ref, kv_ref, o_ref):
    m = pl.program_id(0)
    mask = window_mask(start[m], ends, nseq, m, q_ref.shape[0], kv_ref.shape[1])
    p = softmax_rows(q_ref[...], kv_ref[0, :, :HD], mask)
    o_ref[...] = jnp.dot(p.astype(jnp.bfloat16), kv_ref[0, :, HD:], preferred_element_type=jnp.float32).astype(jnp.bfloat16)


def attend(q, window, start, ends):
    batches, keys, _ = window.shape
    return pl.pallas_call(
        functools.partial(attend_kernel, ends.shape[1]),
        out_shape=jax.ShapeDtypeStruct(q.shape, jnp.bfloat16),
        grid_spec=pltpu.PrefetchScalarGridSpec(
            num_scalar_prefetch=2,
            grid=(batches, H),
            in_specs=[
                pl.BlockSpec((BLK, HD), lambda m, h, *_: (m, h)),
                pl.BlockSpec((1, keys, 2 * HD), lambda m, h, *_: (m, 0, 0)),
            ],
            out_specs=pl.BlockSpec((BLK, HD), lambda m, h, *_: (m, h)),
        ),
        compiler_params=pltpu.CompilerParams(vmem_limit_bytes=VMEM),
        name="attend",
    )(start, ends, q, window)


def attend_back_kernel(nseq, start, ends, q_ref, kv_ref, d_ref, dq_ref, dkv_ref, dkv):
    m, h = pl.program_id(0), pl.program_id(1)
    mask = window_mask(start[m], ends, nseq, m, q_ref.shape[0], kv_ref.shape[1])
    q, k, v, d = q_ref[...], kv_ref[0, :, :HD], kv_ref[0, :, HD:], d_ref[...]
    p = softmax_rows(q, k, mask)
    dp = lax.dot_general(d, v, (((1,), (1,)), ((), ())), preferred_element_type=jnp.float32)
    ds = (p * (dp - jnp.sum(p * dp, axis=1, keepdims=True))).astype(jnp.bfloat16)
    dq_ref[...] = jnp.dot(ds, k, preferred_element_type=jnp.float32).astype(jnp.bfloat16)
    dk = lax.dot_general(ds, q, (((0,), (0,)), ((), ())), preferred_element_type=jnp.float32)
    dv = lax.dot_general(p.astype(jnp.bfloat16), d, (((0,), (0,)), ((), ())), preferred_element_type=jnp.float32)

    @pl.when(h == 0)
    def _():
        dkv[:, :HD] = dk
        dkv[:, HD:] = dv

    @pl.when(h > 0)
    def _():
        dkv[:, :HD] += dk
        dkv[:, HD:] += dv

    @pl.when(h == pl.num_programs(1) - 1)
    def _():
        dkv_ref[0] = dkv[...].astype(jnp.bfloat16)


def attend_back(q, window, datt, start, ends):
    batches, keys, _ = window.shape
    return pl.pallas_call(
        functools.partial(attend_back_kernel, ends.shape[1]),
        out_shape=[jax.ShapeDtypeStruct(q.shape, jnp.bfloat16), jax.ShapeDtypeStruct(window.shape, jnp.bfloat16)],
        grid_spec=pltpu.PrefetchScalarGridSpec(
            num_scalar_prefetch=2,
            grid=(batches, H),
            in_specs=[
                pl.BlockSpec((BLK, HD), lambda m, h, *_: (m, h)),
                pl.BlockSpec((1, keys, 2 * HD), lambda m, h, *_: (m, 0, 0)),
                pl.BlockSpec((BLK, HD), lambda m, h, *_: (m, h)),
            ],
            out_specs=[
                pl.BlockSpec((BLK, HD), lambda m, h, *_: (m, h)),
                pl.BlockSpec((1, keys, 2 * HD), lambda m, h, *_: (m, 0, 0)),
            ],
            scratch_shapes=[pltpu.VMEM((keys, 2 * HD), jnp.float32)],
        ),
        compiler_params=pltpu.CompilerParams(vmem_limit_bytes=VMEM),
        name="attend_back",
    )(start, ends, q, window, datt)


def geglu_parts(gate):
    c = math.sqrt(2.0 / math.pi)
    square = gate * gate
    t = jnp.tanh(c * gate * (1.0 + 0.044715 * square))
    half = 0.5 * (1.0 + t)
    value = gate * half
    slope = half + 0.5 * gate * (1.0 - t * t) * c * (1.0 + 3 * 0.044715 * square)
    return value, slope


def ffn_kernel(n2_ref, n2t_ref, dy_ref, wg_ref, wu_ref, wd_ref, out_ref, dn2_ref, dwg_ref, dwu_ref, dwd_ref):
    n2, dy = n2_ref[...], dy_ref[...]
    wg, wu, wd = wg_ref[...], wu_ref[...], wd_ref[...]
    f32 = jnp.float32
    gate = jnp.dot(n2, wg, preferred_element_type=f32)
    up = jnp.dot(n2, wu, preferred_element_type=f32)
    value, slope = geglu_parts(gate)
    hidden = (value * up).astype(jnp.bfloat16)
    dh = lax.dot_general(dy, wd, (((1,), (1,)), ((), ())), preferred_element_type=f32)
    dgate = (dh * up * slope).astype(jnp.bfloat16)
    dup = (dh * value).astype(jnp.bfloat16)
    out = jnp.dot(hidden, wd, preferred_element_type=f32)
    dn2 = lax.dot_general(dgate, wg, (((1,), (1,)), ((), ())), preferred_element_type=f32)
    dn2 += lax.dot_general(dup, wu, (((1,), (1,)), ((), ())), preferred_element_type=f32)
    dwd_ref[...] = lax.dot_general(hidden, dy, (((0,), (0,)), ((), ())), preferred_element_type=f32).astype(jnp.bfloat16)
    dwg_ref[...] = jnp.dot(n2t_ref[...], dgate, preferred_element_type=f32).astype(jnp.bfloat16)
    dwu_ref[...] = jnp.dot(n2t_ref[...], dup, preferred_element_type=f32).astype(jnp.bfloat16)

    @pl.when(pl.program_id(0) == 0)
    def _():
        out_ref[...] = out
        dn2_ref[...] = dn2

    @pl.when(pl.program_id(0) > 0)
    def _():
        out_ref[...] += out
        dn2_ref[...] += dn2


def ffn(n2, dy, wg, wu, wd, tile):
    tok, width = n2.shape
    hidden = wg.shape[1]
    whole = pl.BlockSpec((tok, width), lambda i: (0, 0))
    cols = pl.BlockSpec((width, tile), lambda i: (0, i))
    rows = pl.BlockSpec((tile, width), lambda i: (i, 0))
    return pl.pallas_call(
        ffn_kernel,
        grid=(hidden // tile,),
        in_specs=[whole, pl.BlockSpec((width, tok), lambda i: (0, 0)), whole, cols, cols, rows],
        out_specs=[whole, whole, cols, cols, rows],
        out_shape=[jax.ShapeDtypeStruct((tok, width), jnp.float32)] * 2
        + [jax.ShapeDtypeStruct(wg.shape, jnp.bfloat16), jax.ShapeDtypeStruct(wu.shape, jnp.bfloat16), jax.ShapeDtypeStruct(wd.shape, jnp.bfloat16)],
        compiler_params=pltpu.CompilerParams(vmem_limit_bytes=VMEM),
        name="ffn",
    )(n2, n2.T, dy, wg, wu, wd)


class Exchange:
    def __init__(self, p, count, send, recv, local):
        self.count, self.send, self.recv, self.local = count, send, recv, local
        self.me = (p.y * 8 + p.x * 4 + p.c * 2) // 2 * p.Z + p.z
        self.Z = p.Z
        self.groups = BLK // 16
        self.wide = 2 * HD * self.groups // count

    def piece(self, d):
        return d % self.groups, pl.ds(pl.multiple_of((d // self.groups) * self.wide, self.wide), self.wide)

    def dev(self, d):
        return (d // self.Z, d % self.Z)

    def copy(self, off, src, dst):
        t = lax.rem(self.me + off, self.count)
        return pltpu.make_async_remote_copy(
            src(t), dst(t), self.send.at[off - 1], self.recv.at[off - 1], device_id=self.dev(t), device_id_type=MESH
        )

    def begin(self, src, dst):
        @pl.loop(1, self.count)
        def _(off):
            self.copy(off, src, dst).start()

        pltpu.make_async_copy(src(self.me), dst(self.me), self.local).start()

    def end(self, src, dst):
        pltpu.make_async_copy(src(self.me), dst(self.me), self.local).wait()

        @pl.loop(1, self.count)
        def _(off):
            self.copy(off, src, dst).wait()


def barrier_all(p, count):
    sem = pltpu.get_barrier_semaphore()
    me = (p.y * 4 + p.x * 2 + p.c) * p.Z + p.z

    @pl.loop(1, count)
    def _(off):
        t = lax.rem(me + off, count)
        pl.semaphore_signal(sem, inc=1, device_id=(t // p.Z, t % p.Z), device_id_type=MESH)

    pl.semaphore_wait(sem, count - 1)


def gather_steps(gs):
    U = len(gs)
    steps = []

    def first(g):
        g.own().start()
        start(g.zs())

    def second(g):
        g.own().wait()
        wait_recv(g.zs())
        start(g.p1())
        start(g.c0())

    def third(g):
        wait_recv(g.p1())
        start(g.p2())
        start(g.c1())

    def fourth(g):
        wait_recv(g.p2())
        start(g.c2())

    def fifth(g):
        wait_recv(g.c0() + g.c1() + g.c2())
        wait_send(g.zs() + g.p1() + g.p2() + g.c0() + g.c1() + g.c2())

    for s in range(U + 4):
        for lag, f in enumerate((first, second, third, fourth, fifth)):
            if 0 <= s - lag < U:
                steps.append(((lag, s - lag), functools.partial(f, gs[s - lag])))
    return steps


def forward_kernel(grid, units, nseq, sources, kvw, *refs):
    f32, bf16 = jnp.float32, jnp.bfloat16
    n = 6
    start_ref, ends_ref, index_ref, x_ref = refs[:4]
    ins, refs = refs[4 : 4 + n], refs[4 + n :]
    fulls, refs = refs[:n], refs[n:]
    n1_ref, q_ref, win_ref, att_ref, mixed_ref, n2_ref, gains_ref, refs = *refs[:7], refs[7:]
    wbuf, small, kv, got, picked, send, recv, local, xsend, xrecv, xlocal, lsem = refs
    p = Place(grid)
    A, B, C, Z = grid
    count = A * B * C * Z
    tok, width = x_ref.shape
    batches = tok // BLK
    barrier_all(p, count)
    gs = [Gather(p, ins[i], fulls[i], rows, cols, send.at[u], recv.at[u], local.at[u]) for u, (i, rows, cols) in enumerate(units)]
    steps = gather_steps(gs)
    last = {i: max(u for u, (j, _, _) in enumerate(units) if j == i) for i in range(n)}
    at = [0]

    def advance(count_=1):
        for _ in range(count_):
            if at[0] < len(steps):
                steps[at[0]][1]()
                at[0] += 1

    def advance_to(i):
        mark = [k for k, (label, _) in enumerate(steps) if label == (4, last[i])][0]
        while at[0] <= mark:
            advance()

    def load(i, dst, sem):
        return pltpu.make_async_copy(fulls[i], dst, lsem.at[sem])

    advance(5)
    x = x_ref[...].astype(f32)
    normed = x * lax.rsqrt(jnp.mean(x * x, axis=-1, keepdims=True) + EPS)
    mixed_ref[...] = normed
    advance_to(0)
    load(0, small, 0).start()
    load(0, small, 0).wait()
    gains = small[..., kvw:].reshape(width, 128).astype(f32).T
    gains_ref[...] = gains[:8]
    n1_ref[...] = (mixed_ref[...] * gains[0:1]).astype(bf16)
    ex1 = Exchange(p, count, xsend.at[0], xrecv.at[0], xlocal.at[0])
    ex2 = Exchange(p, count, xsend.at[1], xrecv.at[1], xlocal.at[1])

    kv_value = jnp.dot(n1_ref[...], small[..., :kvw].reshape(width, kvw), preferred_element_type=f32).astype(bf16)
    kv[...] = kv_value.reshape(kv.shape)

    def src1(t):
        g, c = ex1.piece(t)
        return kv.at[:, g, :, c]

    def dst1(t):
        return got.at[ex1.me]

    ex1.begin(src1, dst1)
    advance_to(1)
    load(1, wbuf, 1).start()
    ex1.end(src1, dst1)

    @pl.loop(0, count)
    def _(t):
        for m in range(batches):
            for i in range(sources):
                picked[t, m, i] = got[index_ref[t, m * sources + i], m]

    def src2(t):
        return picked.at[t]

    def dst2(t):
        g, c = ex2.piece(ex2.me)
        return win_ref.at[:, :, g, :, c]

    ex2.begin(src2, dst2)
    load(1, wbuf, 1).wait()
    tile = 512
    for j in range(0, width, tile):
        w = wbuf[..., j : j + tile].reshape(width, tile)
        q_ref[:, j : j + tile] = (jnp.dot(n1_ref[...], w, preferred_element_type=f32) * (HD**-0.5)).astype(bf16)
        advance()
    advance_to(2)
    load(2, wbuf, 2).start()
    advance(10)
    ex2.end(src2, dst2)
    for m in range(batches):
        mask = window_mask(start_ref[m], ends_ref, nseq, m, BLK, sources * BLK)
        for h0 in range(0, H, 2):

            @pl.loop(h0, h0 + 2)
            def _(h):
                cols = pl.ds(pl.multiple_of(h * HD, HD), HD)
                rows = pl.ds(m * BLK, BLK)
                mask = window_mask(start_ref[m], ends_ref, nseq, m, BLK, sources * BLK)
                k = win_ref[m, :, :, :, :HD].reshape(sources * BLK, HD)
                v = win_ref[m, :, :, :, HD:].reshape(sources * BLK, HD)
                prob = softmax_rows(q_ref[rows, cols], k, mask)
                att_ref[rows, cols] = jnp.dot(prob.astype(bf16), v, preferred_element_type=f32).astype(bf16)

            advance(2)
    load(2, wbuf, 2).wait()
    for j in range(0, width, tile):
        w = wbuf[..., j : j + tile].reshape(width, tile)
        mixed_ref[:, j : j + tile] = x_ref[:, j : j + tile].astype(f32) + jnp.dot(att_ref[...], w, preferred_element_type=f32)
        advance()
    mixed = mixed_ref[...]
    inverse = lax.rsqrt(jnp.mean(mixed * mixed, axis=-1, keepdims=True) + EPS)
    n2_ref[...] = (mixed * inverse * gains_ref[1:2]).astype(bf16)
    while at[0] < len(steps):
        advance()


def forward(grid, shards, units, x, start, ends, index, sources, kvw, collective_id):
    A, B, C, Z = grid
    count = A * B * C * Z
    tok, width = x.shape
    batches = tok // BLK
    bf16 = jnp.bfloat16
    groups = BLK // 16
    wide = 2 * HD * groups // count
    rows = shards[1].shape[0]
    U = len(units)
    any_, vmem, smem = (pl.BlockSpec(memory_space=s) for s in (pl.ANY, pltpu.VMEM, pltpu.SMEM))
    dma = pltpu.SemaphoreType.DMA
    sds = jax.ShapeDtypeStruct
    outs = pl.pallas_call(
        functools.partial(forward_kernel, grid, units, ends.shape[1], sources, kvw),
        out_shape=[sds(tuple(grid) + s.shape, s.dtype) for s in shards]
        + [
            sds((tok, width), bf16),
            sds((tok, width), bf16),
            sds((batches, sources, groups, 16, 2 * HD), bf16),
            sds((tok, width), bf16),
            sds((tok, width), jnp.float32),
            sds((tok, width), bf16),
            sds((8, width), jnp.float32),
        ],
        in_specs=[smem, smem, smem, vmem] + [any_] * 6,
        out_specs=[any_] * 6 + [vmem] * 7,
        scratch_shapes=[
            pltpu.VMEM(tuple(grid) + (rows, width), bf16),
            pltpu.VMEM(tuple(grid) + (rows, shards[0].shape[1]), bf16),
            pltpu.VMEM((batches, groups, 16, 2 * HD), bf16),
            pltpu.VMEM((count, batches, 16, wide), bf16),
            pltpu.VMEM((count, batches, sources, 16, wide), bf16),
            dma((U, 12)),
            dma((U, 12)),
            dma((U,)),
            dma((2, count - 1)),
            dma((2, count - 1)),
            dma((2,)),
            dma((3,)),
        ],
        compiler_params=pltpu.CompilerParams(collective_id=collective_id, has_side_effects=True, vmem_limit_bytes=VMEM),
        name="forward",
    )(start, ends, index, x, *shards)
    fulls = [o.reshape(-1, s.shape[-1]) for o, s in zip(outs, shards)]
    n1, q, window, att, mixed, n2, gains = outs[6:]
    return fulls, n1, q, window.reshape(batches, sources * BLK, 2 * HD), att, mixed, n2, gains

def place_of(perm):
    return jnp.argsort(perm, axis=1).astype(jnp.int32)


def windows_of(kv, perm, sources):
    axes = ("dp", "fsdp")
    batches, rows, cols = kv.shape
    count = perm.shape[1]
    part = rows // count
    pieces = kv.reshape(batches, count, part, cols).transpose(1, 0, 2, 3)
    spread = lax.all_to_all(pieces, axes, split_axis=0, concat_axis=0, tiled=True)
    holder = place_of(perm)
    block = perm[:, :, None] - (sources - 1) + jnp.arange(sources, dtype=jnp.int32)
    source = jnp.take_along_axis(holder[:, None, :], jnp.maximum(block, 0), axis=2)
    index = (source * batches + jnp.arange(batches, dtype=jnp.int32)[:, None, None]).transpose(1, 0, 2).reshape(-1)
    picked = jnp.take(spread.reshape(count * batches, part, cols), index, axis=0).reshape(count, batches * sources, part, cols)
    arrived = lax.all_to_all(picked, axes, split_axis=0, concat_axis=0, tiled=True)
    return arrived.transpose(1, 0, 2, 3).reshape(batches, sources * rows, cols)


def window_sums(grads, perm, sources):
    axes = ("dp", "fsdp")
    batches, wide, cols = grads.shape
    rows = wide // sources
    count = perm.shape[1]
    part = rows // count
    pieces = grads.reshape(batches * sources, count, part, cols).transpose(1, 0, 2, 3)
    spread = lax.all_to_all(pieces, axes, split_axis=0, concat_axis=0, tiled=True)
    holder = place_of(perm)
    block = perm[:, :, None] + (sources - 1) - jnp.arange(sources, dtype=jnp.int32)
    reader = jnp.take_along_axis(holder[:, None, :], jnp.minimum(block, count - 1), axis=2)
    slot = jnp.arange(batches, dtype=jnp.int32)[:, None, None] * sources + jnp.arange(sources, dtype=jnp.int32)
    index = (reader * (batches * sources) + slot).transpose(1, 0, 2)
    picked = jnp.take(spread.reshape(count * batches * sources, part, cols), index.reshape(-1), axis=0)
    picked = picked.reshape(count, batches, sources, part, cols).astype(jnp.float32)
    valid = (block < count).transpose(1, 0, 2)[..., None, None]
    summed = jnp.sum(jnp.where(valid, picked, 0.0), axis=2).astype(jnp.bfloat16)
    arrived = lax.all_to_all(summed, axes, split_axis=0, concat_axis=0, tiled=True)
    return arrived.transpose(1, 0, 2, 3).reshape(batches, rows, cols)


def fast_body(grid, tokens, w_query, w_keyval, w_out, w_gate, w_up, w_down, gain_attn, gain_ffn, cotangent, block_perm, extra_len):
    f32, bf16 = jnp.float32, jnp.bfloat16
    batches, _, rows, width = tokens.shape
    tok = batches * rows
    me = lax.axis_index(("dp", "fsdp"))
    sources = WIN // BLK + 1
    scale = HD ** (-0.5)
    kvw = w_keyval.shape[1]
    gains = jnp.stack([gain_attn, gain_ffn], axis=1)
    small = jnp.concatenate([w_keyval, jnp.pad(gains, ((0, 0), (0, 126)))], axis=1)
    shards = [small, w_query, w_out, w_gate, w_up, w_down]
    units = units_of(shards, width)
    holder = place_of(block_perm)
    block = block_perm[:, :, None] - (sources - 1) + jnp.arange(sources, dtype=jnp.int32)
    index = jnp.take_along_axis(holder[:, None, :], jnp.maximum(block, 0), axis=2)
    index = index.transpose(1, 0, 2).reshape(-1, batches * sources)
    start = lax.dynamic_slice_in_dim(block_perm, me, 1, axis=1)[:, 0] * BLK
    ends = jnp.cumsum(extra_len + (WIN - 1), axis=1).astype(jnp.int32)
    x = tokens.reshape(tok, width)
    fulls, n1b, query, window, att, mixed, n2b, gains = forward(grid, shards, units, x, start, ends, index, sources, kvw, 0)
    small, wq, wo, wg, wu, wd = fulls
    wkv = small[:, :kvw]
    g1, g2 = gains[0], gains[1]
    x = x.astype(f32)
    dy = cotangent.reshape(tok, width)
    r1 = lax.rsqrt(jnp.mean(x * x, axis=-1, keepdims=True) + EPS)
    r2 = lax.rsqrt(jnp.mean(mixed * mixed, axis=-1, keepdims=True) + EPS)
    out, d_n2, d_wgate, d_wup, d_down = ffn(n2b, dy, wg, wu, wd, 512)
    block_out = (mixed + out).astype(bf16)
    d_mixed_norm, d_g2 = norm_back(mixed, r2, g2, d_n2)
    d_mixed = dy.astype(f32) + d_mixed_norm
    d_branch = d_mixed.astype(bf16)
    d_wout = jnp.einsum("ta,td->ad", att, d_branch, preferred_element_type=f32).astype(bf16)
    d_att = jnp.einsum("td,ad->ta", d_branch, wo, preferred_element_type=f32).astype(bf16)
    d_query, d_window = attend_back(query, window, d_att, start, ends)
    d_keyval = window_sums(d_window, block_perm, sources).reshape(tok, kvw)
    d_wquery = (jnp.einsum("td,ta->da", n1b, d_query, preferred_element_type=f32) * scale).astype(bf16)
    d_wkeyval = jnp.einsum("td,tc->dc", n1b, d_keyval, preferred_element_type=f32)
    d_n1 = jnp.einsum("ta,da->td", d_query, wq, preferred_element_type=f32) * scale
    d_n1 = d_n1 + jnp.einsum("tc,dc->td", d_keyval, wkv, preferred_element_type=f32)
    d_x_norm, d_g1 = norm_back(x, r1, g1, d_n1)
    grad_tokens = (d_mixed + d_x_norm).astype(bf16)
    d_gains = jnp.pad(jnp.stack([d_g1, d_g2], axis=1), ((0, 0), (0, 126)))
    d_small = jnp.concatenate([d_wkeyval, d_gains], axis=1).astype(bf16)
    small, dq, do, dg, du, dd = scatter(grid, [d_small, d_wquery, d_wout, d_wgate, d_wup, d_down], units, 1)
    return (
        block_out.reshape(tokens.shape),
        grad_tokens.reshape(tokens.shape),
        dq,
        small[:, :kvw],
        do,
        dg,
        du,
        dd,
        small[:, kvw],
        small[:, kvw + 1],
    )


def units_of(shards, width):
    rows = min(s.shape[0] for s in shards)
    units = []
    for i, s in enumerate(shards):
        for r in range(0, s.shape[0], rows):
            for c in range(0, s.shape[1], width):
                units.append((i, (r, rows), (c, min(width, s.shape[1] - c))))
    return units


def solution(mesh):
    count = mesh.shape["dp"] * mesh.shape["fsdp"]
    grid = (2, 2, 2, mesh.shape["fsdp"])
    whole_tiles = mesh.shape["dp"] == 8 and 1536 % (16 * count) == 0
    run = functools.partial(fast_body, grid) if whole_tiles else body
    placed = (
        P(None, ("dp", "fsdp"), None, None),
        P(("dp", "fsdp"), None),
        P(("dp", "fsdp"), None),
        P(("dp", "fsdp"), None),
        P(("dp", "fsdp"), None),
        P(("dp", "fsdp"), None),
        P(("dp", "fsdp"), None),
        P(("dp", "fsdp")),
        P(("dp", "fsdp")),
        P(None, ("dp", "fsdp"), None, None),
        P(),
        P(),
    )
    return jax.shard_map(
        run,
        mesh=mesh,
        in_specs=placed,
        out_specs=(
            P(None, ("dp", "fsdp"), None, None),
            P(None, ("dp", "fsdp"), None, None),
            P(("dp", "fsdp"), None),
            P(("dp", "fsdp"), None),
            P(("dp", "fsdp"), None),
            P(("dp", "fsdp"), None),
            P(("dp", "fsdp"), None),
            P(("dp", "fsdp"), None),
            P(("dp", "fsdp")),
            P(("dp", "fsdp")),
        ),
        check_vma=False,
    )
```

```python
import functools
import math

import jax
import jax.numpy as jnp
from jax import lax
from jax.experimental import pallas as pl
from jax.experimental.pallas import tpu as pltpu
from jax.sharding import PartitionSpec as P

H = 6
HD = 256
WIN = 1024
BLK = 256


EPS = 1e-06
VMEM = 60 * 1024 * 1024


def for_sending(x):
    return jax.tree.map(lambda a: a.astype(jnp.bfloat16) if a.dtype == jnp.float32 else a, x)


def shifted(value, axis, steps):
    count = lax.axis_size(axis)
    leading, last = (max(0, -steps), min(count, count - steps))
    return lax.ppermute(value, axis, [(source, source + steps) for source in range(leading, last)])


def norm_rows(value, gain):
    inverse = lax.rsqrt(jnp.mean(value * value, axis=-1, keepdims=True) + EPS)
    return (value * inverse * gain, inverse)


def norm_back(value, inverse, gain, grad):
    scaled = grad * gain
    width = value.shape[-1]
    dvalue = (
        inverse * scaled
        - value * inverse**3 * jnp.sum(scaled * value, axis=-1, keepdims=True) / width
    )
    dgain = jnp.sum(grad * value * inverse, axis=0)
    return (dvalue, dgain)


def sequence_of(positions, ends):
    return jnp.sum((positions[:, None] >= ends[None, :]).astype(jnp.int32), axis=1)


def visible_mask(query_pos, key_pos, ends):
    same = sequence_of(query_pos, ends)[:, None] == sequence_of(key_pos, ends)[None, :]
    gap = query_pos[:, None] - key_pos[None, :]
    return same & (gap >= 0) & (gap < WIN) & (key_pos[None, :] >= 0)


def geglu(gate, up):
    return jax.nn.gelu(gate, approximate=True) * up


def move_keys(value, order, count):
    rows = value.shape[0]
    spread = lax.all_to_all(value, ("dp", "fsdp"), split_axis=1, concat_axis=0, tiled=True)
    pieces = spread.reshape(count, rows, spread.shape[1])
    placed = jnp.take(pieces, order, axis=0).reshape(count * rows, spread.shape[1])
    return lax.all_to_all(placed, ("dp", "fsdp"), split_axis=0, concat_axis=1, tiled=True)


def move_grads(value, order, count):
    rows = value.shape[0]
    spread = lax.all_to_all(
        for_sending(value), ("dp", "fsdp"), split_axis=1, concat_axis=0, tiled=True
    ).astype(value.dtype)
    pieces = spread.reshape(count, rows, spread.shape[1])
    placed = jnp.take(pieces, order, axis=0).reshape(count * rows, spread.shape[1])
    return lax.all_to_all(
        for_sending(placed), ("dp", "fsdp"), split_axis=0, concat_axis=1, tiled=True
    ).astype(placed.dtype)


def body(
    tokens,
    w_query,
    w_keyval,
    w_out,
    w_gate,
    w_up,
    w_down,
    gain_attn,
    gain_ffn,
    cotangent,
    block_perm,
    extra_len,
):
    count = lax.axis_size(("dp", "fsdp"))
    me = lax.axis_index(("dp", "fsdp"))
    batches = tokens.shape[0]
    sources = WIN // BLK + 1
    scale = HD ** (-0.5)
    shards = (w_query, w_keyval, w_out, w_gate, w_up, w_down, gain_attn, gain_ffn)
    device_ids = jnp.arange(count, dtype=jnp.int32)
    totals = None
    outputs = []
    input_grads = []
    for batch in range(batches):
        full = (
            lax.all_gather(shards[0], ("dp", "fsdp"), axis=0, tiled=True),
            lax.all_gather(shards[1], ("dp", "fsdp"), axis=0, tiled=True),
            lax.all_gather(shards[2], ("dp", "fsdp"), axis=0, tiled=True),
            lax.all_gather(shards[3], ("dp", "fsdp"), axis=0, tiled=True),
            lax.all_gather(shards[4], ("dp", "fsdp"), axis=0, tiled=True),
            lax.all_gather(shards[5], ("dp", "fsdp"), axis=0, tiled=True),
            lax.all_gather(shards[6], ("dp", "fsdp"), axis=0, tiled=True),
            lax.all_gather(shards[7], ("dp", "fsdp"), axis=0, tiled=True),
        )
        wq, wkv, wo, wg, wu, wd, g1b, g2b = full
        g1 = g1b.astype(jnp.float32)
        g2 = g2b.astype(jnp.float32)
        perm_row = block_perm[batch]
        ends = jnp.cumsum(extra_len[batch] + (WIN - 1))
        mine = lax.dynamic_slice_in_dim(perm_row, me, 1)[0]
        holder = jnp.sum(
            jnp.where(perm_row[None, :] == device_ids[:, None], device_ids[None, :], 0), axis=1
        )
        query_pos = mine * BLK + jnp.arange(BLK, dtype=jnp.int32)
        key_pos = (mine - (sources - 1)) * BLK + jnp.arange(sources * BLK, dtype=jnp.int32)
        mask = jnp.repeat(visible_mask(query_pos, key_pos, ends), H, axis=0)
        x = tokens[batch, 0].astype(jnp.float32)
        n1, r1 = norm_rows(x, g1)
        n1b = n1.astype(jnp.bfloat16)
        query = (jnp.dot(n1b, wq, preferred_element_type=jnp.float32) * scale).astype(jnp.bfloat16)
        query_rows = query.reshape(BLK * H, HD)
        keyval = jnp.dot(n1b, wkv, preferred_element_type=jnp.float32).astype(jnp.bfloat16)
        ordered = move_keys(keyval, holder, count)
        window = [ordered] * sources
        for back in range(1, sources):
            window[sources - 1 - back] = shifted(ordered, ("dp", "fsdp"), back)
        picked = move_keys(jnp.concatenate(window, axis=0), perm_row, count)
        keys_src = picked[:, :HD]
        values_src = picked[:, HD:]
        scores = jnp.einsum("qd,kd->qk", query_rows, keys_src, preferred_element_type=jnp.float32)
        masked = jnp.where(mask, scores, -1e30)
        top = jnp.max(masked, axis=1, keepdims=True)
        expd = jnp.exp(masked - top)
        rowsum = jnp.sum(expd, axis=1, keepdims=True)
        lse = top + jnp.log(rowsum)
        probs_low = (expd / rowsum).astype(jnp.bfloat16)
        att = jnp.dot(probs_low, values_src, preferred_element_type=jnp.float32)
        att_low = att.reshape(BLK, H * HD).astype(jnp.bfloat16)
        mixed = x + jnp.dot(att_low, wo, preferred_element_type=jnp.float32)
        n2, r2 = norm_rows(mixed, g2)
        n2b = n2.astype(jnp.bfloat16)
        gate = jnp.dot(n2b, wg, preferred_element_type=jnp.float32)
        up = jnp.dot(n2b, wu, preferred_element_type=jnp.float32)
        hidden = geglu(gate, up).astype(jnp.bfloat16)
        outputs.append(
            (mixed + jnp.dot(hidden, wd, preferred_element_type=jnp.float32)).astype(jnp.bfloat16)
        )
        wq, wkv, wo, wg, wu, wd, g1b, g2b = (
            lax.all_gather(shards[0], ("dp", "fsdp"), axis=0, tiled=True),
            lax.all_gather(shards[1], ("dp", "fsdp"), axis=0, tiled=True),
            lax.all_gather(shards[2], ("dp", "fsdp"), axis=0, tiled=True),
            lax.all_gather(shards[3], ("dp", "fsdp"), axis=0, tiled=True),
            lax.all_gather(shards[4], ("dp", "fsdp"), axis=0, tiled=True),
            lax.all_gather(shards[5], ("dp", "fsdp"), axis=0, tiled=True),
            lax.all_gather(shards[6], ("dp", "fsdp"), axis=0, tiled=True),
            lax.all_gather(shards[7], ("dp", "fsdp"), axis=0, tiled=True),
        )
        dy = cotangent[batch, 0]
        d_down = jnp.einsum("tf,td->fd", hidden, dy, preferred_element_type=jnp.float32)
        d_hidden = jnp.einsum("td,fd->tf", dy, wd, preferred_element_type=jnp.float32)
        _, geglu_pull = jax.vjp(geglu, gate, up)
        d_gate, d_up = geglu_pull(d_hidden)
        d_gate_low = d_gate.astype(jnp.bfloat16)
        d_up_low = d_up.astype(jnp.bfloat16)
        d_wgate = jnp.einsum("td,tf->df", n2b, d_gate_low, preferred_element_type=jnp.float32)
        d_wup = jnp.einsum("td,tf->df", n2b, d_up_low, preferred_element_type=jnp.float32)
        d_n2 = jnp.einsum("tf,df->td", d_gate_low, wg, preferred_element_type=jnp.float32)
        d_n2 = d_n2 + jnp.einsum("tf,df->td", d_up_low, wu, preferred_element_type=jnp.float32)
        d_mixed_norm, d_g2 = norm_back(mixed, r2, g2, d_n2)
        d_mixed = dy.astype(jnp.float32) + d_mixed_norm
        d_branch = d_mixed.astype(jnp.bfloat16)
        d_wout = jnp.einsum("ta,td->ad", att_low, d_branch, preferred_element_type=jnp.float32)
        d_att = jnp.einsum("td,ad->ta", d_branch, wo, preferred_element_type=jnp.float32)
        d_att_rows = d_att.astype(jnp.bfloat16).reshape(BLK * H, HD)
        again = jnp.einsum("qd,kd->qk", query_rows, keys_src, preferred_element_type=jnp.float32)
        probs = jnp.exp(jnp.where(mask, again, -1e30) - lse)
        d_probs = jnp.einsum(
            "qd,kd->qk", d_att_rows, values_src, preferred_element_type=jnp.float32
        )
        delta = jnp.sum(probs * d_probs, axis=1, keepdims=True)
        d_scores = (probs * (d_probs - delta)).astype(jnp.bfloat16)
        d_query = jnp.dot(d_scores, keys_src, preferred_element_type=jnp.float32).astype(
            jnp.bfloat16
        )
        d_query = d_query.reshape(BLK, H * HD)
        d_keys = jnp.einsum("qk,qd->kd", d_scores, query_rows, preferred_element_type=jnp.float32)
        d_values = jnp.einsum(
            "qk,qd->kd", probs.astype(jnp.bfloat16), d_att_rows, preferred_element_type=jnp.float32
        )
        d_keyval_flat = jnp.concatenate([d_keys, d_values], axis=1)
        ordered_grads = move_grads(d_keyval_flat, holder, count).reshape(sources, BLK, 2 * HD)
        summed = ordered_grads[sources - 1]
        for back in range(1, sources):
            summed = summed + shifted(
                ordered_grads[sources - 1 - back].astype(jnp.bfloat16), ("dp", "fsdp"), -back
            ).astype(jnp.float32)
        d_keyval = move_grads(summed, perm_row, count).astype(jnp.bfloat16)
        d_wquery = jnp.einsum("td,ta->da", n1b, d_query, preferred_element_type=jnp.float32) * scale
        d_wkeyval = jnp.einsum("td,tc->dc", n1b, d_keyval, preferred_element_type=jnp.float32)
        d_n1 = jnp.einsum("ta,da->td", d_query, wq, preferred_element_type=jnp.float32) * scale
        d_n1 = d_n1 + jnp.einsum("tc,dc->td", d_keyval, wkv, preferred_element_type=jnp.float32)
        d_x_norm, d_g1 = norm_back(x, r1, g1, d_n1)
        input_grads.append((d_mixed + d_x_norm).astype(jnp.bfloat16))
        local = (d_wquery, d_wkeyval, d_wout, d_wgate, d_wup, d_down, d_g1, d_g2)
        totals = local if totals is None else tuple((a + b for a, b in zip(totals, local)))
    totals = lax.psum_scatter(totals, ("dp", "fsdp"), scatter_dimension=0, tiled=True)
    block_out = jnp.stack(outputs)[:, None]
    grad_tokens = jnp.stack(input_grads)[:, None]
    return (
        block_out,
        grad_tokens,
        totals[0],
        totals[1],
        totals[2],
        totals[3],
        totals[4],
        totals[5],
        totals[6],
        totals[7],
    )


MESH = pl.DeviceIdType.MESH
BF16, F32 = jnp.bfloat16, jnp.float32


class Place:
    def __init__(self, grid):
        self.grid = grid
        self.Z = grid[3]
        self.count = grid[0] * grid[1] * grid[2] * grid[3]
        dp = lax.axis_index("dp")
        self.z = lax.axis_index("fsdp")
        self.c = dp % 2
        self.x = (dp // 2) % 2
        self.y = dp // 4
        self.me = dp * self.Z + self.z
        self.half = self.z % 2
        self.pair = self.z // 2
        self.core = self.dev(c=1 - self.c)
        self.xdev = self.dev(x=1 - self.x)
        self.ydev = self.dev(y=1 - self.y)
        self.mate = self.dev(z=self.z + 1 - 2 * self.half)
        self.far = self.dev(z=(self.z + 2) % self.Z)

    def dev(self, y=None, x=None, c=None, z=None):
        y = self.y if y is None else y
        x = self.x if x is None else x
        c = self.c if c is None else c
        z = self.z if z is None else z
        return ((y * 2 + x) * 2 + c, z)

    def barrier(self):
        sem = pltpu.get_barrier_semaphore()

        @pl.loop(1, self.count)
        def _(off):
            t = lax.rem(self.me + off, self.count)
            pl.semaphore_signal(sem, inc=1, device_id=(t // self.Z, t % self.Z), device_id_type=MESH)

        pl.semaphore_wait(sem, self.count - 1)


def start(copies):
    for c in copies:
        c.start()


def wait_recv(copies):
    for c in copies:
        c.wait_recv()


def wait_send(copies):
    for c in copies:
        c.wait_send()


def halves(width):
    first = width - (width // 256) * 128
    return [(0, first), (first, width - first)]


class Unit:
    def __init__(self, array, kind, rows, cols):
        self.array, self.kind, self.rows, self.cols = array, kind, rows, cols
        self.width = cols[1]

    def shape(self, grid):
        return grid[:2] + (grid[3] // 2 if self.kind == "rows" else grid[3],) + (self.rows[1], self.width)

    def link_buffers(self, grid):
        a, b, z, r, w = self.shape(grid)
        h = halves(w)
        out = [(a, b, z, r, w), (b, z, r, h[0][1]), (a, z, r, h[1][1]), (z, r, h[0][1]), (z, r, h[1][1])]
        if self.kind == "all":
            return out + [(z - 1, r, w)]
        if self.kind == "cols":
            return out + [(z // 2, r, w), (r, w)]
        return out + [(r, w)]


class Gather:
    def __init__(self, p, unit, src, dst, send, recv, local):
        self.p, self.dst, self.send, self.recv, self.local, self.kind = p, dst, send, recv, local, unit.kind
        self.r, self.all = pl.ds(*unit.rows), pl.ds(*unit.cols)
        self.h = [pl.ds(unit.cols[0] + a, b) for a, b in halves(unit.width)]
        self.src = (lambda half: src.at[half, self.r, self.all]) if unit.kind == "cols" else (lambda half: src.at[self.r, self.all])
        self.spot = p.pair if unit.kind == "rows" else p.z

    def copy(self, k, src, dst, dev):
        return pltpu.make_async_remote_copy(src, dst, self.send.at[k], self.recv.at[k], device_id=dev, device_id_type=MESH)

    def same(self, k, ref, dev):
        return self.copy(k, ref, ref, dev)

    def block(self, y, x, cols):
        return self.dst.at[y, x, self.p.c, :, self.r, cols]

    def own(self):
        p = self.p
        return pltpu.make_async_copy(self.src(p.half), self.dst.at[p.y, p.x, p.c, self.spot, self.r, self.all], self.local)

    def z1(self):
        p = self.p
        there = self.dst.at[p.y, p.x, p.c, self.spot, self.r, self.all]
        if self.kind == "all":
            return [self.copy(i - 1, self.src(0), there, p.dev(z=(p.z + i) % p.Z)) for i in range(1, p.Z)]
        if self.kind == "cols":
            return [self.copy(0, self.src(1 - p.half), there, p.mate)]
        return [self.copy(0, self.src(0), there, p.far)]

    def z2(self):
        p = self.p
        return [self.same(1, self.dst.at[p.y, p.x, p.c, pl.ds(2 * p.pair, 2), self.r, self.all], p.far)]

    def p1(self):
        p = self.p
        return [self.same(3, self.block(p.y, p.x, self.h[0]), p.xdev), self.same(4, self.block(p.y, p.x, self.h[1]), p.ydev)]

    def p2(self):
        p, every = self.p, slice(None)
        return [self.same(5, self.block(p.y, every, self.h[0]), p.ydev), self.same(6, self.block(every, p.x, self.h[1]), p.xdev)]

    def c0(self):
        p = self.p
        return [self.same(7, self.block(p.y, p.x, self.all), p.core)]

    def c1(self):
        p = self.p
        return [self.same(8, self.block(p.y, 1 - p.x, self.h[0]), p.core), self.same(9, self.block(1 - p.y, p.x, self.h[1]), p.core)]

    def c2(self):
        p, every = self.p, slice(None)
        return [self.same(10, self.block(1 - p.y, every, self.h[0]), p.core), self.same(11, self.block(every, 1 - p.x, self.h[1]), p.core)]

    def stages(self):
        def first():
            self.own().start()
            start(self.z1())

        def second():
            self.own().wait()
            wait_recv(self.z1())
            start(self.z2())

        def third():
            if self.kind == "cols":
                wait_recv(self.z2())
            else:
                self.own().wait()
                wait_recv(self.z1())
            start(self.p1() + self.c0())

        def fourth():
            wait_recv(self.p1())
            start(self.p2() + self.c1())

        def fifth():
            wait_recv(self.p2())
            start(self.c2())

        def last():
            wait_recv(self.c0() + self.c1() + self.c2())
            wait_send(self.z1() + (self.z2() if self.kind == "cols" else []) + self.p1() + self.p2() + self.c0() + self.c1() + self.c2())

        return [first] + ([second] if self.kind == "cols" else []) + [third, fourth, fifth, last]


class Scatter:
    def __init__(self, p, unit, src, out, buffers, tmp, send, recv, local):
        self.p, self.unit, self.kind = p, unit, unit.kind
        self.src, self.out, self.tmp, self.send, self.recv, self.local = src, out, tmp, send, recv, local
        self.r, self.cols = pl.ds(*unit.rows), pl.ds(*unit.cols)
        self.h = [pl.ds(a, b) for a, b in halves(unit.width)]
        self.P, self.rest = buffers[0], buffers[1:]
        self.spot = p.pair if unit.kind == "rows" else p.z
        self.n = unit.shape(p.grid)[2]
        self.part = tmp

    def copy(self, k, src, dst, dev):
        return pltpu.make_async_remote_copy(src, dst, self.send.at[k], self.recv.at[k], device_id=dev, device_id_type=MESH)

    def r0(self):
        p = self.p
        return [self.copy(0, self.src.at[:, :, 1 - p.c, :, self.r, self.cols], self.P, p.core)]

    def load(self):
        return pltpu.make_async_copy(self.src.at[:, :, self.p.c, :, self.r, self.cols], self.part, self.local)

    def r1(self):
        p, P = self.p, self.P
        return [self.copy(1, P.at[1 - p.y, :, :, :, self.h[0]], self.rest[0], p.ydev), self.copy(2, P.at[:, 1 - p.x, :, :, self.h[1]], self.rest[1], p.xdev)]

    def r2(self):
        p, P = self.p, self.P
        return [self.copy(3, P.at[p.y, 1 - p.x, :, :, self.h[0]], self.rest[2], p.xdev), self.copy(4, P.at[1 - p.y, p.x, :, :, self.h[1]], self.rest[3], p.ydev)]

    def r3(self):
        p, P = self.p, self.P
        if self.kind == "all":
            return [self.copy(4 + i, P.at[p.y, p.x, (p.z + i) % p.Z], self.rest[4].at[i - 1], p.dev(z=(p.z + i) % p.Z)) for i in range(1, p.Z)]
        if self.kind == "cols":
            return [self.copy(5, P.at[p.y, p.x, pl.ds(2 * (1 - p.pair), 2)], self.rest[4], p.far)]
        return [self.copy(5, P.at[p.y, p.x, 1 - p.pair], self.rest[4], p.far)]

    def r4(self):
        p = self.p
        return [self.copy(6, self.P.at[p.y, p.x, 2 * p.pair + 1 - p.half], self.rest[5], p.mate)]

    def add0(self):
        P, tmp = self.P, self.part
        b, n = P.shape[1], self.n

        @pl.loop(0, P.shape[0] * b * n)
        def _(i):
            at = (i // (b * n), (i // n) % b, i % n)
            P[at] = (P[at].astype(F32) + tmp[at].astype(F32)).astype(BF16)

    def add1(self):
        p, P, n = self.p, self.P, self.n

        @pl.loop(0, 2 * n)
        def _(i):
            b, d = i // n, i % n
            P[p.y, b, d, :, self.h[0]] = (P[p.y, b, d, :, self.h[0]].astype(F32) + self.rest[0][b, d].astype(F32)).astype(BF16)
            P[b, p.x, d, :, self.h[1]] = (P[b, p.x, d, :, self.h[1]].astype(F32) + self.rest[1][b, d].astype(F32)).astype(BF16)

    def add2(self):
        p, P = self.p, self.P

        @pl.loop(0, self.n)
        def _(d):
            for k in (0, 1):
                P[p.y, p.x, d, :, self.h[k]] = (P[p.y, p.x, d, :, self.h[k]].astype(F32) + self.rest[2 + k][d].astype(F32)).astype(BF16)

    def add3(self):
        p, P, got = self.p, self.P, self.rest[4]
        if self.kind == "all":
            s = P[p.y, p.x, p.z].astype(F32)
            for i in range(p.Z - 1):
                s = s + got[i].astype(F32)
            self.out[self.r, self.cols] = s
        elif self.kind == "rows":
            self.out[self.r, self.cols] = P[p.y, p.x, p.pair].astype(F32) + got[...].astype(F32)
        else:
            theirs = 2 * p.pair + 1 - p.half
            self.out[p.half, self.r, self.cols] = P[p.y, p.x, p.z].astype(F32) + got[p.half].astype(F32)
            P[p.y, p.x, theirs] = (P[p.y, p.x, theirs].astype(F32) + got[1 - p.half].astype(F32)).astype(BF16)

    def stages(self):
        def first():
            start(self.r0())
            self.load().start()

        def second():
            self.load().wait()
            wait_recv(self.r0())
            self.add0()
            start(self.r1())

        def third():
            wait_recv(self.r1())
            wait_send(self.r1())
            self.add1()
            start(self.r2())

        def fourth():
            wait_recv(self.r2())
            wait_send(self.r2())
            self.add2()
            start(self.r3())

        def fifth():
            wait_recv(self.r3())
            wait_send(self.r3() + self.r0())
            self.add3()
            if self.kind == "cols":
                start(self.r4())

        def last():
            wait_recv(self.r4())
            wait_send(self.r4())
            self.out[1 - self.p.half, self.r, self.cols] = self.rest[5][...].astype(F32)

        return [first, second, third, fourth, fifth] + ([last] if self.kind == "cols" else [])


def staggered(items, starts=None):
    lists = [i.stages() for i in items]
    starts = starts or list(range(len(items)))
    steps = []
    for s in range(max(b + len(l) for b, l in zip(starts, lists))):
        for u in reversed(range(len(lists))):
            k = s - starts[u]
            if 0 <= k < len(lists[u]):
                steps.append((u, k == len(lists[u]) - 1, lists[u][k]))
    return steps


class Steps:
    def __init__(self, steps):
        self.steps, self.at = steps, 0

    def advance(self, count=1):
        for _ in range(count):
            if self.at < len(self.steps):
                self.steps[self.at][2]()
                self.at += 1

    def through(self, item):
        mark = [k for k, (u, done, _) in enumerate(self.steps) if u == item and done][0]
        self.advance(mark + 1 - self.at)

    def finish(self):
        self.advance(len(self.steps) - self.at)


def scatter_kernel(grid, units, n, *refs):
    ins, outs, refs = refs[:n], refs[n : 2 * n], refs[2 * n :]
    send, recv, local = refs[-3:]
    buffers = list(refs[:-3])
    p = Place(grid)
    p.barrier()
    items = []
    for u, unit in enumerate(units):
        tmp, mine = buffers.pop(0), [buffers.pop(0) for _ in unit.link_buffers(grid)]
        items.append(Scatter(p, unit, ins[unit.array], outs[unit.array], mine, tmp, send.at[u], recv.at[u], local.at[u]))
    Steps(staggered(items)).finish()


def scatter(grid, grads, outs, units, collective_id):
    n, U = len(grads), len(units)
    dma = pltpu.SemaphoreType.DMA
    return pl.pallas_call(
        functools.partial(scatter_kernel, grid, units, n),
        out_shape=[jax.ShapeDtypeStruct(o, F32) for o in outs],
        in_specs=[pl.BlockSpec(memory_space=pl.ANY)] * n,
        out_specs=[pl.BlockSpec(memory_space=pltpu.VMEM)] * n,
        scratch_shapes=[pltpu.VMEM(s, BF16) for u in units for s in [u.shape(grid)] + u.link_buffers(grid)]
        + [dma((U, 8)), dma((U, 8)), dma((U,))],
        compiler_params=pltpu.CompilerParams(collective_id=collective_id, has_side_effects=True, vmem_limit_bytes=VMEM),
        name="scatter",
    )(*grads)

def window_mask(start, ends, nseq, m, queries, keys):
    qpos = start + lax.broadcasted_iota(jnp.int32, (queries, 1), 0)
    first = jnp.maximum(qpos - (WIN - 1), 0)
    for k in range(nseq):
        end = ends[m, k]
        first = jnp.maximum(first, jnp.where(qpos >= end, end, 0))
    kpos = start - (keys - queries) + lax.broadcasted_iota(jnp.int32, (1, keys), 1)
    return (kpos >= first) & (kpos <= qpos)


def softmax_rows(q, k, mask):
    scores = lax.dot_general(q, k, (((1,), (1,)), ((), ())), preferred_element_type=jnp.float32)
    masked = jnp.where(mask, scores, -1e30)
    expd = jnp.exp(masked - jnp.max(masked, axis=1, keepdims=True))
    return expd * (1.0 / jnp.sum(expd, axis=1, keepdims=True))


def attend_kernel(nseq, start, ends, q_ref, kv_ref, o_ref):
    m = pl.program_id(0)
    mask = window_mask(start[m], ends, nseq, m, q_ref.shape[0], kv_ref.shape[1])
    p = softmax_rows(q_ref[...], kv_ref[0, :, :HD], mask)
    o_ref[...] = jnp.dot(p.astype(jnp.bfloat16), kv_ref[0, :, HD:], preferred_element_type=jnp.float32).astype(jnp.bfloat16)


def attend(q, window, start, ends):
    batches, keys, _ = window.shape
    return pl.pallas_call(
        functools.partial(attend_kernel, ends.shape[1]),
        out_shape=jax.ShapeDtypeStruct(q.shape, jnp.bfloat16),
        grid_spec=pltpu.PrefetchScalarGridSpec(
            num_scalar_prefetch=2,
            grid=(batches, H),
            in_specs=[
                pl.BlockSpec((BLK, HD), lambda m, h, *_: (m, h)),
                pl.BlockSpec((1, keys, 2 * HD), lambda m, h, *_: (m, 0, 0)),
            ],
            out_specs=pl.BlockSpec((BLK, HD), lambda m, h, *_: (m, h)),
        ),
        compiler_params=pltpu.CompilerParams(vmem_limit_bytes=VMEM),
        name="attend",
    )(start, ends, q, window)


def attend_back_kernel(nseq, start, ends, q_ref, kv_ref, d_ref, dq_ref, dkv_ref, dkv):
    m, h = pl.program_id(0), pl.program_id(1)
    mask = window_mask(start[m], ends, nseq, m, q_ref.shape[0], kv_ref.shape[1])
    q, k, v, d = q_ref[...], kv_ref[0, :, :HD], kv_ref[0, :, HD:], d_ref[...]
    p = softmax_rows(q, k, mask)
    dp = lax.dot_general(d, v, (((1,), (1,)), ((), ())), preferred_element_type=jnp.float32)
    ds = (p * (dp - jnp.sum(p * dp, axis=1, keepdims=True))).astype(jnp.bfloat16)
    dq_ref[...] = jnp.dot(ds, k, preferred_element_type=jnp.float32).astype(jnp.bfloat16)
    dk = lax.dot_general(ds, q, (((0,), (0,)), ((), ())), preferred_element_type=jnp.float32)
    dv = lax.dot_general(p.astype(jnp.bfloat16), d, (((0,), (0,)), ((), ())), preferred_element_type=jnp.float32)

    @pl.when(h == 0)
    def _():
        dkv[:, :HD] = dk
        dkv[:, HD:] = dv

    @pl.when(h > 0)
    def _():
        dkv[:, :HD] += dk
        dkv[:, HD:] += dv

    @pl.when(h == pl.num_programs(1) - 1)
    def _():
        dkv_ref[0] = dkv[...].astype(jnp.bfloat16)


def attend_back(q, window, datt, start, ends):
    batches, keys, _ = window.shape
    return pl.pallas_call(
        functools.partial(attend_back_kernel, ends.shape[1]),
        out_shape=[jax.ShapeDtypeStruct(q.shape, jnp.bfloat16), jax.ShapeDtypeStruct(window.shape, jnp.bfloat16)],
        grid_spec=pltpu.PrefetchScalarGridSpec(
            num_scalar_prefetch=2,
            grid=(batches, H),
            in_specs=[
                pl.BlockSpec((BLK, HD), lambda m, h, *_: (m, h)),
                pl.BlockSpec((1, keys, 2 * HD), lambda m, h, *_: (m, 0, 0)),
                pl.BlockSpec((BLK, HD), lambda m, h, *_: (m, h)),
            ],
            out_specs=[
                pl.BlockSpec((BLK, HD), lambda m, h, *_: (m, h)),
                pl.BlockSpec((1, keys, 2 * HD), lambda m, h, *_: (m, 0, 0)),
            ],
            scratch_shapes=[pltpu.VMEM((keys, 2 * HD), jnp.float32)],
        ),
        compiler_params=pltpu.CompilerParams(vmem_limit_bytes=VMEM),
        name="attend_back",
    )(start, ends, q, window, datt)


def geglu_parts(gate):
    c = math.sqrt(2.0 / math.pi)
    square = gate * gate
    t = jnp.tanh(c * gate * (1.0 + 0.044715 * square))
    half = 0.5 * (1.0 + t)
    value = gate * half
    slope = half + 0.5 * gate * (1.0 - t * t) * c * (1.0 + 3 * 0.044715 * square)
    return value, slope


def ffn_kernel(n2_ref, n2t_ref, dy_ref, wg_ref, wu_ref, wd_ref, out_ref, dn2_ref, dwg_ref, dwu_ref, dwd_ref):
    n2, dy = n2_ref[...], dy_ref[...]
    wg, wu, wd = wg_ref[...], wu_ref[...], wd_ref[...]
    f32 = jnp.float32
    gate = jnp.dot(n2, wg, preferred_element_type=f32)
    up = jnp.dot(n2, wu, preferred_element_type=f32)
    value, slope = geglu_parts(gate)
    hidden = (value * up).astype(jnp.bfloat16)
    dh = lax.dot_general(dy, wd, (((1,), (1,)), ((), ())), preferred_element_type=f32)
    dgate = (dh * up * slope).astype(jnp.bfloat16)
    dup = (dh * value).astype(jnp.bfloat16)
    out = jnp.dot(hidden, wd, preferred_element_type=f32)
    dn2 = lax.dot_general(dgate, wg, (((1,), (1,)), ((), ())), preferred_element_type=f32)
    dn2 += lax.dot_general(dup, wu, (((1,), (1,)), ((), ())), preferred_element_type=f32)
    dwd_ref[...] = lax.dot_general(hidden, dy, (((0,), (0,)), ((), ())), preferred_element_type=f32).astype(jnp.bfloat16)
    dwg_ref[...] = jnp.dot(n2t_ref[...], dgate, preferred_element_type=f32).astype(jnp.bfloat16)
    dwu_ref[...] = jnp.dot(n2t_ref[...], dup, preferred_element_type=f32).astype(jnp.bfloat16)

    @pl.when(pl.program_id(0) == 0)
    def _():
        out_ref[...] = out
        dn2_ref[...] = dn2

    @pl.when(pl.program_id(0) > 0)
    def _():
        out_ref[...] += out
        dn2_ref[...] += dn2


def ffn(n2, dy, wg, wu, wd, tile):
    tok, width = n2.shape
    hidden = wg.shape[1]
    whole = pl.BlockSpec((tok, width), lambda i: (0, 0), pipeline_mode=pl.Buffered(1))
    cols = pl.BlockSpec((width, tile), lambda i: (0, i))
    rows = pl.BlockSpec((tile, width), lambda i: (i, 0))
    return pl.pallas_call(
        ffn_kernel,
        grid=(hidden // tile,),
        in_specs=[whole, pl.BlockSpec((width, tok), lambda i: (0, 0), pipeline_mode=pl.Buffered(1)), whole, cols, cols, rows],
        out_specs=[whole, whole, cols, cols, rows],
        out_shape=[jax.ShapeDtypeStruct((tok, width), jnp.float32)] * 2
        + [jax.ShapeDtypeStruct(wg.shape, jnp.bfloat16), jax.ShapeDtypeStruct(wu.shape, jnp.bfloat16), jax.ShapeDtypeStruct(wd.shape, jnp.bfloat16)],
        compiler_params=pltpu.CompilerParams(vmem_limit_bytes=VMEM),
        name="ffn",
    )(n2, n2.T, dy, wg, wu, wd)


class Exchange:
    def __init__(self, p, count, send, recv, local):
        self.count, self.send, self.recv, self.local = count, send, recv, local
        self.me = p.me
        self.Z = p.Z
        self.groups = BLK // 16
        self.wide = 2 * HD * self.groups // count

    def piece(self, d):
        return d % self.groups, pl.ds(pl.multiple_of((d // self.groups) * self.wide, self.wide), self.wide)

    def dev(self, d):
        return (d // self.Z, d % self.Z)

    def copy(self, off, src, dst):
        t = lax.rem(self.me + off, self.count)
        return pltpu.make_async_remote_copy(
            src(t), dst(t), self.send.at[off - 1], self.recv.at[off - 1], device_id=self.dev(t), device_id_type=MESH
        )

    def begin(self, src, dst):
        @pl.loop(1, self.count)
        def _(off):
            self.copy(off, src, dst).start()

        pltpu.make_async_copy(src(self.me), dst(self.me), self.local).start()

    def end(self, src, dst):
        pltpu.make_async_copy(src(self.me), dst(self.me), self.local).wait()

        @pl.loop(1, self.count)
        def _(off):
            self.copy(off, src, dst).wait()


def forward_kernel(grid, units, nseq, sources, kvw, *refs):
    f32, bf16 = jnp.float32, jnp.bfloat16
    n = 6
    start_ref, ends_ref, index_ref, x_ref, dy_ref = refs[:5]
    ins, refs = refs[5 : 5 + n], refs[5 + n :]
    fulls, refs = refs[:n], refs[n:]
    dyx_ref, n2x_ref, refs = *refs[:2], refs[2:]
    n1_ref, q_ref, win_ref, att_ref, mixed_ref, gains_ref, refs = *refs[:6], refs[6:]
    n2, wbuf, small, kv, got, picked, send, recv, local, xsend, xrecv, xlocal, lsem, msend, mrecv = refs
    p = Place(grid)
    count = p.count
    tok, width = x_ref.shape
    batches = tok // BLK
    p.barrier()
    items = [Gather(p, t, ins[t.array], fulls[t.array], send.at[u], recv.at[u], local.at[u]) for u, t in enumerate(units)]
    steps = Steps(staggered(items, [0] + list(range(2, len(items) + 1))))
    advance, through = steps.advance, steps.through

    def load(i, dst, sem):
        return pltpu.make_async_copy(fulls[i], dst, lsem.at[sem])

    def to_mate(k, src, dst):
        return (
            pltpu.make_async_copy(src, dst, lsem.at[3 + k]),
            pltpu.make_async_remote_copy(src, dst, msend.at[k], mrecv.at[k], device_id=p.mate, device_id_type=MESH),
        )

    advance(1)
    shared = [to_mate(0, dy_ref, dyx_ref.at[p.half])]
    start(shared[0])
    x = x_ref[...].astype(f32)
    mixed_ref[...] = x * lax.rsqrt(jnp.mean(x * x, axis=-1, keepdims=True) + EPS)
    through(0)
    load(0, small, 0).start()
    load(0, small, 0).wait()
    gains = small[..., kvw:].reshape(width, 128).astype(f32).T
    gains_ref[...] = gains[:8]
    n1_ref[...] = (mixed_ref[...] * gains[0:1]).astype(bf16)
    ex1 = Exchange(p, count, xsend.at[0], xrecv.at[0], xlocal.at[0])
    ex2 = Exchange(p, count, xsend.at[1], xrecv.at[1], xlocal.at[1])

    kv_value = jnp.dot(n1_ref[...], small[..., :kvw].reshape(width, kvw), preferred_element_type=f32).astype(bf16)
    kv[...] = kv_value.reshape(kv.shape)

    def src1(t):
        g, c = ex1.piece(t)
        return kv.at[:, g, :, c]

    def dst1(t):
        return got.at[ex1.me]

    def src2(t):
        return picked.at[t]

    def dst2(t):
        g, c = ex2.piece(ex2.me)
        return win_ref.at[:, :, g, :, c]

    ex1.begin(src1, dst1)
    advance(6)
    ex1.end(src1, dst1)

    @pl.loop(0, count)
    def _(t):
        for m in range(batches):
            for i in range(sources):
                picked[t, m, i] = got[index_ref[t, m * sources + i], m]

    ex2.begin(src2, dst2)
    through(1)
    load(1, wbuf, 1).start()
    advance(2)
    load(1, wbuf, 1).wait()
    tile = 512
    for j in range(0, width, tile):
        w = wbuf[..., j : j + tile].reshape(width, tile)
        q_ref[:, j : j + tile] = (jnp.dot(n1_ref[...], w, preferred_element_type=f32) * (HD**-0.5)).astype(bf16)
        advance()
    through(2)
    load(2, wbuf, 2).start()
    advance(0)
    ex2.end(src2, dst2)
    load(2, wbuf, 2).wait()
    for m in range(batches):
        rows = pl.ds(m * BLK, BLK)
        for h0 in range(0, H, 2):

            @pl.loop(h0, h0 + 2)
            def _(h):
                cols = pl.ds(pl.multiple_of(h * HD, HD), HD)
                mask = window_mask(start_ref[m], ends_ref, nseq, m, BLK, sources * BLK)
                k = win_ref[m, :, :, :, :HD].reshape(sources * BLK, HD)
                v = win_ref[m, :, :, :, HD:].reshape(sources * BLK, HD)
                prob = softmax_rows(q_ref[rows, cols], k, mask)
                att_ref[rows, cols] = jnp.dot(prob.astype(bf16), v, preferred_element_type=f32).astype(bf16)

            advance()
        for j in range(0, width, tile):
            w = wbuf[..., j : j + tile].reshape(width, tile)
            mixed_ref[rows, j : j + tile] = x_ref[rows, j : j + tile].astype(f32) + jnp.dot(att_ref[rows], w, preferred_element_type=f32)
        mixed = mixed_ref[rows]
        inverse = lax.rsqrt(jnp.mean(mixed * mixed, axis=-1, keepdims=True) + EPS)
        n2[rows] = (mixed * inverse * gains_ref[1:2]).astype(bf16)
        shared.append(to_mate(1 + m, n2.at[rows], n2x_ref.at[p.half, rows]))
        start(shared[-1])
        advance(2)
    steps.finish()
    for copies in shared:
        for c in copies:
            c.wait()


def forward(grid, shards, units, x, dy, start, ends, index, sources, kvw, collective_id):
    a, b, c, z = grid
    count = a * b * c * z
    tok, width = x.shape
    batches = tok // BLK
    bf16 = jnp.bfloat16
    groups = BLK // 16
    wide = 2 * HD * groups // count
    rows = shards[1].shape[0]
    U = len(units)
    any_, vmem, smem = (pl.BlockSpec(memory_space=s) for s in (pl.ANY, pltpu.VMEM, pltpu.SMEM))
    dma = pltpu.SemaphoreType.DMA
    sds = jax.ShapeDtypeStruct
    kinds = {t.array: t.kind for t in units}
    whole = [tuple(grid[:3]) + (z // 2 if kinds[i] == "rows" else z,) + s.shape[-2:] for i, s in enumerate(shards)]
    outs = pl.pallas_call(
        functools.partial(forward_kernel, grid, units, ends.shape[1], sources, kvw),
        out_shape=[sds(w, bf16) for w in whole]
        + [sds((2, tok, width), bf16)] * 2
        + [
            sds((tok, width), bf16),
            sds((tok, width), bf16),
            sds((batches, sources, groups, 16, 2 * HD), bf16),
            sds((tok, width), bf16),
            sds((tok, width), jnp.float32),
            sds((8, width), jnp.float32),
        ],
        in_specs=[smem, smem, smem, vmem, any_] + [any_] * 6,
        out_specs=[any_] * 8 + [vmem] * 6,
        scratch_shapes=[
            pltpu.VMEM((tok, width), bf16),
            pltpu.VMEM(tuple(grid) + (rows, width), bf16),
            pltpu.VMEM(tuple(grid) + (rows, shards[0].shape[1]), bf16),
            pltpu.VMEM((batches, groups, 16, 2 * HD), bf16),
            pltpu.VMEM((count, batches, 16, wide), bf16),
            pltpu.VMEM((count, batches, sources, 16, wide), bf16),
            dma((U, 12)),
            dma((U, 12)),
            dma((U,)),
            dma((2, count - 1)),
            dma((2, count - 1)),
            dma((2,)),
            dma((4 + batches,)),
            dma((1 + batches,)),
            dma((1 + batches,)),
        ],
        compiler_params=pltpu.CompilerParams(collective_id=collective_id, has_side_effects=True, vmem_limit_bytes=VMEM),
        name="forward",
    )(start, ends, index, x, dy, *shards)
    fulls = [o.reshape(-1, s.shape[-1]) for o, s in zip(outs, shards)]
    dy_pair, n2_pair, n1, q, window, att, mixed, gains = outs[6:]
    return fulls, dy_pair, n2_pair, n1, q, window.reshape(batches, sources * BLK, 2 * HD), att, mixed, gains

def place_of(perm):
    return jnp.argsort(perm, axis=1).astype(jnp.int32)


def windows_of(kv, perm, sources):
    axes = ("dp", "fsdp")
    batches, rows, cols = kv.shape
    count = perm.shape[1]
    part = rows // count
    pieces = kv.reshape(batches, count, part, cols).transpose(1, 0, 2, 3)
    spread = lax.all_to_all(pieces, axes, split_axis=0, concat_axis=0, tiled=True)
    holder = place_of(perm)
    block = perm[:, :, None] - (sources - 1) + jnp.arange(sources, dtype=jnp.int32)
    source = jnp.take_along_axis(holder[:, None, :], jnp.maximum(block, 0), axis=2)
    index = (source * batches + jnp.arange(batches, dtype=jnp.int32)[:, None, None]).transpose(1, 0, 2).reshape(-1)
    picked = jnp.take(spread.reshape(count * batches, part, cols), index, axis=0).reshape(count, batches * sources, part, cols)
    arrived = lax.all_to_all(picked, axes, split_axis=0, concat_axis=0, tiled=True)
    return arrived.transpose(1, 0, 2, 3).reshape(batches, sources * rows, cols)


def window_sums(grads, perm, sources):
    axes = ("dp", "fsdp")
    batches, wide, cols = grads.shape
    rows = wide // sources
    count = perm.shape[1]
    part = rows // count
    pieces = grads.reshape(batches * sources, count, part, cols).transpose(1, 0, 2, 3)
    spread = lax.all_to_all(pieces, axes, split_axis=0, concat_axis=0, tiled=True)
    holder = place_of(perm)
    block = perm[:, :, None] + (sources - 1) - jnp.arange(sources, dtype=jnp.int32)
    reader = jnp.take_along_axis(holder[:, None, :], jnp.minimum(block, count - 1), axis=2)
    slot = jnp.arange(batches, dtype=jnp.int32)[:, None, None] * sources + jnp.arange(sources, dtype=jnp.int32)
    index = (reader * (batches * sources) + slot).transpose(1, 0, 2)
    picked = jnp.take(spread.reshape(count * batches * sources, part, cols), index.reshape(-1), axis=0)
    picked = picked.reshape(count, batches, sources, part, cols).astype(jnp.float32)
    valid = (block < count).transpose(1, 0, 2)[..., None, None]
    summed = jnp.sum(jnp.where(valid, picked, 0.0), axis=2).astype(jnp.bfloat16)
    arrived = lax.all_to_all(summed, axes, split_axis=0, concat_axis=0, tiled=True)
    return arrived.transpose(1, 0, 2, 3).reshape(batches, rows, cols)


def fast_body(grid, tokens, w_query, w_keyval, w_out, w_gate, w_up, w_down, gain_attn, gain_ffn, cotangent, block_perm, extra_len):
    f32, bf16 = jnp.float32, jnp.bfloat16
    batches, _, rows, width = tokens.shape
    tok = batches * rows
    me = lax.axis_index(("dp", "fsdp"))
    sources = WIN // BLK + 1
    scale = HD ** (-0.5)
    kvw = w_keyval.shape[1]
    gains = jnp.stack([gain_attn, gain_ffn], axis=1)
    small = jnp.concatenate([w_keyval, jnp.pad(gains, ((0, 0), (0, 126)))], axis=1)
    sub = w_down.shape[0]
    half = w_gate.shape[1] // 2
    shards = [small, w_query, w_out, by_parity(w_gate, sub), by_parity(w_up, sub), w_down]
    units = [Unit(i, "all", (0, s.shape[0]), (0, s.shape[1])) for i, s in enumerate(shards[:3])]
    for k in (0, 1):
        units += [Unit(i, "cols", (0, w_gate.shape[0]), (k * half // 2, half // 2)) for i in (3, 4)]
        units += [Unit(5, "rows", (0, sub), (k * width // 2, width // 2))]
    holder = place_of(block_perm)
    block = block_perm[:, :, None] - (sources - 1) + jnp.arange(sources, dtype=jnp.int32)
    index = jnp.take_along_axis(holder[:, None, :], jnp.maximum(block, 0), axis=2)
    index = index.transpose(1, 0, 2).reshape(-1, batches * sources)
    start = lax.dynamic_slice_in_dim(block_perm, me, 1, axis=1)[:, 0] * BLK
    ends = jnp.cumsum(extra_len + (WIN - 1), axis=1).astype(jnp.int32)
    x = tokens.reshape(tok, width)
    dy = cotangent.reshape(tok, width)
    fulls, dy_pair, n2_pair, n1b, query, window, att, mixed, gains = forward(grid, shards, units, x, dy, start, ends, index, sources, kvw, 0)
    small, wq, wo, wg, wu, wd = fulls
    wkv = small[:, :kvw]
    g1, g2 = gains[0], gains[1]
    x = x.astype(f32)
    r1 = lax.rsqrt(jnp.mean(x * x, axis=-1, keepdims=True) + EPS)
    r2 = lax.rsqrt(jnp.mean(mixed * mixed, axis=-1, keepdims=True) + EPS)
    out, d_n2, d_wgate, d_wup, d_down = ffn(n2_pair.reshape(2 * tok, width), dy_pair.reshape(2 * tok, width), wg, wu, wd, 256)
    d_n2 = from_mate(d_n2.reshape(2, tok, width))
    out = from_mate(out.reshape(2, tok, width))
    block_out = (mixed + out).astype(bf16)
    d_mixed_norm, d_g2 = norm_back(mixed, r2, g2, d_n2)
    d_mixed = dy.astype(f32) + d_mixed_norm
    d_branch = d_mixed.astype(bf16)
    d_wout = jnp.einsum("ta,td->ad", att, d_branch, preferred_element_type=f32).astype(bf16)
    d_att = jnp.einsum("td,ad->ta", d_branch, wo, preferred_element_type=f32).astype(bf16)
    d_query, d_window = attend_back(query, window, d_att, start, ends)
    d_keyval = window_sums(d_window, block_perm, sources).reshape(tok, kvw)
    d_wquery = (jnp.einsum("td,ta->da", n1b, d_query, preferred_element_type=f32) * scale).astype(bf16)
    d_wkeyval = jnp.einsum("td,tc->dc", n1b, d_keyval, preferred_element_type=f32)
    d_n1 = jnp.einsum("ta,da->td", d_query, wq, preferred_element_type=f32) * scale
    d_n1 = d_n1 + jnp.einsum("tc,dc->td", d_keyval, wkv, preferred_element_type=f32)
    d_x_norm, d_g1 = norm_back(x, r1, g1, d_n1)
    grad_tokens = (d_mixed + d_x_norm).astype(bf16)
    d_gains = jnp.pad(jnp.stack([d_g1, d_g2], axis=1), ((0, 0), (0, 126)))
    d_small = jnp.concatenate([d_wkeyval, d_gains], axis=1).astype(bf16)
    grads = [d_small, d_wquery, d_wout, d_wgate, d_wup, d_down]
    kinds = ["all"] * 3 + ["cols"] * 2 + ["rows"]
    grads = [
        g.reshape(tuple(grid[:3]) + (grid[3] // 2 if k == "rows" else grid[3], -1, g.shape[1]))
        for g, k in zip(grads, kinds)
    ]
    order = units[3:] + units[2:3] + units[1:2] + units[:1]
    small, dq, do, dg, du, dd = scatter(grid, grads, [s.shape for s in shards], order, 1)
    dg, du = from_parity(dg, sub), from_parity(du, sub)
    return (
        block_out.reshape(tokens.shape),
        grad_tokens.reshape(tokens.shape),
        dq,
        small[:, :kvw],
        do,
        dg,
        du,
        dd,
        small[:, kvw],
        small[:, kvw + 1],
    )


def by_parity(w, sub):
    rows, hidden = w.shape
    return w.reshape(rows, -1, 2, sub).transpose(2, 0, 1, 3).reshape(2, rows, hidden // 2)


def from_parity(w, sub):
    _, rows, part = w.shape
    return w.reshape(2, rows, -1, sub).transpose(1, 2, 0, 3).reshape(rows, 2 * part)


def from_mate(parts):
    z = lax.axis_index("fsdp")
    count = lax.axis_size("fsdp")
    theirs = lax.dynamic_index_in_dim(parts, 1 - z % 2, 0, keepdims=False)
    got = lax.ppermute(theirs.astype(jnp.bfloat16), "fsdp", [(i, i ^ 1) for i in range(count)])
    return lax.dynamic_index_in_dim(parts, z % 2, 0, keepdims=False) + got.astype(jnp.float32)


def solution(mesh):
    count = mesh.shape["dp"] * mesh.shape["fsdp"]
    grid = (2, 2, 2, mesh.shape["fsdp"])
    whole_tiles = mesh.shape["dp"] == 8 and 1536 % (16 * count) == 0
    run = functools.partial(fast_body, grid) if whole_tiles else body
    placed = (
        P(None, ("dp", "fsdp"), None, None),
        P(("dp", "fsdp"), None),
        P(("dp", "fsdp"), None),
        P(("dp", "fsdp"), None),
        P(("dp", "fsdp"), None),
        P(("dp", "fsdp"), None),
        P(("dp", "fsdp"), None),
        P(("dp", "fsdp")),
        P(("dp", "fsdp")),
        P(None, ("dp", "fsdp"), None, None),
        P(),
        P(),
    )
    return jax.shard_map(
        run,
        mesh=mesh,
        in_specs=placed,
        out_specs=(
            P(None, ("dp", "fsdp"), None, None),
            P(None, ("dp", "fsdp"), None, None),
            P(("dp", "fsdp"), None),
            P(("dp", "fsdp"), None),
            P(("dp", "fsdp"), None),
            P(("dp", "fsdp"), None),
            P(("dp", "fsdp"), None),
            P(("dp", "fsdp"), None),
            P(("dp", "fsdp")),
            P(("dp", "fsdp")),
        ),
        check_vma=False,
    )
```

```python
import functools
import math
import types

import jax
import jax.numpy as jnp
from jax import lax
from jax.experimental import pallas as pl
from jax.experimental.pallas import tpu as pltpu
from jax.sharding import PartitionSpec as P

H = 6
HD = 256
WIN = 1024
BLK = 256


EPS = 1e-06
VMEM = 62 * 1024 * 1024


def for_sending(x):
    return jax.tree.map(lambda a: a.astype(jnp.bfloat16) if a.dtype == jnp.float32 else a, x)


def shifted(value, axis, steps):
    count = lax.axis_size(axis)
    leading, last = (max(0, -steps), min(count, count - steps))
    return lax.ppermute(value, axis, [(source, source + steps) for source in range(leading, last)])


def norm_rows(value, gain):
    inverse = lax.rsqrt(jnp.mean(value * value, axis=-1, keepdims=True) + EPS)
    return (value * inverse * gain, inverse)


def norm_back(value, inverse, gain, grad):
    scaled = grad * gain
    width = value.shape[-1]
    dvalue = (
        inverse * scaled
        - value * inverse**3 * jnp.sum(scaled * value, axis=-1, keepdims=True) / width
    )
    dgain = jnp.sum(grad * value * inverse, axis=0)
    return (dvalue, dgain)


def sequence_of(positions, ends):
    return jnp.sum((positions[:, None] >= ends[None, :]).astype(jnp.int32), axis=1)


def visible_mask(query_pos, key_pos, ends):
    same = sequence_of(query_pos, ends)[:, None] == sequence_of(key_pos, ends)[None, :]
    gap = query_pos[:, None] - key_pos[None, :]
    return same & (gap >= 0) & (gap < WIN) & (key_pos[None, :] >= 0)


def geglu(gate, up):
    return jax.nn.gelu(gate, approximate=True) * up


def move_keys(value, order, count):
    rows = value.shape[0]
    spread = lax.all_to_all(value, ("dp", "fsdp"), split_axis=1, concat_axis=0, tiled=True)
    pieces = spread.reshape(count, rows, spread.shape[1])
    placed = jnp.take(pieces, order, axis=0).reshape(count * rows, spread.shape[1])
    return lax.all_to_all(placed, ("dp", "fsdp"), split_axis=0, concat_axis=1, tiled=True)


def move_grads(value, order, count):
    rows = value.shape[0]
    spread = lax.all_to_all(
        for_sending(value), ("dp", "fsdp"), split_axis=1, concat_axis=0, tiled=True
    ).astype(value.dtype)
    pieces = spread.reshape(count, rows, spread.shape[1])
    placed = jnp.take(pieces, order, axis=0).reshape(count * rows, spread.shape[1])
    return lax.all_to_all(
        for_sending(placed), ("dp", "fsdp"), split_axis=0, concat_axis=1, tiled=True
    ).astype(placed.dtype)


def body(
    tokens,
    w_query,
    w_keyval,
    w_out,
    w_gate,
    w_up,
    w_down,
    gain_attn,
    gain_ffn,
    cotangent,
    block_perm,
    extra_len,
):
    count = lax.axis_size(("dp", "fsdp"))
    me = lax.axis_index(("dp", "fsdp"))
    batches = tokens.shape[0]
    sources = WIN // BLK + 1
    scale = HD ** (-0.5)
    shards = (w_query, w_keyval, w_out, w_gate, w_up, w_down, gain_attn, gain_ffn)
    device_ids = jnp.arange(count, dtype=jnp.int32)
    totals = None
    outputs = []
    input_grads = []
    for batch in range(batches):
        full = (
            lax.all_gather(shards[0], ("dp", "fsdp"), axis=0, tiled=True),
            lax.all_gather(shards[1], ("dp", "fsdp"), axis=0, tiled=True),
            lax.all_gather(shards[2], ("dp", "fsdp"), axis=0, tiled=True),
            lax.all_gather(shards[3], ("dp", "fsdp"), axis=0, tiled=True),
            lax.all_gather(shards[4], ("dp", "fsdp"), axis=0, tiled=True),
            lax.all_gather(shards[5], ("dp", "fsdp"), axis=0, tiled=True),
            lax.all_gather(shards[6], ("dp", "fsdp"), axis=0, tiled=True),
            lax.all_gather(shards[7], ("dp", "fsdp"), axis=0, tiled=True),
        )
        wq, wkv, wo, wg, wu, wd, g1b, g2b = full
        g1 = g1b.astype(jnp.float32)
        g2 = g2b.astype(jnp.float32)
        perm_row = block_perm[batch]
        ends = jnp.cumsum(extra_len[batch] + (WIN - 1))
        mine = lax.dynamic_slice_in_dim(perm_row, me, 1)[0]
        holder = jnp.sum(
            jnp.where(perm_row[None, :] == device_ids[:, None], device_ids[None, :], 0), axis=1
        )
        query_pos = mine * BLK + jnp.arange(BLK, dtype=jnp.int32)
        key_pos = (mine - (sources - 1)) * BLK + jnp.arange(sources * BLK, dtype=jnp.int32)
        mask = jnp.repeat(visible_mask(query_pos, key_pos, ends), H, axis=0)
        x = tokens[batch, 0].astype(jnp.float32)
        n1, r1 = norm_rows(x, g1)
        n1b = n1.astype(jnp.bfloat16)
        query = (jnp.dot(n1b, wq, preferred_element_type=jnp.float32) * scale).astype(jnp.bfloat16)
        query_rows = query.reshape(BLK * H, HD)
        keyval = jnp.dot(n1b, wkv, preferred_element_type=jnp.float32).astype(jnp.bfloat16)
        ordered = move_keys(keyval, holder, count)
        window = [ordered] * sources
        for back in range(1, sources):
            window[sources - 1 - back] = shifted(ordered, ("dp", "fsdp"), back)
        picked = move_keys(jnp.concatenate(window, axis=0), perm_row, count)
        keys_src = picked[:, :HD]
        values_src = picked[:, HD:]
        scores = jnp.einsum("qd,kd->qk", query_rows, keys_src, preferred_element_type=jnp.float32)
        masked = jnp.where(mask, scores, -1e30)
        top = jnp.max(masked, axis=1, keepdims=True)
        expd = jnp.exp(masked - top)
        rowsum = jnp.sum(expd, axis=1, keepdims=True)
        lse = top + jnp.log(rowsum)
        probs_low = (expd / rowsum).astype(jnp.bfloat16)
        att = jnp.dot(probs_low, values_src, preferred_element_type=jnp.float32)
        att_low = att.reshape(BLK, H * HD).astype(jnp.bfloat16)
        mixed = x + jnp.dot(att_low, wo, preferred_element_type=jnp.float32)
        n2, r2 = norm_rows(mixed, g2)
        n2b = n2.astype(jnp.bfloat16)
        gate = jnp.dot(n2b, wg, preferred_element_type=jnp.float32)
        up = jnp.dot(n2b, wu, preferred_element_type=jnp.float32)
        hidden = geglu(gate, up).astype(jnp.bfloat16)
        outputs.append(
            (mixed + jnp.dot(hidden, wd, preferred_element_type=jnp.float32)).astype(jnp.bfloat16)
        )
        wq, wkv, wo, wg, wu, wd, g1b, g2b = (
            lax.all_gather(shards[0], ("dp", "fsdp"), axis=0, tiled=True),
            lax.all_gather(shards[1], ("dp", "fsdp"), axis=0, tiled=True),
            lax.all_gather(shards[2], ("dp", "fsdp"), axis=0, tiled=True),
            lax.all_gather(shards[3], ("dp", "fsdp"), axis=0, tiled=True),
            lax.all_gather(shards[4], ("dp", "fsdp"), axis=0, tiled=True),
            lax.all_gather(shards[5], ("dp", "fsdp"), axis=0, tiled=True),
            lax.all_gather(shards[6], ("dp", "fsdp"), axis=0, tiled=True),
            lax.all_gather(shards[7], ("dp", "fsdp"), axis=0, tiled=True),
        )
        dy = cotangent[batch, 0]
        d_down = jnp.einsum("tf,td->fd", hidden, dy, preferred_element_type=jnp.float32)
        d_hidden = jnp.einsum("td,fd->tf", dy, wd, preferred_element_type=jnp.float32)
        _, geglu_pull = jax.vjp(geglu, gate, up)
        d_gate, d_up = geglu_pull(d_hidden)
        d_gate_low = d_gate.astype(jnp.bfloat16)
        d_up_low = d_up.astype(jnp.bfloat16)
        d_wgate = jnp.einsum("td,tf->df", n2b, d_gate_low, preferred_element_type=jnp.float32)
        d_wup = jnp.einsum("td,tf->df", n2b, d_up_low, preferred_element_type=jnp.float32)
        d_n2 = jnp.einsum("tf,df->td", d_gate_low, wg, preferred_element_type=jnp.float32)
        d_n2 = d_n2 + jnp.einsum("tf,df->td", d_up_low, wu, preferred_element_type=jnp.float32)
        d_mixed_norm, d_g2 = norm_back(mixed, r2, g2, d_n2)
        d_mixed = dy.astype(jnp.float32) + d_mixed_norm
        d_branch = d_mixed.astype(jnp.bfloat16)
        d_wout = jnp.einsum("ta,td->ad", att_low, d_branch, preferred_element_type=jnp.float32)
        d_att = jnp.einsum("td,ad->ta", d_branch, wo, preferred_element_type=jnp.float32)
        d_att_rows = d_att.astype(jnp.bfloat16).reshape(BLK * H, HD)
        again = jnp.einsum("qd,kd->qk", query_rows, keys_src, preferred_element_type=jnp.float32)
        probs = jnp.exp(jnp.where(mask, again, -1e30) - lse)
        d_probs = jnp.einsum(
            "qd,kd->qk", d_att_rows, values_src, preferred_element_type=jnp.float32
        )
        delta = jnp.sum(probs * d_probs, axis=1, keepdims=True)
        d_scores = (probs * (d_probs - delta)).astype(jnp.bfloat16)
        d_query = jnp.dot(d_scores, keys_src, preferred_element_type=jnp.float32).astype(
            jnp.bfloat16
        )
        d_query = d_query.reshape(BLK, H * HD)
        d_keys = jnp.einsum("qk,qd->kd", d_scores, query_rows, preferred_element_type=jnp.float32)
        d_values = jnp.einsum(
            "qk,qd->kd", probs.astype(jnp.bfloat16), d_att_rows, preferred_element_type=jnp.float32
        )
        d_keyval_flat = jnp.concatenate([d_keys, d_values], axis=1)
        ordered_grads = move_grads(d_keyval_flat, holder, count).reshape(sources, BLK, 2 * HD)
        summed = ordered_grads[sources - 1]
        for back in range(1, sources):
            summed = summed + shifted(
                ordered_grads[sources - 1 - back].astype(jnp.bfloat16), ("dp", "fsdp"), -back
            ).astype(jnp.float32)
        d_keyval = move_grads(summed, perm_row, count).astype(jnp.bfloat16)
        d_wquery = jnp.einsum("td,ta->da", n1b, d_query, preferred_element_type=jnp.float32) * scale
        d_wkeyval = jnp.einsum("td,tc->dc", n1b, d_keyval, preferred_element_type=jnp.float32)
        d_n1 = jnp.einsum("ta,da->td", d_query, wq, preferred_element_type=jnp.float32) * scale
        d_n1 = d_n1 + jnp.einsum("tc,dc->td", d_keyval, wkv, preferred_element_type=jnp.float32)
        d_x_norm, d_g1 = norm_back(x, r1, g1, d_n1)
        input_grads.append((d_mixed + d_x_norm).astype(jnp.bfloat16))
        local = (d_wquery, d_wkeyval, d_wout, d_wgate, d_wup, d_down, d_g1, d_g2)
        totals = local if totals is None else tuple((a + b for a, b in zip(totals, local)))
    totals = lax.psum_scatter(totals, ("dp", "fsdp"), scatter_dimension=0, tiled=True)
    block_out = jnp.stack(outputs)[:, None]
    grad_tokens = jnp.stack(input_grads)[:, None]
    return (
        block_out,
        grad_tokens,
        totals[0],
        totals[1],
        totals[2],
        totals[3],
        totals[4],
        totals[5],
        totals[6],
        totals[7],
    )


MESH = pl.DeviceIdType.MESH
BF16, F32 = jnp.bfloat16, jnp.float32
ALL, COLS, ROWS = 0, 1, 2
ARRAYS = ("small", "wq", "wo", "wg", "wu", "wd")


class Place:
    def __init__(self, grid):
        self.grid = grid
        self.Z = grid[3]
        self.count = grid[0] * grid[1] * grid[2] * grid[3]
        dp = lax.axis_index("dp")
        self.z = lax.axis_index("fsdp")
        self.c = dp % 2
        self.x = (dp // 2) % 2
        self.y = dp // 4
        self.me = dp * self.Z + self.z
        self.half = self.z % 2
        self.pair = self.z // 2
        self.core = self.dev(c=1 - self.c)
        self.xdev = self.dev(x=1 - self.x)
        self.ydev = self.dev(y=1 - self.y)
        self.mate = self.dev(z=self.z + 1 - 2 * self.half)
        self.far = self.dev(z=(self.z + 2) % self.Z)

    def dev(self, y=None, x=None, c=None, z=None):
        y = self.y if y is None else y
        x = self.x if x is None else x
        c = self.c if c is None else c
        z = self.z if z is None else z
        return ((y * 2 + x) * 2 + c, z)

    def barrier(self):
        sem = pltpu.get_barrier_semaphore()

        @pl.loop(1, self.count)
        def _(off):
            t = lax.rem(self.me + off, self.count)
            pl.semaphore_signal(sem, inc=1, device_id=(t // self.Z, t % self.Z), device_id_type=MESH)

        pl.semaphore_wait(sem, self.count - 1)


def start(copies):
    for c in copies:
        c.start()


def wait_recv(copies):
    for c in copies:
        c.wait_recv()


def wait_send(copies):
    for c in copies:
        c.wait_send()


def halves(width):
    first = width - (width // 256) * 128
    return [(0, first), (first, width - first)]


class Unit:
    def __init__(self, array, kind, rows, cols):
        self.array, self.kind, self.rows, self.cols = array, kind, rows, cols
        self.width = cols[1]

    def shape(self, grid):
        return grid[:2] + (grid[3] // 2 if self.kind == ROWS else grid[3],) + (self.rows[1], self.width)

    def link_buffers(self, grid):
        a, b, z, r, w = self.shape(grid)
        h = halves(w)
        out = [(a, b, z, r, w), (b, z, r, h[0][1]), (a, z, r, h[1][1]), (z, r, h[0][1]), (z, r, h[1][1])]
        if self.kind == ALL:
            return out + [(z - 1, r, w)]
        if self.kind == COLS:
            return out + [(z // 2, r, w), (r, w)]
        return out + [(r, w)]


class Gather:
    def __init__(self, p, unit, src, dst, send, recv, local):
        self.p, self.dst, self.send, self.recv, self.local, self.kind = p, dst, send, recv, local, unit.kind
        self.r, self.all = pl.ds(*unit.rows), pl.ds(*unit.cols)
        self.h = [pl.ds(unit.cols[0] + a, b) for a, b in halves(unit.width)]
        self.src = (lambda half: src.at[half, self.r, self.all]) if unit.kind == COLS else (lambda half: src.at[self.r, self.all])
        self.spot = p.pair if unit.kind == ROWS else p.z

    def copy(self, k, src, dst, dev):
        return pltpu.make_async_remote_copy(src, dst, self.send.at[k], self.recv.at[k], device_id=dev, device_id_type=MESH)

    def same(self, k, ref, dev):
        return self.copy(k, ref, ref, dev)

    def block(self, y, x, cols):
        return self.dst.at[y, x, self.p.c, :, self.r, cols]

    def own(self):
        p = self.p
        return pltpu.make_async_copy(self.src(p.half), self.dst.at[p.y, p.x, p.c, self.spot, self.r, self.all], self.local)

    def z1(self):
        p = self.p
        there = self.dst.at[p.y, p.x, p.c, self.spot, self.r, self.all]
        if self.kind == ALL:
            return [self.copy(i - 1, self.src(0), there, p.dev(z=(p.z + i) % p.Z)) for i in range(1, p.Z)]
        if self.kind == COLS:
            return [self.copy(0, self.src(1 - p.half), there, p.mate)]
        return [self.copy(0, self.src(0), there, p.far)]

    def z2(self):
        p = self.p
        return [self.same(1, self.dst.at[p.y, p.x, p.c, pl.ds(2 * p.pair, 2), self.r, self.all], p.far)]

    def p1(self):
        p = self.p
        return [self.same(3, self.block(p.y, p.x, self.h[0]), p.xdev), self.same(4, self.block(p.y, p.x, self.h[1]), p.ydev)]

    def p2(self):
        p, every = self.p, slice(None)
        return [self.same(5, self.block(p.y, every, self.h[0]), p.ydev), self.same(6, self.block(every, p.x, self.h[1]), p.xdev)]

    def c0(self):
        p = self.p
        return [self.same(7, self.block(p.y, p.x, self.all), p.core)]

    def c1(self):
        p = self.p
        return [self.same(8, self.block(p.y, 1 - p.x, self.h[0]), p.core), self.same(9, self.block(1 - p.y, p.x, self.h[1]), p.core)]

    def c2(self):
        p, every = self.p, slice(None)
        return [self.same(10, self.block(1 - p.y, every, self.h[0]), p.core), self.same(11, self.block(every, 1 - p.x, self.h[1]), p.core)]

    def stages(self):
        def first():
            self.own().start()
            start(self.z1())

        def second():
            self.own().wait()
            wait_recv(self.z1())
            start(self.z2())

        def third():
            if self.kind == COLS:
                wait_recv(self.z2())
            else:
                self.own().wait()
                wait_recv(self.z1())
            start(self.p1() + self.c0())

        def fourth():
            wait_recv(self.p1())
            start(self.p2() + self.c1())

        def fifth():
            wait_recv(self.p2())
            start(self.c2())

        def last():
            wait_recv(self.c0() + self.c1() + self.c2())
            wait_send(self.z1() + (self.z2() if self.kind == COLS else []) + self.p1() + self.p2() + self.c0() + self.c1() + self.c2())

        return [first] + ([second] if self.kind == COLS else []) + [third, fourth, fifth, last]


class Scatter:
    def __init__(self, p, unit, src, out, landing, rest, sems):
        self.p, self.unit, self.kind = p, unit, unit.kind
        self.src, self.out, self.landing, self.rest = src, out, landing, rest
        self.send, self.recv, self.local = sems
        self.r, self.cols = pl.ds(*unit.rows), pl.ds(*unit.cols)
        self.h = [pl.ds(a, b) for a, b in halves(unit.width)]
        self.all = pl.ds(0, unit.width)
        self.n = unit.shape(p.grid)[2]
        self.stage = 0

    def copy(self, k, src, dst, dev):
        return pltpu.make_async_remote_copy(src, dst, self.send.at[k], self.recv.at[k], device_id=dev, device_id_type=MESH)

    def r0(self):
        p = self.p
        return [self.copy(0, self.src.at[:, :, 1 - p.c, :, self.r, self.cols], self.landing, p.core)]

    def loads(self):
        own = self.src.at[:, :, self.p.c, :, self.r, self.cols]
        return [
            pltpu.make_async_copy(self.landing, self.P.at[..., self.all], self.local.at[0]),
            pltpu.make_async_copy(own, self.T.at[..., self.all], self.local.at[1]),
        ]

    def r1(self):
        p, P = self.p, self.P
        return [self.copy(1, P.at[1 - p.y, :, :, :, self.h[0]], self.rest[0], p.ydev), self.copy(2, P.at[:, 1 - p.x, :, :, self.h[1]], self.rest[1], p.xdev)]

    def r2(self):
        p, P = self.p, self.P
        return [self.copy(3, P.at[p.y, 1 - p.x, :, :, self.h[0]], self.rest[2], p.xdev), self.copy(4, P.at[1 - p.y, p.x, :, :, self.h[1]], self.rest[3], p.ydev)]

    def r3(self):
        p, P = self.p, self.P
        if self.kind == ALL:
            return [self.copy(4 + i, P.at[p.y, p.x, (p.z + i) % p.Z, :, self.all], self.rest[4].at[i - 1], p.dev(z=(p.z + i) % p.Z)) for i in range(1, p.Z)]
        if self.kind == COLS:
            return [self.copy(5, P.at[p.y, p.x, pl.ds(2 * (1 - p.pair), 2), :, self.all], self.rest[4], p.far)]
        return [self.copy(5, P.at[p.y, p.x, 1 - p.pair, :, self.all], self.rest[4], p.far)]

    def r4(self):
        p = self.p
        return [self.copy(6, self.P.at[p.y, p.x, 2 * p.pair + 1 - p.half, :, self.all], self.rest[5], p.mate)]

    def add0(self):
        P, T, b, n = self.P, self.T, self.P.shape[1], self.n

        @pl.loop(0, P.shape[0] * b * n)
        def _(i):
            at = (i // (b * n), (i // n) % b, i % n, slice(None), self.all)
            P[at] = P[at] + T[at]

    def add1(self):
        p, P, n = self.p, self.P, self.n

        @pl.loop(0, 2 * n)
        def _(i):
            b, d = i // n, i % n
            P[p.y, b, d, :, self.h[0]] = P[p.y, b, d, :, self.h[0]] + self.rest[0][b, d]
            P[b, p.x, d, :, self.h[1]] = P[b, p.x, d, :, self.h[1]] + self.rest[1][b, d]

    def add2(self):
        p, P = self.p, self.P

        @pl.loop(0, self.n)
        def _(d):
            for k in (0, 1):
                P[p.y, p.x, d, :, self.h[k]] = P[p.y, p.x, d, :, self.h[k]] + self.rest[2 + k][d]

    def add3(self):
        p, got = self.p, self.rest[4]
        mine = lambda d: self.P[p.y, p.x, d, :, self.all].astype(F32)
        if self.kind == ALL:
            s = mine(p.z)
            for i in range(p.Z - 1):
                s = s + got[i].astype(F32)
            self.out[self.r, self.cols] = s
        elif self.kind == ROWS:
            self.out[self.r, self.cols] = mine(p.pair) + got[...].astype(F32)
        else:
            theirs = 2 * p.pair + 1 - p.half
            self.out[p.half, self.r, self.cols] = mine(p.z) + got[p.half].astype(F32)
            self.P[p.y, p.x, theirs, :, self.all] = (mine(theirs) + got[1 - p.half].astype(F32)).astype(BF16)

    def first(self):
        start(self.r0())

    @property
    def P(self):
        return self.pool.at[self.slot]

    def admit(self, pool, slot, T):
        self.pool, self.slot, self.T = pool, slot, T
        wait_recv(self.r0())
        start(self.loads())

    def settle(self):
        for c in self.loads():
            c.wait()
        self.add0()
        start(self.r1())

    def next(self):
        k, self.stage = self.stage, self.stage + 1
        if k == 0:
            wait_recv(self.r1())
            wait_send(self.r1())
            self.add1()
            start(self.r2())
        elif k == 1:
            wait_recv(self.r2())
            wait_send(self.r2())
            self.add2()
            start(self.r3())
        elif k == 2:
            wait_recv(self.r3())
            wait_send(self.r3() + self.r0())
            self.add3()
            if self.kind == COLS:
                start(self.r4())
        else:
            wait_recv(self.r4())
            wait_send(self.r4())
            self.out[1 - self.p.half, self.r, self.cols] = self.rest[5][...].astype(F32)
        return self.stage < (4 if self.kind == COLS else 3)


class Sums:
    def __init__(self, pools):
        self.pools, self.used = pools, {k: 0 for k in pools}
        self.queue, self.under_way = [], []

    def add(self, item):
        item.first()
        self.queue.append(item)

    def tick(self, count=1):
        for _ in range(count):
            new = self.queue.pop(0) if self.queue else None
            if new is not None:
                key = ROWS if new.kind == ROWS else ALL
                P, T = self.pools[key]
                new.admit(P, self.used[key] % P.shape[0], T)
                self.used[key] += 1
            self.under_way = [i for i in self.under_way if i.next()]
            if new is not None:
                new.settle()
                self.under_way.append(new)

    def finish(self):
        while self.queue or self.under_way:
            self.tick()


def staggered(items, starts=None):
    lists = [i.stages() for i in items]
    starts = starts or list(range(len(items)))
    steps = []
    for s in range(max(b + len(l) for b, l in zip(starts, lists))):
        for u in reversed(range(len(lists))):
            k = s - starts[u]
            if 0 <= k < len(lists[u]):
                steps.append((u, k == len(lists[u]) - 1, lists[u][k]))
    return steps


class Steps:
    def __init__(self, steps):
        self.steps, self.at = steps, 0

    def advance(self, count=1):
        for _ in range(count):
            if self.at < len(self.steps):
                self.steps[self.at][2]()
                self.at += 1

    def through(self, item):
        mark = [k for k, (u, done, _) in enumerate(self.steps) if u == item and done][0]
        self.advance(mark + 1 - self.at)

    def finish(self):
        self.advance(len(self.steps) - self.at)

def window_mask(start, ends, nseq, m, queries, keys):
    qpos = start + lax.broadcasted_iota(jnp.int32, (queries, 1), 0)
    first = jnp.maximum(qpos - (WIN - 1), 0)
    for k in range(nseq):
        end = ends[m, k]
        first = jnp.maximum(first, jnp.where(qpos >= end, end, 0))
    kpos = start - (keys - queries) + lax.broadcasted_iota(jnp.int32, (1, keys), 1)
    return (kpos >= first) & (kpos <= qpos)


def softmax_rows(q, k, mask):
    scores = lax.dot_general(q, k, (((1,), (1,)), ((), ())), preferred_element_type=jnp.float32)
    masked = jnp.where(mask, scores, -1e30)
    expd = jnp.exp(masked - jnp.max(masked, axis=1, keepdims=True))
    return expd * (1.0 / jnp.sum(expd, axis=1, keepdims=True))


def geglu_parts(gate):
    c = math.sqrt(2.0 / math.pi)
    square = gate * gate
    t = jnp.tanh(c * gate * (1.0 + 0.044715 * square))
    half = 0.5 * (1.0 + t)
    value = gate * half
    slope = half + 0.5 * gate * (1.0 - t * t) * c * (1.0 + 3 * 0.044715 * square)
    return value, slope


class Exchange:
    def __init__(self, p, count, send, recv, local):
        self.count, self.send, self.recv, self.local = count, send, recv, local
        self.me = p.me
        self.Z = p.Z
        self.groups = BLK // 16
        self.wide = 2 * HD * self.groups // count

    def piece(self, d):
        return d % self.groups, pl.ds(pl.multiple_of((d // self.groups) * self.wide, self.wide), self.wide)

    def dev(self, d):
        return (d // self.Z, d % self.Z)

    def copy(self, off, src, dst):
        t = lax.rem(self.me + off, self.count)
        return pltpu.make_async_remote_copy(
            src(t), dst(t), self.send.at[off - 1], self.recv.at[off - 1], device_id=self.dev(t), device_id_type=MESH
        )

    def begin(self, src, dst):
        @pl.loop(1, self.count)
        def _(off):
            self.copy(off, src, dst).start()

        pltpu.make_async_copy(src(self.me), dst(self.me), self.local).start()

    def end(self, src, dst):
        pltpu.make_async_copy(src(self.me), dst(self.me), self.local).wait()

        @pl.loop(1, self.count)
        def _(off):
            self.copy(off, src, dst).wait()


def forward_kernel(grid, units, nseq, sources, kvw, *refs):
    f32, bf16 = jnp.float32, jnp.bfloat16
    n = 6
    start_ref, ends_ref, index_ref, x_ref, dy_ref = refs[:5]
    ins, refs = refs[5 : 5 + n], refs[5 + n :]
    fulls, refs = refs[:n], refs[n:]
    dyx_ref, n2x_ref, refs = *refs[:2], refs[2:]
    n1_ref, q_ref, win_ref, att_ref, mixed_ref, gains_ref, refs = *refs[:6], refs[6:]
    n2, wbuf, small, kv, got, picked, send, recv, local, xsend, xrecv, xlocal, lsem, msend, mrecv = refs
    p = Place(grid)
    count = p.count
    tok, width = x_ref.shape
    batches = tok // BLK
    p.barrier()
    items = [Gather(p, t, ins[t.array], fulls[t.array], send.at[u], recv.at[u], local.at[u]) for u, t in enumerate(units)]
    steps = Steps(staggered(items, [0] + list(range(2, len(items) + 1))))
    advance, through = steps.advance, steps.through

    def load(i, dst, sem):
        return pltpu.make_async_copy(fulls[i], dst, lsem.at[sem])

    def to_mate(k, src, dst):
        return (
            pltpu.make_async_copy(src, dst, lsem.at[3 + k]),
            pltpu.make_async_remote_copy(src, dst, msend.at[k], mrecv.at[k], device_id=p.mate, device_id_type=MESH),
        )

    advance(1)
    shared = [to_mate(0, dy_ref, dyx_ref.at[p.half])]
    start(shared[0])
    x = x_ref[...].astype(f32)
    mixed_ref[...] = x * lax.rsqrt(jnp.mean(x * x, axis=-1, keepdims=True) + EPS)
    through(0)
    load(0, small, 0).start()
    load(0, small, 0).wait()
    gains = small[..., kvw:].reshape(width, 128).astype(f32).T
    gains_ref[...] = gains[:8]
    n1_ref[...] = (mixed_ref[...] * gains[0:1]).astype(bf16)
    ex1 = Exchange(p, count, xsend.at[0], xrecv.at[0], xlocal.at[0])
    ex2 = Exchange(p, count, xsend.at[1], xrecv.at[1], xlocal.at[1])

    kv_value = jnp.dot(n1_ref[...], small[..., :kvw].reshape(width, kvw), preferred_element_type=f32).astype(bf16)
    kv[...] = kv_value.reshape(kv.shape)

    def src1(t):
        g, c = ex1.piece(t)
        return kv.at[:, g, :, c]

    def dst1(t):
        return got.at[ex1.me]

    def src2(t):
        return picked.at[t]

    def dst2(t):
        g, c = ex2.piece(ex2.me)
        return win_ref.at[:, :, g, :, c]

    ex1.begin(src1, dst1)
    advance(6)
    ex1.end(src1, dst1)

    @pl.loop(0, count)
    def _(t):
        for m in range(batches):
            for i in range(sources):
                picked[t, m, i] = got[index_ref[t, m * sources + i], m]

    ex2.begin(src2, dst2)
    through(1)
    load(1, wbuf, 1).start()
    advance(2)
    load(1, wbuf, 1).wait()
    tile = 512
    for j in range(0, width, tile):
        w = wbuf[..., j : j + tile].reshape(width, tile)
        q_ref[:, j : j + tile] = (jnp.dot(n1_ref[...], w, preferred_element_type=f32) * (HD**-0.5)).astype(bf16)
        advance()
    through(2)
    load(2, wbuf, 2).start()
    advance(0)
    ex2.end(src2, dst2)
    load(2, wbuf, 2).wait()
    for m in range(batches):
        rows = pl.ds(m * BLK, BLK)
        for h0 in range(0, H, 2):

            @pl.loop(h0, h0 + 2)
            def _(h):
                cols = pl.ds(pl.multiple_of(h * HD, HD), HD)
                mask = window_mask(start_ref[m], ends_ref, nseq, m, BLK, sources * BLK)
                k = win_ref[m, :, :, :, :HD].reshape(sources * BLK, HD)
                v = win_ref[m, :, :, :, HD:].reshape(sources * BLK, HD)
                prob = softmax_rows(q_ref[rows, cols], k, mask)
                att_ref[rows, cols] = jnp.dot(prob.astype(bf16), v, preferred_element_type=f32).astype(bf16)

            advance()
        for j in range(0, width, tile):
            w = wbuf[..., j : j + tile].reshape(width, tile)
            mixed_ref[rows, j : j + tile] = x_ref[rows, j : j + tile].astype(f32) + jnp.dot(att_ref[rows], w, preferred_element_type=f32)
        mixed = mixed_ref[rows]
        inverse = lax.rsqrt(jnp.mean(mixed * mixed, axis=-1, keepdims=True) + EPS)
        n2[rows] = (mixed * inverse * gains_ref[1:2]).astype(bf16)
        shared.append(to_mate(1 + m, n2.at[rows], n2x_ref.at[p.half, rows]))
        start(shared[-1])
        advance(2)
    steps.finish()
    for copies in shared:
        for c in copies:
            c.wait()


def forward(grid, shards, units, x, dy, start, ends, index, sources, kvw, collective_id):
    a, b, c, z = grid
    count = a * b * c * z
    tok, width = x.shape
    batches = tok // BLK
    bf16 = jnp.bfloat16
    groups = BLK // 16
    wide = 2 * HD * groups // count
    rows = shards[1].shape[0]
    U = len(units)
    any_, vmem, smem = (pl.BlockSpec(memory_space=s) for s in (pl.ANY, pltpu.VMEM, pltpu.SMEM))
    dma = pltpu.SemaphoreType.DMA
    sds = jax.ShapeDtypeStruct
    kinds = {t.array: t.kind for t in units}
    whole = [tuple(grid[:3]) + (z // 2 if kinds[i] == ROWS else z,) + s.shape[-2:] for i, s in enumerate(shards)]
    outs = pl.pallas_call(
        functools.partial(forward_kernel, grid, units, ends.shape[1], sources, kvw),
        out_shape=[sds(w, bf16) for w in whole]
        + [sds((2, tok, width), bf16)] * 2
        + [
            sds((tok, width), bf16),
            sds((tok, width), bf16),
            sds((batches, sources, groups, 16, 2 * HD), bf16),
            sds((tok, width), bf16),
            sds((tok, width), jnp.float32),
            sds((8, width), jnp.float32),
        ],
        in_specs=[smem, smem, smem, vmem, any_] + [any_] * 6,
        out_specs=[any_] * 8 + [vmem] * 6,
        scratch_shapes=[
            pltpu.VMEM((tok, width), bf16),
            pltpu.VMEM(tuple(grid) + (rows, width), bf16),
            pltpu.VMEM(tuple(grid) + (rows, shards[0].shape[1]), bf16),
            pltpu.VMEM((batches, groups, 16, 2 * HD), bf16),
            pltpu.VMEM((count, batches, 16, wide), bf16),
            pltpu.VMEM((count, batches, sources, 16, wide), bf16),
            dma((U, 12)),
            dma((U, 12)),
            dma((U,)),
            dma((2, count - 1)),
            dma((2, count - 1)),
            dma((2,)),
            dma((4 + batches,)),
            dma((1 + batches,)),
            dma((1 + batches,)),
        ],
        compiler_params=pltpu.CompilerParams(collective_id=collective_id, has_side_effects=True, vmem_limit_bytes=VMEM),
        name="forward",
    )(start, ends, index, x, dy, *shards)
    fulls = [o.reshape(-1, s.shape[-1]) for o, s in zip(outs, shards)]
    dy_pair, n2_pair, n1, q, window, att, mixed, gains = outs[6:]
    return fulls, dy_pair, n2_pair, n1, q, window, att, mixed, gains


def backward_kernel(grid, units, nseq, sources, kvw, names, *refs):
    r = types.SimpleNamespace(**dict(zip(names, refs)))
    rest = list(refs[len(names) :])
    p = Place(grid)
    count = p.count
    landings = [rest.pop(0) for _ in units]
    parts = [[rest.pop(0) for _ in u.link_buffers(grid)[1:]] for u in units]
    P_all, T_all, sums, dkv_own, send, recv, local, xsend, xrecv, xlocal, msend, mrecv, sem = rest
    tok, width = r.n1.shape
    batches = tok // BLK
    hidden = r.wg.shape[1]
    grads = [r.g_small, r.g_wq, r.g_wo, r.g_wg, r.g_wu, r.g_wd]
    outs = [r.o_small, r.o_wq, r.o_wo, r.o_wg, r.o_wu, r.o_wd]
    items = {}
    for u, unit in enumerate(units):
        items[unit.array, unit.cols[0]] = Scatter(
            p, unit, grads[unit.array], outs[unit.array], landings[u], parts[u], (send.at[u], recv.at[u], local.at[u])
        )
    rs = Sums({ALL: (P_all, T_all), ROWS: None})
    p.barrier()
    dot = functools.partial(jnp.dot, preferred_element_type=F32)

    def dot_t(a, b):
        return lax.dot_general(a, b, (((1,), (1,)), ((), ())), preferred_element_type=F32)

    def t_dot(a, b):
        return lax.dot_general(a, b, (((0,), (0,)), ((), ())), preferred_element_type=F32)

    def local_copy(src, dst, k):
        return pltpu.make_async_copy(src, dst, sem.at[k])

    def fetch(src, dst, k):
        c = local_copy(src, dst, k)
        c.start()
        c.wait()

    def to_mate(k, src, dst):
        return pltpu.make_async_remote_copy(src, dst, msend.at[k], mrecv.at[k], device_id=p.mate, device_id_type=MESH)

    dn2_swap = to_mate(0, r.dn2_to, r.dn2_got)
    out_swap = to_mate(1, r.out_to, r.out_got)
    tile = 256
    tiles = hidden // tile
    third = tiles // 3
    f32_tok, bf_tok = pltpu.VMEM((tok, width), F32), pltpu.VMEM((tok, width), BF16)
    panel = grid + (width // count,)

    def ffn(n2, n2t, dy, dn2, wg, wu, wd, put_g, put_u, hid, hid_t):
        def weights(i, slot):
            cols = pl.ds(i * tile, tile)
            return [
                local_copy(r.wg.at[:, cols], wg.at[slot], 3 * slot),
                local_copy(r.wu.at[:, cols], wu.at[slot], 3 * slot + 1),
                local_copy(r.wd.at[cols], wd.at[slot], 3 * slot + 2),
            ]

        def results(i, slot):
            cols = pl.ds(i * tile, tile)
            return [
                local_copy(put_g.at[slot], r.g_wg.at[..., cols], 6 + 4 * slot),
                local_copy(put_u.at[slot], r.g_wu.at[..., cols], 7 + 4 * slot),
                local_copy(hid.at[slot], r.hidden.at[:, cols], 8 + 4 * slot),
                local_copy(hid_t.at[slot], r.hidden_t.at[cols], 9 + 4 * slot),
            ]

        start(weights(0, 0))
        first = [local_copy(r.n2, n2, 14), local_copy(r.dy, dy, 15)]
        start(first)
        dn2[...] = jnp.zeros_like(dn2)
        for c in first:
            c.wait()
        for k in range(2):
            n2t[:, k * tok : (k + 1) * tok] = n2[k].T
        def step(i, slot, ahead, behind):
            if ahead is not None:
                start(weights(ahead, 1 - slot))
            for c in weights(i, slot):
                c.wait()
            if behind is not None:
                for c in results(behind, slot):
                    c.wait()
            rows = n2[...].reshape(2 * tok, width)
            gate = dot(rows, wg[slot])
            up = dot(rows, wu[slot])
            value, slope = geglu_parts(gate)
            low = (value * up).astype(BF16)
            hid[slot] = low
            hid_t[slot] = low.T
            dh = dot_t(dy[...].reshape(2 * tok, width), wd[slot])
            dg = (dh * up * slope).astype(BF16)
            du = (dh * value).astype(BF16)
            back = dot_t(dg, wg[slot]) + dot_t(du, wu[slot])
            dn2[...] += back.reshape(dn2.shape)
            put_g[slot] = dot(n2t[...], dg).astype(BF16).reshape(panel + (tile,))
            put_u[slot] = dot(n2t[...], du).astype(BF16).reshape(panel + (tile,))
            start(results(i, slot))

        for i in range(tiles):
            done = i % third == third - 1
            step(i, i % 2, i + 1 if i + 1 < tiles else None, i - 2 if i % third >= 2 else None)
            if done:
                for j in (i - 1, i):
                    for c in results(j, j % 2):
                        c.wait()
                rs.add(items[3, (i + 1 - third) * tile])
                rs.add(items[4, (i + 1 - third) * tile])
            if i >= third - 1:
                rs.tick(1)
        n2[0] = dn2[1 - p.half].astype(BF16)
        fetch(n2.at[0], r.dn2_to, 14)
        dn2_swap.start()
        fetch(dn2.at[p.half], r.dn2_own, 14)

    pair = pltpu.VMEM((2, tok, width), BF16)
    pl.run_scoped(
        ffn,
        pair,
        pltpu.VMEM((width, 2 * tok), BF16),
        pair,
        pltpu.VMEM((2, tok, width), F32),
        pltpu.VMEM((2, width, tile), BF16),
        pltpu.VMEM((2, width, tile), BF16),
        pltpu.VMEM((2, tile, width), BF16),
        pltpu.VMEM((2,) + panel + (tile,), BF16),
        pltpu.VMEM((2,) + panel + (tile,), BF16),
        pltpu.VMEM((2, 2 * tok, tile), BF16),
        pltpu.VMEM((2, tile, 2 * tok), BF16),
    )

    def ffn_rest(dy, hid_t, put_rows, hid, wd, out):
        rows, part = hidden // 2, width // 3
        pulls = [local_copy(r.dy, dy, 0)] + [local_copy(r.hidden_t.at[pl.ds(y * rows, rows)], hid_t.at[y], 1 + y) for y in range(2)]
        start(pulls)
        for c in pulls:
            c.wait()
        for k in range(3):
            cols = pl.ds(k * part, part)
            puts = [local_copy(put_rows.at[y], r.g_wd.at[y, :, :, :, :, cols], 4 + y) for y in range(2)]
            for y in range(2):
                value = dot(hid_t[y], dy[:, :, cols].reshape(2 * tok, part))
                put_rows[y] = value.astype(BF16).reshape(put_rows.shape[1:])
                puts[y].start()
            for c in puts:
                c.wait()
            rs.add(items[5, k * part])
            rs.tick(1)
        some = hidden // 3
        for turn in range(2):
            who = 1 - p.half if turn == 0 else p.half

            def pull(k):
                cols = pl.ds(k * some, some)
                return [
                    local_copy(r.hidden.at[pl.ds(pl.multiple_of(who * tok, tok), tok), cols], hid.at[k % 2], 6 + 2 * (k % 2)),
                    local_copy(r.wd.at[cols], wd.at[k % 2], 7 + 2 * (k % 2)),
                ]

            start(pull(0))
            for k in range(3):
                if k < 2:
                    start(pull(k + 1))
                for c in pull(k):
                    c.wait()
                value = dot(hid[k % 2], wd[k % 2])
                out[...] = value if k == 0 else out[...] + value
            if turn == 0:
                dy[0] = out[...].astype(BF16)
                fetch(dy.at[0], r.out_to, 10)
                out_swap.start()
            else:
                fetch(out, r.out_own, 10)

    def weight_grad(a, b, into, array, k0, scale=None):
        half = width // 2

        def run(at, put):
            at[...] = a.T
            n = half // tile
            for k in range(2):
                puts = [local_copy(put.at[j], into.at[..., pl.ds(k * half + j * tile, tile)], k0 + j) for j in range(n)]
                for j in range(n):
                    c0 = k * half + j * tile
                    value = dot(at[...], b[:, c0 : c0 + tile])
                    value = value if scale is None else value * scale
                    put[j] = value.astype(BF16).reshape(panel + (tile,))
                    puts[j].start()
                for c in puts:
                    c.wait()
                rs.add(items[array, k * half])

        pl.run_scoped(run, pltpu.VMEM((width, tok), BF16), pltpu.VMEM((half // tile,) + panel + (tile,), BF16))

    gains = r.gains

    def norm_back(value, gain, grad):
        inverse = lax.rsqrt(jnp.mean(value * value, axis=-1, keepdims=True) + EPS)
        u = grad * gain
        along = jnp.sum(u * value, axis=-1, keepdims=True) / width
        return inverse * u - value * (inverse * inverse * inverse) * along, jnp.sum(grad * value * inverse, axis=0, keepdims=True)

    def phase_c(dmixed, datt, dq, dgain):
        dgain[...] = jnp.zeros_like(dgain)

        def through_ffn(mixed, dn2, got2, dy, att, wo):
            pulls = [
                local_copy(r.mixed, mixed, 0),
                local_copy(r.dn2_own, dn2, 1),
                local_copy(r.dy.at[p.half], dy, 2),
                local_copy(r.wo, wo, 3),
                local_copy(r.att, att, 4),
            ]
            start(pulls)
            dn2_swap.wait()
            fetch(r.dn2_got, got2, 5)
            for c in pulls:
                c.wait()
            total = jnp.zeros((1, width), F32)
            for i in range(0, tok, 128):
                rows = pl.ds(i, 128)
                d, g = norm_back(mixed[rows], gains[1:2], dn2[rows] + got2[rows].astype(F32))
                total = total + g
                d = dy[rows].astype(F32) + d
                dmixed[rows] = d
                dy[rows] = d.astype(BF16)
            dgain[1:2] = total
            for j in range(0, width, 512):
                datt[:, j : j + 512] = dot_t(dy[...], wo[j : j + 512]).astype(BF16)
            rs.tick()
            weight_grad(att[...], dy, r.g_wo, 2, 6)

        pl.run_scoped(
            through_ffn,
            f32_tok,
            f32_tok,
            bf_tok,
            bf_tok,
            bf_tok,
            pltpu.VMEM((width, width), BF16),
        )
        rs.tick()

        def through_attention(dkvw, n1, w, small, x):
            later = [local_copy(r.n1, n1, 0), local_copy(r.wq, w, 1), local_copy(r.small, small, 2), local_copy(r.x, x, 3)]
            start(later)

            def heads(q, win, dkv):
                pulls = [local_copy(r.q, q, 4), local_copy(r.window, win, 5)]
                start(pulls)
                for c in pulls:
                    c.wait()
                for m in range(batches):
                    rows = pl.ds(m * BLK, BLK)
                    dkv[...] = jnp.zeros_like(dkv)
                    for h0 in range(0, H, 3):

                        @pl.loop(h0, h0 + 3)
                        def _(h):
                            cols = pl.ds(pl.multiple_of(h * HD, HD), HD)
                            mask = window_mask(r.start[m], r.ends, nseq, m, BLK, sources * BLK)
                            k = win[m, :, :, :, :HD].reshape(sources * BLK, HD)
                            v = win[m, :, :, :, HD:].reshape(sources * BLK, HD)
                            qh, d = q[rows, cols], datt[rows, cols]
                            prob = softmax_rows(qh, k, mask)
                            dp = dot_t(d, v)
                            ds = (prob * (dp - jnp.sum(prob * dp, axis=1, keepdims=True))).astype(BF16)
                            dq[rows, cols] = dot(ds, k).astype(BF16)
                            dkv[:, :HD] += t_dot(ds, qh)
                            dkv[:, HD:] += t_dot(prob.astype(BF16), d)

                        rs.tick(1)
                    dkvw[m] = dkv[...].astype(BF16).reshape(dkvw.shape[1:])

            pl.run_scoped(heads, bf_tok, pltpu.VMEM(r.window.shape, BF16), pltpu.VMEM((sources * BLK, kvw), F32))
            ex1 = Exchange(p, count, xsend.at[0], xrecv.at[0], xlocal.at[0])
            ex2 = Exchange(p, count, xsend.at[1], xrecv.at[1], xlocal.at[1])

            def src1(t):
                g, c = ex1.piece(t)
                return dkvw.at[:, :, g, :, c]

            def dst1(t):
                return r.got.at[ex1.me]

            def src2(t):
                return sums.at[t]

            def dst2(t):
                g, c = ex2.piece(ex2.me)
                return dkv_own.at[:, g, :, c]

            ex1.begin(src1, dst1)
            for c in later:
                c.wait()
            weight_grad(n1[...], dq, r.g_wq, 1, 6, HD**-0.5)
            rs.tick()

            def output(mixed, own, theirs, low):
                out_swap.wait()
                for i in range(0, tok, 256):
                    rows = pl.ds(i, 256)
                    pulls = [local_copy(r.mixed.at[rows], mixed, 8), local_copy(r.out_own.at[rows], own, 9), local_copy(r.out_got.at[rows], theirs, 10)]
                    start(pulls)
                    for c in pulls:
                        c.wait()
                    low[...] = (mixed[...] + own[...] + theirs[...].astype(F32)).astype(BF16)
                    fetch(low, r.block_out.at[rows], 11)

            some, some_low = pltpu.VMEM((256, width), F32), pltpu.VMEM((256, width), BF16)
            pl.run_scoped(output, some, some, some_low, some_low)
            rs.tick(0)

            def to_input(dn1, got):
                for j in range(0, width, 512):
                    dn1[:, j : j + 512] = dot_t(dq[...], w[j : j + 512]) * (HD**-0.5)
                ex1.end(src1, dst1)
                fetch(r.got, got, 8)

                @pl.loop(0, count)
                def _(d):
                    for m in range(batches):
                        s = jnp.zeros(sums.shape[2:], F32)
                        for i in range(sources):
                            k = m * sources + i
                            s = s + jnp.where(r.valid[d, k] > 0, got[r.index[d, k], m, i].astype(F32), 0.0)
                        sums[d, m] = s.astype(BF16)

                ex2.begin(src2, dst2)
                rs.tick(0)
                ex2.end(src2, dst2)
                dkv = dkv_own[...].reshape(tok, kvw)
                part = width // grid[0]
                for j in range(grid[0]):
                    dn1[:, j * part : (j + 1) * part] += dot_t(dkv, small[j, ..., :kvw].reshape(part, kvw))
                total = jnp.zeros((1, width), F32)
                for i in range(0, tok, 128):
                    rows = pl.ds(i, 128)
                    d, g = norm_back(x[rows].astype(F32), gains[0:1], dn1[rows])
                    total = total + g
                    x[rows] = (dmixed[rows] + d).astype(BF16)
                dgain[0:1] = total
                store = local_copy(x, r.grad_tokens, 3)
                store.start()
                for j in range(grid[0]):
                    value = t_dot(n1[:, j * part : (j + 1) * part], dkv)
                    small[j, ..., :kvw] = value.astype(BF16).reshape(panel[1:] + (kvw,))
                both = jnp.concatenate([dgain[...], jnp.zeros((120, width), F32)], axis=0)
                small[..., kvw:] = both.T.astype(BF16).reshape(panel + (128,))
                fetch(small, r.g_small, 2)
                rs.add(items[0, 0])
                rs.tick()
                store.wait()

            pl.run_scoped(to_input, f32_tok, pltpu.VMEM(r.got.shape, BF16))

        pl.run_scoped(
            through_attention,
            pltpu.VMEM((batches, sources, BLK // 16, 16, kvw), BF16),
            bf_tok,
            pltpu.VMEM((width, width), BF16),
            pltpu.VMEM(panel + (kvw + 128,), BF16),
            bf_tok,
        )

    def rest_of_it(P_rows, T_rows):
        rs.pools[ROWS] = (P_rows, T_rows)
        pl.run_scoped(
            ffn_rest,
            pair,
            pltpu.VMEM((2, hidden // 2, 2 * tok), BF16),
            pltpu.VMEM((2, 2, 2, p.Z // 2, hidden // 16, width // 3), BF16),
            pltpu.VMEM((2, tok, hidden // 3), BF16),
            pltpu.VMEM((2, hidden // 3, width), BF16),
            f32_tok,
        )
        pl.run_scoped(phase_c, f32_tok, bf_tok, bf_tok, pltpu.VMEM((8, width), F32))
        rs.finish()

    slot_rows = [u for u in units if u.kind == ROWS][0].shape(grid)
    pl.run_scoped(rest_of_it, pltpu.VMEM((3,) + slot_rows, BF16), pltpu.VMEM(slot_rows, BF16))


def backward(grid, fulls, shapes, saved, start, ends, index, valid, units, sources, kvw, collective_id):
    any_, vmem, smem = (pl.BlockSpec(memory_space=s) for s in (pl.ANY, pltpu.VMEM, pltpu.SMEM))
    sds, dma = jax.ShapeDtypeStruct, pltpu.SemaphoreType.DMA
    a, b, c, z = grid
    count = a * b * c * z
    tok, width = saved["n1"].shape
    batches = tok // BLK
    hidden = fulls[3].shape[1]
    U = len(units)
    kinds = {t.array: t.kind for t in units}
    whole = [grid[:3] + (z // 2 if kinds[i] == ROWS else z,) + s[-2:] for i, s in enumerate(shapes)]
    fulls = [fulls[0].reshape(whole[0])] + fulls[1:]
    inputs = dict(start=(start, smem), ends=(ends, smem), index=(index, smem), valid=(valid, smem))
    inputs.update({k: (v, any_) for k, v in zip(ARRAYS, fulls)})
    inputs.update({k: (v, any_) for k, v in saved.items()})
    inputs.update(gains=(saved["gains"], vmem))
    outputs = {"o_" + k: (sds(s, F32), vmem) for k, s in zip(ARRAYS, shapes)}
    low, high = (sds((tok, width), BF16), any_), (sds((tok, width), F32), any_)
    outputs.update(block_out=low, grad_tokens=low, dn2_to=low, dn2_got=low, out_to=low, out_got=low, dn2_own=high, out_own=high)
    wide = kvw * (BLK // 16) // count
    outputs.update(hidden=(sds((2 * tok, hidden), BF16), any_), hidden_t=(sds((hidden, 2 * tok), BF16), any_))
    outputs.update(got=(sds((count, batches, sources, 16, wide), BF16), any_))
    outputs.update({"g_" + k: (sds(w, BF16), any_) for k, w in zip(ARRAYS, whole)})
    names = list(inputs) + list(outputs)
    slot = (a, b, z, width // count, width // 2)
    results = pl.pallas_call(
        functools.partial(backward_kernel, grid, units, ends.shape[1], sources, kvw, names),
        out_shape=[s for s, _ in outputs.values()] + [sds(u.shape(grid), BF16) for u in units],
        in_specs=[s for _, s in inputs.values()],
        out_specs=[s for _, s in outputs.values()] + [any_] * U,
        scratch_shapes=[pltpu.VMEM(s, BF16) for u in units for s in u.link_buffers(grid)[1:]]
        + [
            pltpu.VMEM((5,) + slot, BF16),
            pltpu.VMEM(slot, BF16),
            pltpu.VMEM((count, batches, 16, wide), BF16),
            pltpu.VMEM((batches, BLK // 16, 16, kvw), BF16),
            dma((U, 8)),
            dma((U, 8)),
            dma((U, 2)),
            dma((2, count - 1)),
            dma((2, count - 1)),
            dma((2,)),
            dma((2,)),
            dma((2,)),
            dma((16,)),
        ],
        compiler_params=pltpu.CompilerParams(collective_id=collective_id, has_side_effects=True, vmem_limit_bytes=VMEM),
        name="backward",
    )(*[v for v, _ in inputs.values()])
    found = dict(zip(outputs, results))
    return found["block_out"], found["grad_tokens"], results[: len(ARRAYS)]

def place_of(perm):
    return jnp.argsort(perm, axis=1).astype(jnp.int32)


def fast_body(grid, tokens, w_query, w_keyval, w_out, w_gate, w_up, w_down, gain_attn, gain_ffn, cotangent, block_perm, extra_len):
    batches, _, rows, width = tokens.shape
    tok = batches * rows
    me = lax.axis_index(("dp", "fsdp"))
    count = lax.axis_size(("dp", "fsdp"))
    sources = WIN // BLK + 1
    kvw = w_keyval.shape[1]
    gains = jnp.stack([gain_attn, gain_ffn], axis=1)
    small = jnp.concatenate([w_keyval, jnp.pad(gains, ((0, 0), (0, 126)))], axis=1)
    sub = w_down.shape[0]
    half = w_gate.shape[1] // 2
    shards = [small, w_query, w_out, by_parity(w_gate, sub), by_parity(w_up, sub), w_down]
    units = [Unit(i, ALL, (0, s.shape[0]), (0, s.shape[1])) for i, s in enumerate(shards[:3])]
    for k in (0, 1):
        units += [Unit(i, COLS, (0, w_gate.shape[0]), (k * half // 2, half // 2)) for i in (3, 4)]
        units += [Unit(5, ROWS, (0, sub), (k * width // 2, width // 2))]
    holder = place_of(block_perm)
    block = block_perm[:, :, None] - (sources - 1) + jnp.arange(sources, dtype=jnp.int32)
    index = jnp.take_along_axis(holder[:, None, :], jnp.maximum(block, 0), axis=2)
    index = index.transpose(1, 0, 2).reshape(-1, batches * sources)
    start = lax.dynamic_slice_in_dim(block_perm, me, 1, axis=1)[:, 0] * BLK
    ends = jnp.cumsum(extra_len + (WIN - 1), axis=1).astype(jnp.int32)
    x = tokens.reshape(tok, width)
    dy = cotangent.reshape(tok, width)
    fulls, dy_pair, n2_pair, n1b, query, window, att, mixed, gains = forward(grid, shards, units, x, dy, start, ends, index, sources, kvw, 0)
    block = block_perm[:, :, None] + (sources - 1) - jnp.arange(sources, dtype=jnp.int32)
    reader = jnp.take_along_axis(holder[:, None, :], jnp.minimum(block, count - 1), axis=2)
    reader = reader.transpose(1, 0, 2).reshape(-1, batches * sources)
    valid = (block < count).astype(jnp.int32).transpose(1, 0, 2).reshape(-1, batches * sources)
    saved = dict(n2=n2_pair, dy=dy_pair, n1=n1b, q=query, window=window, att=att, mixed=mixed, x=x, gains=gains)
    back = [Unit(i, ALL, (0, s.shape[0]), (c, min(width // 2, s.shape[1] - c))) for i, s in enumerate(shards[:3]) for c in range(0, s.shape[1], width // 2)]
    for k in range(3):
        back += [Unit(i, COLS, (0, w_gate.shape[0]), (k * half // 3, half // 3)) for i in (3, 4)]
        back += [Unit(5, ROWS, (0, sub), (k * width // 3, width // 3))]
    block_out, grad_tokens, grads = backward(
        grid, fulls, [s.shape for s in shards], saved, start, ends, reader, valid, back, sources, kvw, 1
    )
    small, dq, do, dg, du, dd = grads
    dg, du = from_parity(dg, sub), from_parity(du, sub)
    return (
        block_out.reshape(tokens.shape),
        grad_tokens.reshape(tokens.shape),
        dq,
        small[:, :kvw],
        do,
        dg,
        du,
        dd,
        small[:, kvw],
        small[:, kvw + 1],
    )


def by_parity(w, sub):
    rows, hidden = w.shape
    return w.reshape(rows, -1, 2, sub).transpose(2, 0, 1, 3).reshape(2, rows, hidden // 2)


def from_parity(w, sub):
    _, rows, part = w.shape
    return w.reshape(2, rows, -1, sub).transpose(1, 2, 0, 3).reshape(rows, 2 * part)


def solution(mesh):
    count = mesh.shape["dp"] * mesh.shape["fsdp"]
    grid = (2, 2, 2, mesh.shape["fsdp"])
    whole_tiles = mesh.shape["dp"] == 8 and 1536 % (16 * count) == 0
    run = functools.partial(fast_body, grid) if whole_tiles else body
    placed = (
        P(None, ("dp", "fsdp"), None, None),
        P(("dp", "fsdp"), None),
        P(("dp", "fsdp"), None),
        P(("dp", "fsdp"), None),
        P(("dp", "fsdp"), None),
        P(("dp", "fsdp"), None),
        P(("dp", "fsdp"), None),
        P(("dp", "fsdp")),
        P(("dp", "fsdp")),
        P(None, ("dp", "fsdp"), None, None),
        P(),
        P(),
    )
    return jax.shard_map(
        run,
        mesh=mesh,
        in_specs=placed,
        out_specs=(
            P(None, ("dp", "fsdp"), None, None),
            P(None, ("dp", "fsdp"), None, None),
            P(("dp", "fsdp"), None),
            P(("dp", "fsdp"), None),
            P(("dp", "fsdp"), None),
            P(("dp", "fsdp"), None),
            P(("dp", "fsdp"), None),
            P(("dp", "fsdp"), None),
            P(("dp", "fsdp")),
            P(("dp", "fsdp")),
        ),
        check_vma=False,
    )
```

```python
import functools
import math
import types

import jax
import jax.numpy as jnp
from jax import lax
from jax.experimental import pallas as pl
from jax.experimental.pallas import tpu as pltpu
from jax.sharding import PartitionSpec as P

H = 6
HD = 256
WIN = 1024
BLK = 256


EPS = 1e-06
VMEM = 62 * 1024 * 1024


def for_sending(x):
    return jax.tree.map(lambda a: a.astype(jnp.bfloat16) if a.dtype == jnp.float32 else a, x)


def shifted(value, axis, steps):
    count = lax.axis_size(axis)
    leading, last = (max(0, -steps), min(count, count - steps))
    return lax.ppermute(value, axis, [(source, source + steps) for source in range(leading, last)])


def norm_rows(value, gain):
    inverse = lax.rsqrt(jnp.mean(value * value, axis=-1, keepdims=True) + EPS)
    return (value * inverse * gain, inverse)


def norm_back(value, inverse, gain, grad):
    scaled = grad * gain
    width = value.shape[-1]
    dvalue = (
        inverse * scaled
        - value * inverse**3 * jnp.sum(scaled * value, axis=-1, keepdims=True) / width
    )
    dgain = jnp.sum(grad * value * inverse, axis=0)
    return (dvalue, dgain)


def sequence_of(positions, ends):
    return jnp.sum((positions[:, None] >= ends[None, :]).astype(jnp.int32), axis=1)


def visible_mask(query_pos, key_pos, ends):
    same = sequence_of(query_pos, ends)[:, None] == sequence_of(key_pos, ends)[None, :]
    gap = query_pos[:, None] - key_pos[None, :]
    return same & (gap >= 0) & (gap < WIN) & (key_pos[None, :] >= 0)


def geglu(gate, up):
    return jax.nn.gelu(gate, approximate=True) * up


def move_keys(value, order, count):
    rows = value.shape[0]
    spread = lax.all_to_all(value, ("dp", "fsdp"), split_axis=1, concat_axis=0, tiled=True)
    pieces = spread.reshape(count, rows, spread.shape[1])
    placed = jnp.take(pieces, order, axis=0).reshape(count * rows, spread.shape[1])
    return lax.all_to_all(placed, ("dp", "fsdp"), split_axis=0, concat_axis=1, tiled=True)


def move_grads(value, order, count):
    rows = value.shape[0]
    spread = lax.all_to_all(
        for_sending(value), ("dp", "fsdp"), split_axis=1, concat_axis=0, tiled=True
    ).astype(value.dtype)
    pieces = spread.reshape(count, rows, spread.shape[1])
    placed = jnp.take(pieces, order, axis=0).reshape(count * rows, spread.shape[1])
    return lax.all_to_all(
        for_sending(placed), ("dp", "fsdp"), split_axis=0, concat_axis=1, tiled=True
    ).astype(placed.dtype)


def body(
    tokens,
    w_query,
    w_keyval,
    w_out,
    w_gate,
    w_up,
    w_down,
    gain_attn,
    gain_ffn,
    cotangent,
    block_perm,
    extra_len,
):
    count = lax.axis_size(("dp", "fsdp"))
    me = lax.axis_index(("dp", "fsdp"))
    batches = tokens.shape[0]
    sources = WIN // BLK + 1
    scale = HD ** (-0.5)
    shards = (w_query, w_keyval, w_out, w_gate, w_up, w_down, gain_attn, gain_ffn)
    device_ids = jnp.arange(count, dtype=jnp.int32)
    totals = None
    outputs = []
    input_grads = []
    for batch in range(batches):
        full = (
            lax.all_gather(shards[0], ("dp", "fsdp"), axis=0, tiled=True),
            lax.all_gather(shards[1], ("dp", "fsdp"), axis=0, tiled=True),
            lax.all_gather(shards[2], ("dp", "fsdp"), axis=0, tiled=True),
            lax.all_gather(shards[3], ("dp", "fsdp"), axis=0, tiled=True),
            lax.all_gather(shards[4], ("dp", "fsdp"), axis=0, tiled=True),
            lax.all_gather(shards[5], ("dp", "fsdp"), axis=0, tiled=True),
            lax.all_gather(shards[6], ("dp", "fsdp"), axis=0, tiled=True),
            lax.all_gather(shards[7], ("dp", "fsdp"), axis=0, tiled=True),
        )
        wq, wkv, wo, wg, wu, wd, g1b, g2b = full
        g1 = g1b.astype(jnp.float32)
        g2 = g2b.astype(jnp.float32)
        perm_row = block_perm[batch]
        ends = jnp.cumsum(extra_len[batch] + (WIN - 1))
        mine = lax.dynamic_slice_in_dim(perm_row, me, 1)[0]
        holder = jnp.sum(
            jnp.where(perm_row[None, :] == device_ids[:, None], device_ids[None, :], 0), axis=1
        )
        query_pos = mine * BLK + jnp.arange(BLK, dtype=jnp.int32)
        key_pos = (mine - (sources - 1)) * BLK + jnp.arange(sources * BLK, dtype=jnp.int32)
        mask = jnp.repeat(visible_mask(query_pos, key_pos, ends), H, axis=0)
        x = tokens[batch, 0].astype(jnp.float32)
        n1, r1 = norm_rows(x, g1)
        n1b = n1.astype(jnp.bfloat16)
        query = (jnp.dot(n1b, wq, preferred_element_type=jnp.float32) * scale).astype(jnp.bfloat16)
        query_rows = query.reshape(BLK * H, HD)
        keyval = jnp.dot(n1b, wkv, preferred_element_type=jnp.float32).astype(jnp.bfloat16)
        ordered = move_keys(keyval, holder, count)
        window = [ordered] * sources
        for back in range(1, sources):
            window[sources - 1 - back] = shifted(ordered, ("dp", "fsdp"), back)
        picked = move_keys(jnp.concatenate(window, axis=0), perm_row, count)
        keys_src = picked[:, :HD]
        values_src = picked[:, HD:]
        scores = jnp.einsum("qd,kd->qk", query_rows, keys_src, preferred_element_type=jnp.float32)
        masked = jnp.where(mask, scores, -1e30)
        top = jnp.max(masked, axis=1, keepdims=True)
        expd = jnp.exp(masked - top)
        rowsum = jnp.sum(expd, axis=1, keepdims=True)
        lse = top + jnp.log(rowsum)
        probs_low = (expd / rowsum).astype(jnp.bfloat16)
        att = jnp.dot(probs_low, values_src, preferred_element_type=jnp.float32)
        att_low = att.reshape(BLK, H * HD).astype(jnp.bfloat16)
        mixed = x + jnp.dot(att_low, wo, preferred_element_type=jnp.float32)
        n2, r2 = norm_rows(mixed, g2)
        n2b = n2.astype(jnp.bfloat16)
        gate = jnp.dot(n2b, wg, preferred_element_type=jnp.float32)
        up = jnp.dot(n2b, wu, preferred_element_type=jnp.float32)
        hidden = geglu(gate, up).astype(jnp.bfloat16)
        outputs.append(
            (mixed + jnp.dot(hidden, wd, preferred_element_type=jnp.float32)).astype(jnp.bfloat16)
        )
        wq, wkv, wo, wg, wu, wd, g1b, g2b = (
            lax.all_gather(shards[0], ("dp", "fsdp"), axis=0, tiled=True),
            lax.all_gather(shards[1], ("dp", "fsdp"), axis=0, tiled=True),
            lax.all_gather(shards[2], ("dp", "fsdp"), axis=0, tiled=True),
            lax.all_gather(shards[3], ("dp", "fsdp"), axis=0, tiled=True),
            lax.all_gather(shards[4], ("dp", "fsdp"), axis=0, tiled=True),
            lax.all_gather(shards[5], ("dp", "fsdp"), axis=0, tiled=True),
            lax.all_gather(shards[6], ("dp", "fsdp"), axis=0, tiled=True),
            lax.all_gather(shards[7], ("dp", "fsdp"), axis=0, tiled=True),
        )
        dy = cotangent[batch, 0]
        d_down = jnp.einsum("tf,td->fd", hidden, dy, preferred_element_type=jnp.float32)
        d_hidden = jnp.einsum("td,fd->tf", dy, wd, preferred_element_type=jnp.float32)
        _, geglu_pull = jax.vjp(geglu, gate, up)
        d_gate, d_up = geglu_pull(d_hidden)
        d_gate_low = d_gate.astype(jnp.bfloat16)
        d_up_low = d_up.astype(jnp.bfloat16)
        d_wgate = jnp.einsum("td,tf->df", n2b, d_gate_low, preferred_element_type=jnp.float32)
        d_wup = jnp.einsum("td,tf->df", n2b, d_up_low, preferred_element_type=jnp.float32)
        d_n2 = jnp.einsum("tf,df->td", d_gate_low, wg, preferred_element_type=jnp.float32)
        d_n2 = d_n2 + jnp.einsum("tf,df->td", d_up_low, wu, preferred_element_type=jnp.float32)
        d_mixed_norm, d_g2 = norm_back(mixed, r2, g2, d_n2)
        d_mixed = dy.astype(jnp.float32) + d_mixed_norm
        d_branch = d_mixed.astype(jnp.bfloat16)
        d_wout = jnp.einsum("ta,td->ad", att_low, d_branch, preferred_element_type=jnp.float32)
        d_att = jnp.einsum("td,ad->ta", d_branch, wo, preferred_element_type=jnp.float32)
        d_att_rows = d_att.astype(jnp.bfloat16).reshape(BLK * H, HD)
        again = jnp.einsum("qd,kd->qk", query_rows, keys_src, preferred_element_type=jnp.float32)
        probs = jnp.exp(jnp.where(mask, again, -1e30) - lse)
        d_probs = jnp.einsum(
            "qd,kd->qk", d_att_rows, values_src, preferred_element_type=jnp.float32
        )
        delta = jnp.sum(probs * d_probs, axis=1, keepdims=True)
        d_scores = (probs * (d_probs - delta)).astype(jnp.bfloat16)
        d_query = jnp.dot(d_scores, keys_src, preferred_element_type=jnp.float32).astype(
            jnp.bfloat16
        )
        d_query = d_query.reshape(BLK, H * HD)
        d_keys = jnp.einsum("qk,qd->kd", d_scores, query_rows, preferred_element_type=jnp.float32)
        d_values = jnp.einsum(
            "qk,qd->kd", probs.astype(jnp.bfloat16), d_att_rows, preferred_element_type=jnp.float32
        )
        d_keyval_flat = jnp.concatenate([d_keys, d_values], axis=1)
        ordered_grads = move_grads(d_keyval_flat, holder, count).reshape(sources, BLK, 2 * HD)
        summed = ordered_grads[sources - 1]
        for back in range(1, sources):
            summed = summed + shifted(
                ordered_grads[sources - 1 - back].astype(jnp.bfloat16), ("dp", "fsdp"), -back
            ).astype(jnp.float32)
        d_keyval = move_grads(summed, perm_row, count).astype(jnp.bfloat16)
        d_wquery = jnp.einsum("td,ta->da", n1b, d_query, preferred_element_type=jnp.float32) * scale
        d_wkeyval = jnp.einsum("td,tc->dc", n1b, d_keyval, preferred_element_type=jnp.float32)
        d_n1 = jnp.einsum("ta,da->td", d_query, wq, preferred_element_type=jnp.float32) * scale
        d_n1 = d_n1 + jnp.einsum("tc,dc->td", d_keyval, wkv, preferred_element_type=jnp.float32)
        d_x_norm, d_g1 = norm_back(x, r1, g1, d_n1)
        input_grads.append((d_mixed + d_x_norm).astype(jnp.bfloat16))
        local = (d_wquery, d_wkeyval, d_wout, d_wgate, d_wup, d_down, d_g1, d_g2)
        totals = local if totals is None else tuple((a + b for a, b in zip(totals, local)))
    totals = lax.psum_scatter(totals, ("dp", "fsdp"), scatter_dimension=0, tiled=True)
    block_out = jnp.stack(outputs)[:, None]
    grad_tokens = jnp.stack(input_grads)[:, None]
    return (
        block_out,
        grad_tokens,
        totals[0],
        totals[1],
        totals[2],
        totals[3],
        totals[4],
        totals[5],
        totals[6],
        totals[7],
    )


MESH = pl.DeviceIdType.MESH
BF16, F32 = jnp.bfloat16, jnp.float32
ALL, COLS, ROWS = 0, 1, 2
ARRAYS = ("small", "wq", "wo", "wg", "wu", "wd")


class Place:
    def __init__(self, grid):
        self.grid = grid
        self.Z = grid[3]
        self.count = grid[0] * grid[1] * grid[2] * grid[3]
        dp = lax.axis_index("dp")
        self.z = lax.axis_index("fsdp")
        self.c = dp % 2
        self.x = (dp // 2) % 2
        self.y = dp // 4
        self.me = dp * self.Z + self.z
        self.half = self.z % 2
        self.pair = self.z // 2
        self.core = self.dev(c=1 - self.c)
        self.xdev = self.dev(x=1 - self.x)
        self.ydev = self.dev(y=1 - self.y)
        self.mate = self.dev(z=self.z + 1 - 2 * self.half)
        self.far = self.dev(z=(self.z + 2) % self.Z)

    def dev(self, y=None, x=None, c=None, z=None):
        y = self.y if y is None else y
        x = self.x if x is None else x
        c = self.c if c is None else c
        z = self.z if z is None else z
        return ((y * 2 + x) * 2 + c, z)

    def barrier(self):
        sem = pltpu.get_barrier_semaphore()

        @pl.loop(1, self.count)
        def _(off):
            t = lax.rem(self.me + off, self.count)
            pl.semaphore_signal(sem, inc=1, device_id=(t // self.Z, t % self.Z), device_id_type=MESH)

        pl.semaphore_wait(sem, self.count - 1)


def start(copies):
    for c in copies:
        c.start()


def wait_recv(copies):
    for c in copies:
        c.wait_recv()


def wait_send(copies):
    for c in copies:
        c.wait_send()


def halves(width):
    first = width - (width // 256) * 128
    return [(0, first), (first, width - first)]


class Unit:
    def __init__(self, array, kind, rows, cols):
        self.array, self.kind, self.rows, self.cols = array, kind, rows, cols
        self.width = cols[1]

    def shape(self, grid):
        return grid[:2] + (grid[3] // 2 if self.kind == ROWS else grid[3],) + (self.rows[1], self.width)

    def link_buffers(self, grid):
        a, b, z, r, w = self.shape(grid)
        h = halves(w)
        out = [(a, b, z, r, w), (b, z, r, h[0][1]), (a, z, r, h[1][1]), (z, r, h[0][1]), (z, r, h[1][1])]
        if self.kind == ALL:
            return out + [(z - 1, r, w)]
        if self.kind == COLS:
            return out + [(z // 2, r, w), (r, w)]
        return out + [(r, w)]


class Gather:
    def __init__(self, p, unit, src, dst, send, recv, local):
        self.p, self.dst, self.send, self.recv, self.local, self.kind = p, dst, send, recv, local, unit.kind
        self.r, self.all = pl.ds(*unit.rows), pl.ds(*unit.cols)
        self.h = [pl.ds(unit.cols[0] + a, b) for a, b in halves(unit.width)]
        self.src = (lambda half: src.at[half, self.r, self.all]) if unit.kind == COLS else (lambda half: src.at[self.r, self.all])
        self.spot = p.pair if unit.kind == ROWS else p.z

    def copy(self, k, src, dst, dev):
        return pltpu.make_async_remote_copy(src, dst, self.send.at[k], self.recv.at[k], device_id=dev, device_id_type=MESH)

    def same(self, k, ref, dev):
        return self.copy(k, ref, ref, dev)

    def block(self, y, x, cols):
        return self.dst.at[y, x, self.p.c, :, self.r, cols]

    def own(self):
        p = self.p
        return pltpu.make_async_copy(self.src(p.half), self.dst.at[p.y, p.x, p.c, self.spot, self.r, self.all], self.local)

    def z1(self):
        p = self.p
        there = self.dst.at[p.y, p.x, p.c, self.spot, self.r, self.all]
        if self.kind == ALL:
            return [self.copy(i - 1, self.src(0), there, p.dev(z=(p.z + i) % p.Z)) for i in range(1, p.Z)]
        if self.kind == COLS:
            return [self.copy(0, self.src(1 - p.half), there, p.mate)]
        return [self.copy(0, self.src(0), there, p.far)]

    def z2(self):
        p = self.p
        return [self.same(1, self.dst.at[p.y, p.x, p.c, pl.ds(2 * p.pair, 2), self.r, self.all], p.far)]

    def p1(self):
        p = self.p
        return [self.same(3, self.block(p.y, p.x, self.h[0]), p.xdev), self.same(4, self.block(p.y, p.x, self.h[1]), p.ydev)]

    def p2(self):
        p, every = self.p, slice(None)
        return [self.same(5, self.block(p.y, every, self.h[0]), p.ydev), self.same(6, self.block(every, p.x, self.h[1]), p.xdev)]

    def c0(self):
        p = self.p
        return [self.same(7, self.block(p.y, p.x, self.all), p.core)]

    def c1(self):
        p = self.p
        return [self.same(8, self.block(p.y, 1 - p.x, self.h[0]), p.core), self.same(9, self.block(1 - p.y, p.x, self.h[1]), p.core)]

    def c2(self):
        p, every = self.p, slice(None)
        return [self.same(10, self.block(1 - p.y, every, self.h[0]), p.core), self.same(11, self.block(every, 1 - p.x, self.h[1]), p.core)]

    def stages(self):
        def first():
            self.own().start()
            start(self.z1())

        def second():
            self.own().wait()
            wait_recv(self.z1())
            start(self.z2())

        def third():
            if self.kind == COLS:
                wait_recv(self.z2())
            else:
                self.own().wait()
                wait_recv(self.z1())
            start(self.p1() + self.c0())

        def fourth():
            wait_recv(self.p1())
            start(self.p2() + self.c1())

        def fifth():
            wait_recv(self.p2())
            start(self.c2())

        def last():
            wait_recv(self.c0() + self.c1() + self.c2())
            wait_send(self.z1() + (self.z2() if self.kind == COLS else []) + self.p1() + self.p2() + self.c0() + self.c1() + self.c2())

        return [first] + ([second] if self.kind == COLS else []) + [third, fourth, fifth, last]


class Scatter:
    def __init__(self, p, unit, src, out, landing, rest, sems):
        self.p, self.unit, self.kind = p, unit, unit.kind
        self.src, self.out, self.landing, self.rest = src, out, landing, rest
        self.send, self.recv, self.local = sems
        self.r, self.cols = pl.ds(*unit.rows), pl.ds(*unit.cols)
        self.h = [pl.ds(a, b) for a, b in halves(unit.width)]
        self.all = pl.ds(0, unit.width)
        self.n = unit.shape(p.grid)[2]
        self.stage = 0

    def copy(self, k, src, dst, dev):
        return pltpu.make_async_remote_copy(src, dst, self.send.at[k], self.recv.at[k], device_id=dev, device_id_type=MESH)

    def r0(self):
        p = self.p
        return [self.copy(0, self.src.at[:, :, 1 - p.c, :, self.r, self.cols], self.landing, p.core)]

    def loads(self):
        own = self.src.at[:, :, self.p.c, :, self.r, self.cols]
        return [
            pltpu.make_async_copy(self.landing, self.P.at[..., self.all], self.local.at[0]),
            pltpu.make_async_copy(own, self.T.at[..., self.all], self.local.at[1]),
        ]

    def r1(self):
        p, P = self.p, self.P
        return [self.copy(1, P.at[1 - p.y, :, :, :, self.h[0]], self.rest[0], p.ydev), self.copy(2, P.at[:, 1 - p.x, :, :, self.h[1]], self.rest[1], p.xdev)]

    def r2(self):
        p, P = self.p, self.P
        return [self.copy(3, P.at[p.y, 1 - p.x, :, :, self.h[0]], self.rest[2], p.xdev), self.copy(4, P.at[1 - p.y, p.x, :, :, self.h[1]], self.rest[3], p.ydev)]

    def r3(self):
        p, P = self.p, self.P
        if self.kind == ALL:
            return [self.copy(4 + i, P.at[p.y, p.x, (p.z + i) % p.Z, :, self.all], self.rest[4].at[i - 1], p.dev(z=(p.z + i) % p.Z)) for i in range(1, p.Z)]
        if self.kind == COLS:
            return [self.copy(5, P.at[p.y, p.x, pl.ds(2 * (1 - p.pair), 2), :, self.all], self.rest[4], p.far)]
        return [self.copy(5, P.at[p.y, p.x, 1 - p.pair, :, self.all], self.rest[4], p.far)]

    def r4(self):
        p = self.p
        return [self.copy(6, self.P.at[p.y, p.x, 2 * p.pair + 1 - p.half, :, self.all], self.rest[5], p.mate)]

    def add0(self):
        P, T, b, n = self.P, self.T, self.P.shape[1], self.n

        @pl.loop(0, P.shape[0] * b * n)
        def _(i):
            at = (i // (b * n), (i // n) % b, i % n, slice(None), self.all)
            P[at] = P[at] + T[at]

    def add1(self):
        p, P, n = self.p, self.P, self.n

        @pl.loop(0, 2 * n)
        def _(i):
            b, d = i // n, i % n
            P[p.y, b, d, :, self.h[0]] = P[p.y, b, d, :, self.h[0]] + self.rest[0][b, d]
            P[b, p.x, d, :, self.h[1]] = P[b, p.x, d, :, self.h[1]] + self.rest[1][b, d]

    def add2(self):
        p, P = self.p, self.P

        @pl.loop(0, self.n)
        def _(d):
            for k in (0, 1):
                P[p.y, p.x, d, :, self.h[k]] = P[p.y, p.x, d, :, self.h[k]] + self.rest[2 + k][d]

    def add3(self):
        p, got = self.p, self.rest[4]
        mine = lambda d: self.P[p.y, p.x, d, :, self.all].astype(F32)
        if self.kind == ALL:
            s = mine(p.z)
            for i in range(p.Z - 1):
                s = s + got[i].astype(F32)
            self.out[self.r, self.cols] = s
        elif self.kind == ROWS:
            self.out[self.r, self.cols] = mine(p.pair) + got[...].astype(F32)
        else:
            theirs = 2 * p.pair + 1 - p.half
            self.out[p.half, self.r, self.cols] = mine(p.z) + got[p.half].astype(F32)
            self.P[p.y, p.x, theirs, :, self.all] = (mine(theirs) + got[1 - p.half].astype(F32)).astype(BF16)

    def first(self):
        start(self.r0())

    @property
    def P(self):
        return self.pool.at[self.slot]

    def admit(self, pool, slot, T):
        self.pool, self.slot, self.T = pool, slot, T
        wait_recv(self.r0())
        start(self.loads())

    def settle(self):
        for c in self.loads():
            c.wait()
        self.add0()
        start(self.r1())

    def next(self):
        k, self.stage = self.stage, self.stage + 1
        if k == 0:
            wait_recv(self.r1())
            wait_send(self.r1())
            self.add1()
            start(self.r2())
        elif k == 1:
            wait_recv(self.r2())
            wait_send(self.r2())
            self.add2()
            start(self.r3())
        elif k == 2:
            wait_recv(self.r3())
            wait_send(self.r3() + self.r0())
            self.add3()
            if self.kind == COLS:
                start(self.r4())
        else:
            wait_recv(self.r4())
            wait_send(self.r4())
            self.out[1 - self.p.half, self.r, self.cols] = self.rest[5][...].astype(F32)
        return self.stage < (4 if self.kind == COLS else 3)


class Sums:
    def __init__(self, pools):
        self.pools, self.used = pools, {k: 0 for k in pools}
        self.queue, self.under_way = [], []

    def add(self, item):
        item.first()
        self.queue.append(item)

    def tick(self, count=1):
        for _ in range(count):
            new = self.queue.pop(0) if self.queue else None
            if new is not None:
                key = ROWS if new.kind == ROWS else ALL
                P, T = self.pools[key]
                new.admit(P, self.used[key] % P.shape[0], T)
                self.used[key] += 1
            self.under_way = [i for i in self.under_way if i.next()]
            if new is not None:
                new.settle()
                self.under_way.append(new)

    def finish(self):
        while self.queue or self.under_way:
            self.tick()


def staggered(items, starts=None):
    lists = [i.stages() for i in items]
    starts = starts or list(range(len(items)))
    steps = []
    for s in range(max(b + len(l) for b, l in zip(starts, lists))):
        for u in reversed(range(len(lists))):
            k = s - starts[u]
            if 0 <= k < len(lists[u]):
                steps.append((u, k == len(lists[u]) - 1, lists[u][k]))
    return steps


class Steps:
    def __init__(self, steps):
        self.steps, self.at = steps, 0

    def advance(self, count=1):
        for _ in range(count):
            if self.at < len(self.steps):
                self.steps[self.at][2]()
                self.at += 1

    def through(self, item):
        mark = [k for k, (u, done, _) in enumerate(self.steps) if u == item and done][0]
        self.advance(mark + 1 - self.at)

    def finish(self):
        self.advance(len(self.steps) - self.at)

def window_mask(start, ends, nseq, m, queries, keys):
    qpos = start + lax.broadcasted_iota(jnp.int32, (queries, 1), 0)
    first = jnp.maximum(qpos - (WIN - 1), 0)
    for k in range(nseq):
        end = ends[m, k]
        first = jnp.maximum(first, jnp.where(qpos >= end, end, 0))
    kpos = start - (keys - queries) + lax.broadcasted_iota(jnp.int32, (1, keys), 1)
    return (kpos >= first) & (kpos <= qpos)


def softmax_rows(q, k, mask):
    scores = lax.dot_general(q, k, (((1,), (1,)), ((), ())), preferred_element_type=jnp.float32)
    masked = jnp.where(mask, scores, -1e30)
    expd = jnp.exp(masked - jnp.max(masked, axis=1, keepdims=True))
    return expd * (1.0 / jnp.sum(expd, axis=1, keepdims=True))


def geglu_parts(gate):
    c = math.sqrt(2.0 / math.pi)
    square = gate * gate
    t = jnp.tanh(c * gate * (1.0 + 0.044715 * square))
    half = 0.5 * (1.0 + t)
    value = gate * half
    slope = half + 0.5 * gate * (1.0 - t * t) * c * (1.0 + 3 * 0.044715 * square)
    return value, slope


class Exchange:
    def __init__(self, p, count, send, recv, local):
        self.count, self.send, self.recv, self.local = count, send, recv, local
        self.me = p.me
        self.Z = p.Z
        self.groups = BLK // 16
        self.wide = 2 * HD * self.groups // count

    def piece(self, d):
        return d % self.groups, pl.ds(pl.multiple_of((d // self.groups) * self.wide, self.wide), self.wide)

    def dev(self, d):
        return (d // self.Z, d % self.Z)

    def copy(self, off, src, dst):
        t = lax.rem(self.me + off, self.count)
        return pltpu.make_async_remote_copy(
            src(t), dst(t), self.send.at[off - 1], self.recv.at[off - 1], device_id=self.dev(t), device_id_type=MESH
        )

    def begin(self, src, dst):
        @pl.loop(1, self.count)
        def _(off):
            self.copy(off, src, dst).start()

        pltpu.make_async_copy(src(self.me), dst(self.me), self.local).start()

    def end(self, src, dst):
        pltpu.make_async_copy(src(self.me), dst(self.me), self.local).wait()

        @pl.loop(1, self.count)
        def _(off):
            self.copy(off, src, dst).wait()


def forward_kernel(grid, units, nseq, sources, kvw, *refs):
    f32, bf16 = jnp.float32, jnp.bfloat16
    n = 6
    start_ref, ends_ref, index_ref, x_ref, dy_ref = refs[:5]
    ins, refs = refs[5 : 5 + n], refs[5 + n :]
    fulls, refs = refs[:n], refs[n:]
    dyx_ref, n2x_ref, refs = *refs[:2], refs[2:]
    n1_ref, q_ref, win_ref, att_ref, mixed_ref, gains_ref, refs = *refs[:6], refs[6:]
    n2, wbuf, small, kv, got, picked, send, recv, local, xsend, xrecv, xlocal, lsem, msend, mrecv = refs
    p = Place(grid)
    count = p.count
    tok, width = x_ref.shape
    batches = tok // BLK
    p.barrier()
    items = [Gather(p, t, ins[t.array], fulls[t.array], send.at[u], recv.at[u], local.at[u]) for u, t in enumerate(units)]
    steps = Steps(staggered(items, [0] + list(range(2, len(items) + 1))))
    advance, through = steps.advance, steps.through

    def load(i, dst, sem):
        return pltpu.make_async_copy(fulls[i], dst, lsem.at[sem])

    def to_mate(k, src, dst):
        return (
            pltpu.make_async_copy(src, dst, lsem.at[3 + k]),
            pltpu.make_async_remote_copy(src, dst, msend.at[k], mrecv.at[k], device_id=p.mate, device_id_type=MESH),
        )

    advance(1)
    shared = [to_mate(0, dy_ref, dyx_ref.at[p.half])]
    start(shared[0])
    x = x_ref[...].astype(f32)
    mixed_ref[...] = x * lax.rsqrt(jnp.mean(x * x, axis=-1, keepdims=True) + EPS)
    through(0)
    load(0, small, 0).start()
    load(0, small, 0).wait()
    gains = small[..., kvw:].reshape(width, 128).astype(f32).T
    gains_ref[...] = gains[:8]
    n1_ref[...] = (mixed_ref[...] * gains[0:1]).astype(bf16)
    ex1 = Exchange(p, count, xsend.at[0], xrecv.at[0], xlocal.at[0])
    ex2 = Exchange(p, count, xsend.at[1], xrecv.at[1], xlocal.at[1])

    kv_value = jnp.dot(n1_ref[...], small[..., :kvw].reshape(width, kvw), preferred_element_type=f32).astype(bf16)
    kv[...] = kv_value.reshape(kv.shape)

    def src1(t):
        g, c = ex1.piece(t)
        return kv.at[:, g, :, c]

    def dst1(t):
        return got.at[ex1.me]

    def src2(t):
        return picked.at[t]

    def dst2(t):
        g, c = ex2.piece(ex2.me)
        return win_ref.at[:, :, g, :, c]

    ex1.begin(src1, dst1)
    advance(6)
    ex1.end(src1, dst1)

    @pl.loop(0, count)
    def _(t):
        for m in range(batches):
            for i in range(sources):
                picked[t, m, i] = got[index_ref[t, m * sources + i], m]

    ex2.begin(src2, dst2)
    through(1)
    load(1, wbuf, 1).start()
    advance(2)
    load(1, wbuf, 1).wait()
    tile = 512
    for j in range(0, width, tile):
        w = wbuf[..., j : j + tile].reshape(width, tile)
        q_ref[:, j : j + tile] = (jnp.dot(n1_ref[...], w, preferred_element_type=f32) * (HD**-0.5)).astype(bf16)
        advance()
    through(2)
    load(2, wbuf, 2).start()
    advance(0)
    ex2.end(src2, dst2)
    load(2, wbuf, 2).wait()
    for m in range(batches):
        rows = pl.ds(m * BLK, BLK)
        for h0 in range(0, H, 2):

            @pl.loop(h0, h0 + 2)
            def _(h):
                cols = pl.ds(pl.multiple_of(h * HD, HD), HD)
                mask = window_mask(start_ref[m], ends_ref, nseq, m, BLK, sources * BLK)
                k = win_ref[m, :, :, :, :HD].reshape(sources * BLK, HD)
                v = win_ref[m, :, :, :, HD:].reshape(sources * BLK, HD)
                prob = softmax_rows(q_ref[rows, cols], k, mask)
                att_ref[rows, cols] = jnp.dot(prob.astype(bf16), v, preferred_element_type=f32).astype(bf16)

            advance()
        for j in range(0, width, tile):
            w = wbuf[..., j : j + tile].reshape(width, tile)
            mixed_ref[rows, j : j + tile] = x_ref[rows, j : j + tile].astype(f32) + jnp.dot(att_ref[rows], w, preferred_element_type=f32)
        mixed = mixed_ref[rows]
        inverse = lax.rsqrt(jnp.mean(mixed * mixed, axis=-1, keepdims=True) + EPS)
        n2[rows] = (mixed * inverse * gains_ref[1:2]).astype(bf16)
        shared.append(to_mate(1 + m, n2.at[rows], n2x_ref.at[p.half, rows]))
        start(shared[-1])
        advance(2)
    steps.finish()
    for copies in shared:
        for c in copies:
            c.wait()


def forward(grid, shards, units, x, dy, start, ends, index, sources, kvw, collective_id):
    a, b, c, z = grid
    count = a * b * c * z
    tok, width = x.shape
    batches = tok // BLK
    bf16 = jnp.bfloat16
    groups = BLK // 16
    wide = 2 * HD * groups // count
    rows = shards[1].shape[0]
    U = len(units)
    any_, vmem, smem = (pl.BlockSpec(memory_space=s) for s in (pl.ANY, pltpu.VMEM, pltpu.SMEM))
    dma = pltpu.SemaphoreType.DMA
    sds = jax.ShapeDtypeStruct
    kinds = {t.array: t.kind for t in units}
    whole = [tuple(grid[:3]) + (z // 2 if kinds[i] == ROWS else z,) + s.shape[-2:] for i, s in enumerate(shards)]
    outs = pl.pallas_call(
        functools.partial(forward_kernel, grid, units, ends.shape[1], sources, kvw),
        out_shape=[sds(w, bf16) for w in whole]
        + [sds((2, tok, width), bf16)] * 2
        + [
            sds((tok, width), bf16),
            sds((tok, width), bf16),
            sds((batches, sources, groups, 16, 2 * HD), bf16),
            sds((tok, width), bf16),
            sds((tok, width), jnp.float32),
            sds((8, width), jnp.float32),
        ],
        in_specs=[smem, smem, smem, vmem, any_] + [any_] * 6,
        out_specs=[any_] * 8 + [vmem] * 6,
        scratch_shapes=[
            pltpu.VMEM((tok, width), bf16),
            pltpu.VMEM(tuple(grid) + (rows, width), bf16),
            pltpu.VMEM(tuple(grid) + (rows, shards[0].shape[1]), bf16),
            pltpu.VMEM((batches, groups, 16, 2 * HD), bf16),
            pltpu.VMEM((count, batches, 16, wide), bf16),
            pltpu.VMEM((count, batches, sources, 16, wide), bf16),
            dma((U, 12)),
            dma((U, 12)),
            dma((U,)),
            dma((2, count - 1)),
            dma((2, count - 1)),
            dma((2,)),
            dma((4 + batches,)),
            dma((1 + batches,)),
            dma((1 + batches,)),
        ],
        compiler_params=pltpu.CompilerParams(collective_id=collective_id, has_side_effects=True, vmem_limit_bytes=VMEM),
        name="forward",
    )(start, ends, index, x, dy, *shards)
    fulls = [o.reshape(-1, s.shape[-1]) for o, s in zip(outs, shards)]
    dy_pair, n2_pair, n1, q, window, att, mixed, gains = outs[6:]
    return fulls, dy_pair, n2_pair, n1, q, window, att, mixed, gains


def backward_kernel(grid, units, nseq, sources, kvw, names, *refs):
    r = types.SimpleNamespace(**dict(zip(names, refs)))
    rest = list(refs[len(names) :])
    p = Place(grid)
    count = p.count
    landings = [rest.pop(0) for _ in units]
    parts = [[rest.pop(0) for _ in u.link_buffers(grid)[1:]] for u in units]
    P_all, T_all, sums, dkv_own, send, recv, local, xsend, xrecv, xlocal, msend, mrecv, sem = rest
    tok, width = r.n1.shape
    batches = tok // BLK
    hidden = r.wg.shape[1]
    grads = [r.g_small, r.g_wq, r.g_wo, r.g_wg, r.g_wu, r.g_wd]
    outs = [r.o_small, r.o_wq, r.o_wo, r.o_wg, r.o_wu, r.o_wd]
    items = {}
    for u, unit in enumerate(units):
        items[unit.array, unit.cols[0]] = Scatter(
            p, unit, grads[unit.array], outs[unit.array], landings[u], parts[u], (send.at[u], recv.at[u], local.at[u])
        )
    rs = Sums({ALL: (P_all, T_all), ROWS: None})
    p.barrier()
    dot = functools.partial(jnp.dot, preferred_element_type=F32)

    def dot_t(a, b):
        return lax.dot_general(a, b, (((1,), (1,)), ((), ())), preferred_element_type=F32)

    def t_dot(a, b):
        return lax.dot_general(a, b, (((0,), (0,)), ((), ())), preferred_element_type=F32)

    def local_copy(src, dst, k):
        return pltpu.make_async_copy(src, dst, sem.at[k])

    def fetch(src, dst, k):
        c = local_copy(src, dst, k)
        c.start()
        c.wait()

    def to_mate(k, src, dst):
        return pltpu.make_async_remote_copy(src, dst, msend.at[k], mrecv.at[k], device_id=p.mate, device_id_type=MESH)

    dn2_swap = to_mate(0, r.dn2_to, r.dn2_got)
    out_swap = to_mate(1, r.out_to, r.out_got)
    tile = 256
    tiles = hidden // tile
    third = tiles // 3
    f32_tok, bf_tok = pltpu.VMEM((tok, width), F32), pltpu.VMEM((tok, width), BF16)
    panel = grid + (width // count,)

    def ffn(n2, n2t, dy, dn2, wg, wu, wd, put_g, put_u, hid, hid_t):
        def weights(i, slot):
            cols = pl.ds(i * tile, tile)
            return [
                local_copy(r.wg.at[:, cols], wg.at[slot], 3 * slot),
                local_copy(r.wu.at[:, cols], wu.at[slot], 3 * slot + 1),
                local_copy(r.wd.at[cols], wd.at[slot], 3 * slot + 2),
            ]

        def results(i, slot):
            cols = pl.ds(i * tile, tile)
            return [
                local_copy(put_g.at[slot], r.g_wg.at[..., cols], 6 + 4 * slot),
                local_copy(put_u.at[slot], r.g_wu.at[..., cols], 7 + 4 * slot),
                local_copy(hid.at[slot], r.hidden.at[:, cols], 8 + 4 * slot),
                local_copy(hid_t.at[slot], r.hidden_t.at[cols], 9 + 4 * slot),
            ]

        start(weights(0, 0))
        first = [local_copy(r.n2, n2, 14), local_copy(r.dy, dy, 15)]
        start(first)
        dn2[...] = jnp.zeros_like(dn2)
        for c in first:
            c.wait()
        for k in range(2):
            n2t[:, k * tok : (k + 1) * tok] = n2[k].T
        def step(i, slot, ahead, behind):
            if ahead is not None:
                start(weights(ahead, 1 - slot))
            for c in weights(i, slot):
                c.wait()
            if behind is not None:
                for c in results(behind, slot):
                    c.wait()
            rows = n2[...].reshape(2 * tok, width)
            gate = dot(rows, wg[slot])
            up = dot(rows, wu[slot])
            value, slope = geglu_parts(gate)
            low = (value * up).astype(BF16)
            hid[slot] = low
            hid_t[slot] = low.T
            dh = dot_t(dy[...].reshape(2 * tok, width), wd[slot])
            dg = (dh * up * slope).astype(BF16)
            du = (dh * value).astype(BF16)
            back = dot_t(dg, wg[slot]) + dot_t(du, wu[slot])
            dn2[...] += back.reshape(dn2.shape)
            put_g[slot] = dot(n2t[...], dg).astype(BF16).reshape(panel + (tile,))
            put_u[slot] = dot(n2t[...], du).astype(BF16).reshape(panel + (tile,))
            start(results(i, slot))

        for i in range(tiles):
            done = i % third == third - 1
            step(i, i % 2, i + 1 if i + 1 < tiles else None, i - 2 if i % third >= 2 else None)
            if done:
                for j in (i - 1, i):
                    for c in results(j, j % 2):
                        c.wait()
                rs.add(items[3, (i + 1 - third) * tile])
                rs.add(items[4, (i + 1 - third) * tile])
            if i >= third - 1:
                rs.tick(1)
        n2[0] = dn2[1 - p.half].astype(BF16)
        fetch(n2.at[0], r.dn2_to, 14)
        dn2_swap.start()
        fetch(dn2.at[p.half], r.dn2_own, 14)

    pair = pltpu.VMEM((2, tok, width), BF16)
    pl.run_scoped(
        ffn,
        pair,
        pltpu.VMEM((width, 2 * tok), BF16),
        pair,
        pltpu.VMEM((2, tok, width), F32),
        pltpu.VMEM((2, width, tile), BF16),
        pltpu.VMEM((2, width, tile), BF16),
        pltpu.VMEM((2, tile, width), BF16),
        pltpu.VMEM((2,) + panel + (tile,), BF16),
        pltpu.VMEM((2,) + panel + (tile,), BF16),
        pltpu.VMEM((2, 2 * tok, tile), BF16),
        pltpu.VMEM((2, tile, 2 * tok), BF16),
    )

    def ffn_rest(dy, hid_t, put_rows, hid, wd, out):
        rows, part = hidden // 2, width // 3
        pulls = [local_copy(r.dy, dy, 0)] + [local_copy(r.hidden_t.at[pl.ds(y * rows, rows)], hid_t.at[y], 1 + y) for y in range(2)]
        start(pulls)
        for c in pulls:
            c.wait()
        for k in range(3):
            cols = pl.ds(k * part, part)
            puts = [local_copy(put_rows.at[y], r.g_wd.at[y, :, :, :, :, cols], 4 + y) for y in range(2)]
            for y in range(2):
                value = dot(hid_t[y], dy[:, :, cols].reshape(2 * tok, part))
                put_rows[y] = value.astype(BF16).reshape(put_rows.shape[1:])
                puts[y].start()
            for c in puts:
                c.wait()
            rs.add(items[5, k * part])
            rs.tick(1)
        some = hidden // 3
        for turn in range(2):
            who = 1 - p.half if turn == 0 else p.half

            def pull(k):
                cols = pl.ds(k * some, some)
                return [
                    local_copy(r.hidden.at[pl.ds(pl.multiple_of(who * tok, tok), tok), cols], hid.at[k % 2], 6 + 2 * (k % 2)),
                    local_copy(r.wd.at[cols], wd.at[k % 2], 7 + 2 * (k % 2)),
                ]

            start(pull(0))
            for k in range(3):
                if k < 2:
                    start(pull(k + 1))
                for c in pull(k):
                    c.wait()
                value = dot(hid[k % 2], wd[k % 2])
                out[...] = value if k == 0 else out[...] + value
            if turn == 0:
                dy[0] = out[...].astype(BF16)
                fetch(dy.at[0], r.out_to, 10)
                out_swap.start()
            else:
                fetch(out, r.out_own, 10)

    def weight_grad(a, b, into, array, k0, scale=None):
        half = width // 2

        def run(at, put):
            at[...] = a.T
            n = half // tile
            for k in range(2):
                puts = [local_copy(put.at[j], into.at[..., pl.ds(k * half + j * tile, tile)], k0 + j) for j in range(n)]
                for j in range(n):
                    c0 = k * half + j * tile
                    value = dot(at[...], b[:, c0 : c0 + tile])
                    value = value if scale is None else value * scale
                    put[j] = value.astype(BF16).reshape(panel + (tile,))
                    puts[j].start()
                for c in puts:
                    c.wait()
                rs.add(items[array, k * half])

        pl.run_scoped(run, pltpu.VMEM((width, tok), BF16), pltpu.VMEM((half // tile,) + panel + (tile,), BF16))

    gains = r.gains

    def norm_back(value, gain, grad):
        inverse = lax.rsqrt(jnp.mean(value * value, axis=-1, keepdims=True) + EPS)
        u = grad * gain
        along = jnp.sum(u * value, axis=-1, keepdims=True) / width
        return inverse * u - value * (inverse * inverse * inverse) * along, jnp.sum(grad * value * inverse, axis=0, keepdims=True)

    def phase_c(dmixed, datt, dq, dgain):
        dgain[...] = jnp.zeros_like(dgain)

        def through_ffn(mixed, dn2, got2, dy, wo):
            pulls = [
                local_copy(r.mixed, mixed, 0),
                local_copy(r.dn2_own, dn2, 1),
                local_copy(r.dy.at[p.half], dy, 2),
                local_copy(r.wo, wo, 3),
            ]
            start(pulls)
            dn2_swap.wait()
            fetch(r.dn2_got, got2, 5)
            for c in pulls:
                c.wait()
            total = jnp.zeros((1, width), F32)
            for i in range(0, tok, 128):
                rows = pl.ds(i, 128)
                d, g = norm_back(mixed[rows], gains[1:2], dn2[rows] + got2[rows].astype(F32))
                total = total + g
                d = dy[rows].astype(F32) + d
                dmixed[rows] = d
                dy[rows] = d.astype(BF16)
            dgain[1:2] = total
            for j in range(0, width, 512):
                datt[:, j : j + 512] = dot_t(dy[...], wo[j : j + 512]).astype(BF16)
            fetch(dy, r.dn2_to, 5)

        pl.run_scoped(
            through_ffn,
            f32_tok,
            f32_tok,
            bf_tok,
            bf_tok,
            pltpu.VMEM((width, width), BF16),
        )

        def through_attention(dkvw, n1, w, small, x):
            later = [local_copy(r.n1, n1, 0), local_copy(r.wq, w, 1), local_copy(r.small, small, 2), local_copy(r.x, x, 3)]
            start(later)

            def heads(q, win, dkv):
                pulls = [local_copy(r.q, q, 4), local_copy(r.window, win, 5)]
                start(pulls)
                for c in pulls:
                    c.wait()
                for m in range(batches):
                    rows = pl.ds(m * BLK, BLK)
                    dkv[...] = jnp.zeros_like(dkv)
                    for h0 in range(0, H, 3):

                        @pl.loop(h0, h0 + 3)
                        def _(h):
                            cols = pl.ds(pl.multiple_of(h * HD, HD), HD)
                            mask = window_mask(r.start[m], r.ends, nseq, m, BLK, sources * BLK)
                            k = win[m, :, :, :, :HD].reshape(sources * BLK, HD)
                            v = win[m, :, :, :, HD:].reshape(sources * BLK, HD)
                            qh, d = q[rows, cols], datt[rows, cols]
                            prob = softmax_rows(qh, k, mask)
                            dp = dot_t(d, v)
                            ds = (prob * (dp - jnp.sum(prob * dp, axis=1, keepdims=True))).astype(BF16)
                            dq[rows, cols] = dot(ds, k).astype(BF16)
                            dkv[:, :HD] += t_dot(ds, qh)
                            dkv[:, HD:] += t_dot(prob.astype(BF16), d)

                        rs.tick(1 if h0 > 0 and m == 0 else 0)
                    dkvw[m] = dkv[...].astype(BF16).reshape(dkvw.shape[1:])

            pl.run_scoped(heads, bf_tok, pltpu.VMEM(r.window.shape, BF16), pltpu.VMEM((sources * BLK, kvw), F32))
            ex1 = Exchange(p, count, xsend.at[0], xrecv.at[0], xlocal.at[0])
            ex2 = Exchange(p, count, xsend.at[1], xrecv.at[1], xlocal.at[1])

            def src1(t):
                g, c = ex1.piece(t)
                return dkvw.at[:, :, g, :, c]

            def dst1(t):
                return r.got.at[ex1.me]

            def src2(t):
                return sums.at[t]

            def dst2(t):
                g, c = ex2.piece(ex2.me)
                return dkv_own.at[:, g, :, c]

            ex1.begin(src1, dst1)
            for c in later:
                c.wait()

            def out_grad(att, dbranch):
                pulls = [local_copy(r.att, att, 4), local_copy(r.dn2_to, dbranch, 5)]
                start(pulls)
                for c in pulls:
                    c.wait()
                weight_grad(att[...], dbranch, r.g_wo, 2, 6)

            pl.run_scoped(out_grad, bf_tok, bf_tok)
            rs.tick()
            weight_grad(n1[...], dq, r.g_wq, 1, 6, HD**-0.5)
            rs.tick()

            def output(mixed, own, theirs, low):
                out_swap.wait()
                for i in range(0, tok, 256):
                    rows = pl.ds(i, 256)
                    pulls = [local_copy(r.mixed.at[rows], mixed, 8), local_copy(r.out_own.at[rows], own, 9), local_copy(r.out_got.at[rows], theirs, 10)]
                    start(pulls)
                    for c in pulls:
                        c.wait()
                    low[...] = (mixed[...] + own[...] + theirs[...].astype(F32)).astype(BF16)
                    fetch(low, r.block_out.at[rows], 11)

            some, some_low = pltpu.VMEM((256, width), F32), pltpu.VMEM((256, width), BF16)
            pl.run_scoped(output, some, some, some_low, some_low)
            rs.tick(2)

            def to_input(dn1, got):
                for j in range(0, width, 512):
                    dn1[:, j : j + 512] = dot_t(dq[...], w[j : j + 512]) * (HD**-0.5)
                ex1.end(src1, dst1)
                fetch(r.got, got, 8)

                @pl.loop(0, count)
                def _(d):
                    for m in range(batches):
                        s = jnp.zeros(sums.shape[2:], F32)
                        for i in range(sources):
                            k = m * sources + i
                            s = s + jnp.where(r.valid[d, k] > 0, got[r.index[d, k], m, i].astype(F32), 0.0)
                        sums[d, m] = s.astype(BF16)

                ex2.begin(src2, dst2)
                rs.tick(1)
                ex2.end(src2, dst2)
                dkv = dkv_own[...].reshape(tok, kvw)
                part = width // grid[0]
                for j in range(grid[0]):
                    dn1[:, j * part : (j + 1) * part] += dot_t(dkv, small[j, ..., :kvw].reshape(part, kvw))
                total = jnp.zeros((1, width), F32)
                for i in range(0, tok, 128):
                    rows = pl.ds(i, 128)
                    d, g = norm_back(x[rows].astype(F32), gains[0:1], dn1[rows])
                    total = total + g
                    x[rows] = (dmixed[rows] + d).astype(BF16)
                dgain[0:1] = total
                store = local_copy(x, r.grad_tokens, 3)
                store.start()
                for j in range(grid[0]):
                    value = t_dot(n1[:, j * part : (j + 1) * part], dkv)
                    small[j, ..., :kvw] = value.astype(BF16).reshape(panel[1:] + (kvw,))
                both = jnp.concatenate([dgain[...], jnp.zeros((120, width), F32)], axis=0)
                small[..., kvw:] = both.T.astype(BF16).reshape(panel + (128,))
                fetch(small, r.g_small, 2)
                rs.add(items[0, 0])
                rs.tick()
                store.wait()

            pl.run_scoped(to_input, f32_tok, pltpu.VMEM(r.got.shape, BF16))

        pl.run_scoped(
            through_attention,
            pltpu.VMEM((batches, sources, BLK // 16, 16, kvw), BF16),
            bf_tok,
            pltpu.VMEM((width, width), BF16),
            pltpu.VMEM(panel + (kvw + 128,), BF16),
            bf_tok,
        )

    def rest_of_it(P_rows, T_rows):
        rs.pools[ROWS] = (P_rows, T_rows)
        pl.run_scoped(
            ffn_rest,
            pair,
            pltpu.VMEM((2, hidden // 2, 2 * tok), BF16),
            pltpu.VMEM((2, 2, 2, p.Z // 2, hidden // 16, width // 3), BF16),
            pltpu.VMEM((2, tok, hidden // 3), BF16),
            pltpu.VMEM((2, hidden // 3, width), BF16),
            f32_tok,
        )
        pl.run_scoped(phase_c, f32_tok, bf_tok, bf_tok, pltpu.VMEM((8, width), F32))
        rs.finish()

    slot_rows = [u for u in units if u.kind == ROWS][0].shape(grid)
    pl.run_scoped(rest_of_it, pltpu.VMEM((3,) + slot_rows, BF16), pltpu.VMEM(slot_rows, BF16))


def backward(grid, fulls, shapes, saved, start, ends, index, valid, units, sources, kvw, collective_id):
    any_, vmem, smem = (pl.BlockSpec(memory_space=s) for s in (pl.ANY, pltpu.VMEM, pltpu.SMEM))
    sds, dma = jax.ShapeDtypeStruct, pltpu.SemaphoreType.DMA
    a, b, c, z = grid
    count = a * b * c * z
    tok, width = saved["n1"].shape
    batches = tok // BLK
    hidden = fulls[3].shape[1]
    U = len(units)
    kinds = {t.array: t.kind for t in units}
    whole = [grid[:3] + (z // 2 if kinds[i] == ROWS else z,) + s[-2:] for i, s in enumerate(shapes)]
    fulls = [fulls[0].reshape(whole[0])] + fulls[1:]
    inputs = dict(start=(start, smem), ends=(ends, smem), index=(index, smem), valid=(valid, smem))
    inputs.update({k: (v, any_) for k, v in zip(ARRAYS, fulls)})
    inputs.update({k: (v, any_) for k, v in saved.items()})
    inputs.update(gains=(saved["gains"], vmem))
    outputs = {"o_" + k: (sds(s, F32), vmem) for k, s in zip(ARRAYS, shapes)}
    low, high = (sds((tok, width), BF16), any_), (sds((tok, width), F32), any_)
    outputs.update(block_out=low, grad_tokens=low, dn2_to=low, dn2_got=low, out_to=low, out_got=low, dn2_own=high, out_own=high)
    wide = kvw * (BLK // 16) // count
    outputs.update(hidden=(sds((2 * tok, hidden), BF16), any_), hidden_t=(sds((hidden, 2 * tok), BF16), any_))
    outputs.update(got=(sds((count, batches, sources, 16, wide), BF16), any_))
    outputs.update({"g_" + k: (sds(w, BF16), any_) for k, w in zip(ARRAYS, whole)})
    names = list(inputs) + list(outputs)
    slot = (a, b, z, width // count, width // 2)
    results = pl.pallas_call(
        functools.partial(backward_kernel, grid, units, ends.shape[1], sources, kvw, names),
        out_shape=[s for s, _ in outputs.values()] + [sds(u.shape(grid), BF16) for u in units],
        in_specs=[s for _, s in inputs.values()],
        out_specs=[s for _, s in outputs.values()] + [any_] * U,
        scratch_shapes=[pltpu.VMEM(s, BF16) for u in units for s in u.link_buffers(grid)[1:]]
        + [
            pltpu.VMEM((5,) + slot, BF16),
            pltpu.VMEM(slot, BF16),
            pltpu.VMEM((count, batches, 16, wide), BF16),
            pltpu.VMEM((batches, BLK // 16, 16, kvw), BF16),
            dma((U, 8)),
            dma((U, 8)),
            dma((U, 2)),
            dma((2, count - 1)),
            dma((2, count - 1)),
            dma((2,)),
            dma((2,)),
            dma((2,)),
            dma((16,)),
        ],
        compiler_params=pltpu.CompilerParams(collective_id=collective_id, has_side_effects=True, vmem_limit_bytes=VMEM),
        name="backward",
    )(*[v for v, _ in inputs.values()])
    found = dict(zip(outputs, results))
    return found["block_out"], found["grad_tokens"], results[: len(ARRAYS)]

def holders_of(perm, block):
    count = perm.shape[1]
    same = perm[:, None, None, :] == block[..., None]
    found = jnp.max(jnp.where(same, jnp.arange(count, dtype=jnp.int32), 0), axis=-1)
    return found.transpose(1, 0, 2).reshape(count, -1)


def fast_body(grid, tokens, w_query, w_keyval, w_out, w_gate, w_up, w_down, gain_attn, gain_ffn, cotangent, block_perm, extra_len):
    batches, _, rows, width = tokens.shape
    tok = batches * rows
    me = lax.axis_index(("dp", "fsdp"))
    count = lax.axis_size(("dp", "fsdp"))
    sources = WIN // BLK + 1
    kvw = w_keyval.shape[1]
    gains = jnp.stack([gain_attn, gain_ffn], axis=1)
    small = jnp.concatenate([w_keyval, jnp.pad(gains, ((0, 0), (0, 126)))], axis=1)
    sub = w_down.shape[0]
    half = w_gate.shape[1] // 2
    shards = [small, w_query, w_out, by_parity(w_gate, sub), by_parity(w_up, sub), w_down]
    units = [Unit(i, ALL, (0, s.shape[0]), (0, s.shape[1])) for i, s in enumerate(shards[:3])]
    for k in (0, 1):
        units += [Unit(i, COLS, (0, w_gate.shape[0]), (k * half // 2, half // 2)) for i in (3, 4)]
        units += [Unit(5, ROWS, (0, sub), (k * width // 2, width // 2))]
    lags = jnp.arange(sources, dtype=jnp.int32)
    index = holders_of(block_perm, jnp.maximum(block_perm[:, :, None] - (sources - 1) + lags, 0))
    start = lax.dynamic_slice_in_dim(block_perm, me, 1, axis=1)[:, 0] * BLK
    ends = jnp.cumsum(extra_len + (WIN - 1), axis=1).astype(jnp.int32)
    x = tokens.reshape(tok, width)
    dy = cotangent.reshape(tok, width)
    fulls, dy_pair, n2_pair, n1b, query, window, att, mixed, gains = forward(grid, shards, units, x, dy, start, ends, index, sources, kvw, 0)
    block = block_perm[:, :, None] + (sources - 1) - lags
    reader = holders_of(block_perm, jnp.minimum(block, count - 1))
    valid = (block < count).astype(jnp.int32).transpose(1, 0, 2).reshape(-1, batches * sources)
    saved = dict(n2=n2_pair, dy=dy_pair, n1=n1b, q=query, window=window, att=att, mixed=mixed, x=x, gains=gains)
    back = [Unit(i, ALL, (0, s.shape[0]), (c, min(width // 2, s.shape[1] - c))) for i, s in enumerate(shards[:3]) for c in range(0, s.shape[1], width // 2)]
    for k in range(3):
        back += [Unit(i, COLS, (0, w_gate.shape[0]), (k * half // 3, half // 3)) for i in (3, 4)]
        back += [Unit(5, ROWS, (0, sub), (k * width // 3, width // 3))]
    block_out, grad_tokens, grads = backward(
        grid, fulls, [s.shape for s in shards], saved, start, ends, reader, valid, back, sources, kvw, 1
    )
    small, dq, do, dg, du, dd = grads
    dg, du = from_parity(dg, sub), from_parity(du, sub)
    return (
        block_out.reshape(tokens.shape),
        grad_tokens.reshape(tokens.shape),
        dq,
        small[:, :kvw],
        do,
        dg,
        du,
        dd,
        small[:, kvw],
        small[:, kvw + 1],
    )


def by_parity(w, sub):
    rows, hidden = w.shape
    return w.reshape(rows, -1, 2, sub).transpose(2, 0, 1, 3).reshape(2, rows, hidden // 2)


def from_parity(w, sub):
    _, rows, part = w.shape
    return w.reshape(2, rows, -1, sub).transpose(1, 2, 0, 3).reshape(rows, 2 * part)


def solution(mesh):
    count = mesh.shape["dp"] * mesh.shape["fsdp"]
    grid = (2, 2, 2, mesh.shape["fsdp"])
    whole_tiles = mesh.shape["dp"] == 8 and 1536 % (16 * count) == 0
    run = functools.partial(fast_body, grid) if whole_tiles else body
    placed = (
        P(None, ("dp", "fsdp"), None, None),
        P(("dp", "fsdp"), None),
        P(("dp", "fsdp"), None),
        P(("dp", "fsdp"), None),
        P(("dp", "fsdp"), None),
        P(("dp", "fsdp"), None),
        P(("dp", "fsdp"), None),
        P(("dp", "fsdp")),
        P(("dp", "fsdp")),
        P(None, ("dp", "fsdp"), None, None),
        P(),
        P(),
    )
    return jax.shard_map(
        run,
        mesh=mesh,
        in_specs=placed,
        out_specs=(
            P(None, ("dp", "fsdp"), None, None),
            P(None, ("dp", "fsdp"), None, None),
            P(("dp", "fsdp"), None),
            P(("dp", "fsdp"), None),
            P(("dp", "fsdp"), None),
            P(("dp", "fsdp"), None),
            P(("dp", "fsdp"), None),
            P(("dp", "fsdp"), None),
            P(("dp", "fsdp")),
            P(("dp", "fsdp")),
        ),
        check_vma=False,
    )
```

```python
import functools
import math
import types

import jax
import jax.numpy as jnp
from jax import lax
from jax.experimental import pallas as pl
from jax.experimental.pallas import tpu as pltpu
from jax.sharding import PartitionSpec as P

H = 6
HD = 256
WIN = 1024
BLK = 256


EPS = 1e-06
VMEM = 62 * 1024 * 1024


def for_sending(x):
    return jax.tree.map(lambda a: a.astype(jnp.bfloat16) if a.dtype == jnp.float32 else a, x)


def shifted(value, axis, steps):
    count = lax.axis_size(axis)
    leading, last = (max(0, -steps), min(count, count - steps))
    return lax.ppermute(value, axis, [(source, source + steps) for source in range(leading, last)])


def norm_rows(value, gain):
    inverse = lax.rsqrt(jnp.mean(value * value, axis=-1, keepdims=True) + EPS)
    return (value * inverse * gain, inverse)


def norm_back(value, inverse, gain, grad):
    scaled = grad * gain
    width = value.shape[-1]
    dvalue = (
        inverse * scaled
        - value * inverse**3 * jnp.sum(scaled * value, axis=-1, keepdims=True) / width
    )
    dgain = jnp.sum(grad * value * inverse, axis=0)
    return (dvalue, dgain)


def sequence_of(positions, ends):
    return jnp.sum((positions[:, None] >= ends[None, :]).astype(jnp.int32), axis=1)


def visible_mask(query_pos, key_pos, ends):
    same = sequence_of(query_pos, ends)[:, None] == sequence_of(key_pos, ends)[None, :]
    gap = query_pos[:, None] - key_pos[None, :]
    return same & (gap >= 0) & (gap < WIN) & (key_pos[None, :] >= 0)


def geglu(gate, up):
    return jax.nn.gelu(gate, approximate=True) * up


def move_keys(value, order, count):
    rows = value.shape[0]
    spread = lax.all_to_all(value, ("dp", "fsdp"), split_axis=1, concat_axis=0, tiled=True)
    pieces = spread.reshape(count, rows, spread.shape[1])
    placed = jnp.take(pieces, order, axis=0).reshape(count * rows, spread.shape[1])
    return lax.all_to_all(placed, ("dp", "fsdp"), split_axis=0, concat_axis=1, tiled=True)


def move_grads(value, order, count):
    rows = value.shape[0]
    spread = lax.all_to_all(
        for_sending(value), ("dp", "fsdp"), split_axis=1, concat_axis=0, tiled=True
    ).astype(value.dtype)
    pieces = spread.reshape(count, rows, spread.shape[1])
    placed = jnp.take(pieces, order, axis=0).reshape(count * rows, spread.shape[1])
    return lax.all_to_all(
        for_sending(placed), ("dp", "fsdp"), split_axis=0, concat_axis=1, tiled=True
    ).astype(placed.dtype)


def body(
    tokens,
    w_query,
    w_keyval,
    w_out,
    w_gate,
    w_up,
    w_down,
    gain_attn,
    gain_ffn,
    cotangent,
    block_perm,
    extra_len,
):
    count = lax.axis_size(("dp", "fsdp"))
    me = lax.axis_index(("dp", "fsdp"))
    batches = tokens.shape[0]
    sources = WIN // BLK + 1
    scale = HD ** (-0.5)
    shards = (w_query, w_keyval, w_out, w_gate, w_up, w_down, gain_attn, gain_ffn)
    device_ids = jnp.arange(count, dtype=jnp.int32)
    totals = None
    outputs = []
    input_grads = []
    for batch in range(batches):
        full = (
            lax.all_gather(shards[0], ("dp", "fsdp"), axis=0, tiled=True),
            lax.all_gather(shards[1], ("dp", "fsdp"), axis=0, tiled=True),
            lax.all_gather(shards[2], ("dp", "fsdp"), axis=0, tiled=True),
            lax.all_gather(shards[3], ("dp", "fsdp"), axis=0, tiled=True),
            lax.all_gather(shards[4], ("dp", "fsdp"), axis=0, tiled=True),
            lax.all_gather(shards[5], ("dp", "fsdp"), axis=0, tiled=True),
            lax.all_gather(shards[6], ("dp", "fsdp"), axis=0, tiled=True),
            lax.all_gather(shards[7], ("dp", "fsdp"), axis=0, tiled=True),
        )
        wq, wkv, wo, wg, wu, wd, g1b, g2b = full
        g1 = g1b.astype(jnp.float32)
        g2 = g2b.astype(jnp.float32)
        perm_row = block_perm[batch]
        ends = jnp.cumsum(extra_len[batch] + (WIN - 1))
        mine = lax.dynamic_slice_in_dim(perm_row, me, 1)[0]
        holder = jnp.sum(
            jnp.where(perm_row[None, :] == device_ids[:, None], device_ids[None, :], 0), axis=1
        )
        query_pos = mine * BLK + jnp.arange(BLK, dtype=jnp.int32)
        key_pos = (mine - (sources - 1)) * BLK + jnp.arange(sources * BLK, dtype=jnp.int32)
        mask = jnp.repeat(visible_mask(query_pos, key_pos, ends), H, axis=0)
        x = tokens[batch, 0].astype(jnp.float32)
        n1, r1 = norm_rows(x, g1)
        n1b = n1.astype(jnp.bfloat16)
        query = (jnp.dot(n1b, wq, preferred_element_type=jnp.float32) * scale).astype(jnp.bfloat16)
        query_rows = query.reshape(BLK * H, HD)
        keyval = jnp.dot(n1b, wkv, preferred_element_type=jnp.float32).astype(jnp.bfloat16)
        ordered = move_keys(keyval, holder, count)
        window = [ordered] * sources
        for back in range(1, sources):
            window[sources - 1 - back] = shifted(ordered, ("dp", "fsdp"), back)
        picked = move_keys(jnp.concatenate(window, axis=0), perm_row, count)
        keys_src = picked[:, :HD]
        values_src = picked[:, HD:]
        scores = jnp.einsum("qd,kd->qk", query_rows, keys_src, preferred_element_type=jnp.float32)
        masked = jnp.where(mask, scores, -1e30)
        top = jnp.max(masked, axis=1, keepdims=True)
        expd = jnp.exp(masked - top)
        rowsum = jnp.sum(expd, axis=1, keepdims=True)
        lse = top + jnp.log(rowsum)
        probs_low = (expd / rowsum).astype(jnp.bfloat16)
        att = jnp.dot(probs_low, values_src, preferred_element_type=jnp.float32)
        att_low = att.reshape(BLK, H * HD).astype(jnp.bfloat16)
        mixed = x + jnp.dot(att_low, wo, preferred_element_type=jnp.float32)
        n2, r2 = norm_rows(mixed, g2)
        n2b = n2.astype(jnp.bfloat16)
        gate = jnp.dot(n2b, wg, preferred_element_type=jnp.float32)
        up = jnp.dot(n2b, wu, preferred_element_type=jnp.float32)
        hidden = geglu(gate, up).astype(jnp.bfloat16)
        outputs.append(
            (mixed + jnp.dot(hidden, wd, preferred_element_type=jnp.float32)).astype(jnp.bfloat16)
        )
        wq, wkv, wo, wg, wu, wd, g1b, g2b = (
            lax.all_gather(shards[0], ("dp", "fsdp"), axis=0, tiled=True),
            lax.all_gather(shards[1], ("dp", "fsdp"), axis=0, tiled=True),
            lax.all_gather(shards[2], ("dp", "fsdp"), axis=0, tiled=True),
            lax.all_gather(shards[3], ("dp", "fsdp"), axis=0, tiled=True),
            lax.all_gather(shards[4], ("dp", "fsdp"), axis=0, tiled=True),
            lax.all_gather(shards[5], ("dp", "fsdp"), axis=0, tiled=True),
            lax.all_gather(shards[6], ("dp", "fsdp"), axis=0, tiled=True),
            lax.all_gather(shards[7], ("dp", "fsdp"), axis=0, tiled=True),
        )
        dy = cotangent[batch, 0]
        d_down = jnp.einsum("tf,td->fd", hidden, dy, preferred_element_type=jnp.float32)
        d_hidden = jnp.einsum("td,fd->tf", dy, wd, preferred_element_type=jnp.float32)
        _, geglu_pull = jax.vjp(geglu, gate, up)
        d_gate, d_up = geglu_pull(d_hidden)
        d_gate_low = d_gate.astype(jnp.bfloat16)
        d_up_low = d_up.astype(jnp.bfloat16)
        d_wgate = jnp.einsum("td,tf->df", n2b, d_gate_low, preferred_element_type=jnp.float32)
        d_wup = jnp.einsum("td,tf->df", n2b, d_up_low, preferred_element_type=jnp.float32)
        d_n2 = jnp.einsum("tf,df->td", d_gate_low, wg, preferred_element_type=jnp.float32)
        d_n2 = d_n2 + jnp.einsum("tf,df->td", d_up_low, wu, preferred_element_type=jnp.float32)
        d_mixed_norm, d_g2 = norm_back(mixed, r2, g2, d_n2)
        d_mixed = dy.astype(jnp.float32) + d_mixed_norm
        d_branch = d_mixed.astype(jnp.bfloat16)
        d_wout = jnp.einsum("ta,td->ad", att_low, d_branch, preferred_element_type=jnp.float32)
        d_att = jnp.einsum("td,ad->ta", d_branch, wo, preferred_element_type=jnp.float32)
        d_att_rows = d_att.astype(jnp.bfloat16).reshape(BLK * H, HD)
        again = jnp.einsum("qd,kd->qk", query_rows, keys_src, preferred_element_type=jnp.float32)
        probs = jnp.exp(jnp.where(mask, again, -1e30) - lse)
        d_probs = jnp.einsum(
            "qd,kd->qk", d_att_rows, values_src, preferred_element_type=jnp.float32
        )
        delta = jnp.sum(probs * d_probs, axis=1, keepdims=True)
        d_scores = (probs * (d_probs - delta)).astype(jnp.bfloat16)
        d_query = jnp.dot(d_scores, keys_src, preferred_element_type=jnp.float32).astype(
            jnp.bfloat16
        )
        d_query = d_query.reshape(BLK, H * HD)
        d_keys = jnp.einsum("qk,qd->kd", d_scores, query_rows, preferred_element_type=jnp.float32)
        d_values = jnp.einsum(
            "qk,qd->kd", probs.astype(jnp.bfloat16), d_att_rows, preferred_element_type=jnp.float32
        )
        d_keyval_flat = jnp.concatenate([d_keys, d_values], axis=1)
        ordered_grads = move_grads(d_keyval_flat, holder, count).reshape(sources, BLK, 2 * HD)
        summed = ordered_grads[sources - 1]
        for back in range(1, sources):
            summed = summed + shifted(
                ordered_grads[sources - 1 - back].astype(jnp.bfloat16), ("dp", "fsdp"), -back
            ).astype(jnp.float32)
        d_keyval = move_grads(summed, perm_row, count).astype(jnp.bfloat16)
        d_wquery = jnp.einsum("td,ta->da", n1b, d_query, preferred_element_type=jnp.float32) * scale
        d_wkeyval = jnp.einsum("td,tc->dc", n1b, d_keyval, preferred_element_type=jnp.float32)
        d_n1 = jnp.einsum("ta,da->td", d_query, wq, preferred_element_type=jnp.float32) * scale
        d_n1 = d_n1 + jnp.einsum("tc,dc->td", d_keyval, wkv, preferred_element_type=jnp.float32)
        d_x_norm, d_g1 = norm_back(x, r1, g1, d_n1)
        input_grads.append((d_mixed + d_x_norm).astype(jnp.bfloat16))
        local = (d_wquery, d_wkeyval, d_wout, d_wgate, d_wup, d_down, d_g1, d_g2)
        totals = local if totals is None else tuple((a + b for a, b in zip(totals, local)))
    totals = lax.psum_scatter(totals, ("dp", "fsdp"), scatter_dimension=0, tiled=True)
    block_out = jnp.stack(outputs)[:, None]
    grad_tokens = jnp.stack(input_grads)[:, None]
    return (
        block_out,
        grad_tokens,
        totals[0],
        totals[1],
        totals[2],
        totals[3],
        totals[4],
        totals[5],
        totals[6],
        totals[7],
    )


MESH = pl.DeviceIdType.MESH
BF16, F32 = jnp.bfloat16, jnp.float32
ALL, COLS, ROWS = 0, 1, 2
ARRAYS = ("small", "wq", "wo", "wg", "wu", "wd")


class Place:
    def __init__(self, grid):
        self.grid = grid
        self.Z = grid[3]
        self.count = grid[0] * grid[1] * grid[2] * grid[3]
        dp = lax.axis_index("dp")
        self.z = lax.axis_index("fsdp")
        self.c = dp % 2
        self.x = (dp // 2) % 2
        self.y = dp // 4
        self.me = dp * self.Z + self.z
        self.half = self.z % 2
        self.pair = self.z // 2
        self.core = self.dev(c=1 - self.c)
        self.xdev = self.dev(x=1 - self.x)
        self.ydev = self.dev(y=1 - self.y)
        self.mate = self.dev(z=self.z + 1 - 2 * self.half)
        self.far = self.dev(z=(self.z + 2) % self.Z)

    def dev(self, y=None, x=None, c=None, z=None):
        y = self.y if y is None else y
        x = self.x if x is None else x
        c = self.c if c is None else c
        z = self.z if z is None else z
        return ((y * 2 + x) * 2 + c, z)

    def barrier(self):
        sem = pltpu.get_barrier_semaphore()

        @pl.loop(1, self.count)
        def _(off):
            t = lax.rem(self.me + off, self.count)
            pl.semaphore_signal(sem, inc=1, device_id=(t // self.Z, t % self.Z), device_id_type=MESH)

        pl.semaphore_wait(sem, self.count - 1)


def start(copies):
    for c in copies:
        c.start()


def wait_recv(copies):
    for c in copies:
        c.wait_recv()


def wait_send(copies):
    for c in copies:
        c.wait_send()


def halves(width):
    first = width - (width // 256) * 128
    return [(0, first), (first, width - first)]


class Unit:
    def __init__(self, array, kind, rows, cols):
        self.array, self.kind, self.rows, self.cols = array, kind, rows, cols
        self.width = cols[1]

    def shape(self, grid):
        return grid[:2] + (grid[3] // 2 if self.kind == ROWS else grid[3],) + (self.rows[1], self.width)

    def link_buffers(self, grid):
        a, b, z, r, w = self.shape(grid)
        h = halves(w)
        out = [(a, b, z, r, w), (b, z, r, h[0][1]), (a, z, r, h[1][1]), (z, r, h[0][1]), (z, r, h[1][1])]
        if self.kind == ALL:
            return out + [(z - 1, r, w)]
        if self.kind == COLS:
            return out + [(z // 2, r, w), (r, w)]
        return out + [(r, w)]


class Gather:
    def __init__(self, p, unit, src, dst, send, recv, local):
        self.p, self.dst, self.send, self.recv, self.local, self.kind = p, dst, send, recv, local, unit.kind
        self.r, self.all = pl.ds(*unit.rows), pl.ds(*unit.cols)
        self.h = [pl.ds(unit.cols[0] + a, b) for a, b in halves(unit.width)]
        self.src = (lambda half: src.at[half, self.r, self.all]) if unit.kind == COLS else (lambda half: src.at[self.r, self.all])
        self.spot = p.pair if unit.kind == ROWS else p.z

    def copy(self, k, src, dst, dev):
        return pltpu.make_async_remote_copy(src, dst, self.send.at[k], self.recv.at[k], device_id=dev, device_id_type=MESH)

    def same(self, k, ref, dev):
        return self.copy(k, ref, ref, dev)

    def block(self, y, x, cols):
        return self.dst.at[y, x, self.p.c, :, self.r, cols]

    def own(self):
        p = self.p
        return pltpu.make_async_copy(self.src(p.half), self.dst.at[p.y, p.x, p.c, self.spot, self.r, self.all], self.local)

    def z1(self):
        p = self.p
        there = self.dst.at[p.y, p.x, p.c, self.spot, self.r, self.all]
        if self.kind == ALL:
            return [self.copy(i - 1, self.src(0), there, p.dev(z=(p.z + i) % p.Z)) for i in range(1, p.Z)]
        if self.kind == COLS:
            return [self.copy(0, self.src(1 - p.half), there, p.mate)]
        return [self.copy(0, self.src(0), there, p.far)]

    def z2(self):
        p = self.p
        return [self.same(1, self.dst.at[p.y, p.x, p.c, pl.ds(2 * p.pair, 2), self.r, self.all], p.far)]

    def p1(self):
        p = self.p
        return [self.same(3, self.block(p.y, p.x, self.h[0]), p.xdev), self.same(4, self.block(p.y, p.x, self.h[1]), p.ydev)]

    def p2(self):
        p, every = self.p, slice(None)
        return [self.same(5, self.block(p.y, every, self.h[0]), p.ydev), self.same(6, self.block(every, p.x, self.h[1]), p.xdev)]

    def c0(self):
        p = self.p
        return [self.same(7, self.block(p.y, p.x, self.all), p.core)]

    def c1(self):
        p = self.p
        return [self.same(8, self.block(p.y, 1 - p.x, self.h[0]), p.core), self.same(9, self.block(1 - p.y, p.x, self.h[1]), p.core)]

    def c2(self):
        p, every = self.p, slice(None)
        return [self.same(10, self.block(1 - p.y, every, self.h[0]), p.core), self.same(11, self.block(every, 1 - p.x, self.h[1]), p.core)]

    def stages(self):
        def first():
            self.own().start()
            start(self.z1())

        def second():
            self.own().wait()
            wait_recv(self.z1())
            start(self.z2())

        def third():
            if self.kind == COLS:
                wait_recv(self.z2())
            else:
                self.own().wait()
                wait_recv(self.z1())
            start(self.p1() + self.c0())

        def fourth():
            wait_recv(self.p1())
            start(self.p2() + self.c1())

        def fifth():
            wait_recv(self.p2())
            start(self.c2())

        def last():
            wait_recv(self.c0() + self.c1() + self.c2())
            wait_send(self.z1() + (self.z2() if self.kind == COLS else []) + self.p1() + self.p2() + self.c0() + self.c1() + self.c2())

        return [first] + ([second] if self.kind == COLS else []) + [third, fourth, fifth, last]


class Scatter:
    def __init__(self, p, unit, src, out, landing, rest, sems):
        self.p, self.unit, self.kind = p, unit, unit.kind
        self.src, self.out, self.landing, self.rest = src, out, landing, rest
        self.send, self.recv, self.local = sems
        self.r, self.cols = pl.ds(*unit.rows), pl.ds(*unit.cols)
        self.h = [pl.ds(a, b) for a, b in halves(unit.width)]
        self.all = pl.ds(0, unit.width)
        self.n = unit.shape(p.grid)[2]
        self.stage = 0

    def copy(self, k, src, dst, dev):
        return pltpu.make_async_remote_copy(src, dst, self.send.at[k], self.recv.at[k], device_id=dev, device_id_type=MESH)

    def r0(self):
        p = self.p
        return [self.copy(0, self.src.at[:, :, 1 - p.c, :, self.r, self.cols], self.landing, p.core)]

    def loads(self):
        own = self.src.at[:, :, self.p.c, :, self.r, self.cols]
        return [
            pltpu.make_async_copy(self.landing, self.P.at[..., self.all], self.local.at[0]),
            pltpu.make_async_copy(own, self.T.at[..., self.all], self.local.at[1]),
        ]

    def r1(self):
        p, P = self.p, self.P
        return [self.copy(1, P.at[1 - p.y, :, :, :, self.h[0]], self.rest[0], p.ydev), self.copy(2, P.at[:, 1 - p.x, :, :, self.h[1]], self.rest[1], p.xdev)]

    def r2(self):
        p, P = self.p, self.P
        return [self.copy(3, P.at[p.y, 1 - p.x, :, :, self.h[0]], self.rest[2], p.xdev), self.copy(4, P.at[1 - p.y, p.x, :, :, self.h[1]], self.rest[3], p.ydev)]

    def r3(self):
        p, P = self.p, self.P
        if self.kind == ALL:
            return [self.copy(4 + i, P.at[p.y, p.x, (p.z + i) % p.Z, :, self.all], self.rest[4].at[i - 1], p.dev(z=(p.z + i) % p.Z)) for i in range(1, p.Z)]
        if self.kind == COLS:
            return [self.copy(5, P.at[p.y, p.x, pl.ds(2 * (1 - p.pair), 2), :, self.all], self.rest[4], p.far)]
        return [self.copy(5, P.at[p.y, p.x, 1 - p.pair, :, self.all], self.rest[4], p.far)]

    def r4(self):
        p = self.p
        return [self.copy(6, self.P.at[p.y, p.x, 2 * p.pair + 1 - p.half, :, self.all], self.rest[5], p.mate)]

    def add0(self):
        P, T, b, n = self.P, self.T, self.P.shape[1], self.n

        @pl.loop(0, P.shape[0] * b * n)
        def _(i):
            at = (i // (b * n), (i // n) % b, i % n, slice(None), self.all)
            P[at] = P[at] + T[at]

    def add1(self):
        p, P, n = self.p, self.P, self.n

        @pl.loop(0, 2 * n)
        def _(i):
            b, d = i // n, i % n
            P[p.y, b, d, :, self.h[0]] = P[p.y, b, d, :, self.h[0]] + self.rest[0][b, d]
            P[b, p.x, d, :, self.h[1]] = P[b, p.x, d, :, self.h[1]] + self.rest[1][b, d]

    def add2(self):
        p, P = self.p, self.P

        @pl.loop(0, self.n)
        def _(d):
            for k in (0, 1):
                P[p.y, p.x, d, :, self.h[k]] = P[p.y, p.x, d, :, self.h[k]] + self.rest[2 + k][d]

    def add3(self):
        p, got = self.p, self.rest[4]
        mine = lambda d: self.P[p.y, p.x, d, :, self.all].astype(F32)
        if self.kind == ALL:
            s = mine(p.z)
            for i in range(p.Z - 1):
                s = s + got[i].astype(F32)
            self.out[self.r, self.cols] = s
        elif self.kind == ROWS:
            self.out[self.r, self.cols] = mine(p.pair) + got[...].astype(F32)
        else:
            theirs = 2 * p.pair + 1 - p.half
            self.out[p.half, self.r, self.cols] = mine(p.z) + got[p.half].astype(F32)
            self.P[p.y, p.x, theirs, :, self.all] = (mine(theirs) + got[1 - p.half].astype(F32)).astype(BF16)

    def first(self):
        start(self.r0())

    @property
    def P(self):
        return self.pool.at[self.slot]

    def admit(self, pool, slot, T):
        self.pool, self.slot, self.T = pool, slot, T
        wait_recv(self.r0())
        start(self.loads())

    def settle(self):
        for c in self.loads():
            c.wait()
        self.add0()
        start(self.r1())

    def next(self):
        k, self.stage = self.stage, self.stage + 1
        if k == 0:
            wait_recv(self.r1())
            wait_send(self.r1())
            self.add1()
            start(self.r2())
        elif k == 1:
            wait_recv(self.r2())
            wait_send(self.r2())
            self.add2()
            start(self.r3())
        elif k == 2:
            wait_recv(self.r3())
            wait_send(self.r3() + self.r0())
            self.add3()
            if self.kind == COLS:
                start(self.r4())
        else:
            wait_recv(self.r4())
            wait_send(self.r4())
            self.out[1 - self.p.half, self.r, self.cols] = self.rest[5][...].astype(F32)
        return self.stage < (4 if self.kind == COLS else 3)


class Sums:
    def __init__(self, pools):
        self.pools, self.used = pools, {k: 0 for k in pools}
        self.queue, self.under_way = [], []

    def add(self, item):
        item.first()
        self.queue.append(item)

    def tick(self, count=1):
        for _ in range(count):
            new = self.queue.pop(0) if self.queue else None
            if new is not None:
                key = ROWS if new.kind == ROWS else ALL
                P, T = self.pools[key]
                new.admit(P, self.used[key] % P.shape[0], T)
                self.used[key] += 1
            self.under_way = [i for i in self.under_way if i.next()]
            if new is not None:
                new.settle()
                self.under_way.append(new)

    def finish(self):
        while self.queue or self.under_way:
            self.tick()


def staggered(items, starts=None):
    lists = [i.stages() for i in items]
    starts = starts or list(range(len(items)))
    steps = []
    for s in range(max(b + len(l) for b, l in zip(starts, lists))):
        for u in reversed(range(len(lists))):
            k = s - starts[u]
            if 0 <= k < len(lists[u]):
                steps.append((u, k == len(lists[u]) - 1, lists[u][k]))
    return steps


class Steps:
    def __init__(self, steps):
        self.steps, self.at = steps, 0

    def advance(self, count=1):
        for _ in range(count):
            if self.at < len(self.steps):
                self.steps[self.at][2]()
                self.at += 1

    def through(self, item):
        mark = [k for k, (u, done, _) in enumerate(self.steps) if u == item and done][0]
        self.advance(mark + 1 - self.at)

    def finish(self):
        self.advance(len(self.steps) - self.at)

def window_mask(start, ends, nseq, m, queries, keys):
    qpos = start + lax.broadcasted_iota(jnp.int32, (queries, 1), 0)
    first = jnp.maximum(qpos - (WIN - 1), 0)
    for k in range(nseq):
        end = ends[m, k]
        first = jnp.maximum(first, jnp.where(qpos >= end, end, 0))
    kpos = start - (keys - queries) + lax.broadcasted_iota(jnp.int32, (1, keys), 1)
    return (kpos >= first) & (kpos <= qpos)


def softmax_rows(q, k, mask):
    scores = lax.dot_general(q, k, (((1,), (1,)), ((), ())), preferred_element_type=jnp.float32)
    masked = jnp.where(mask, scores, -1e30)
    expd = jnp.exp(masked - jnp.max(masked, axis=1, keepdims=True))
    return expd * (1.0 / jnp.sum(expd, axis=1, keepdims=True))


def geglu_parts(gate):
    c = math.sqrt(2.0 / math.pi)
    square = gate * gate
    t = jnp.tanh(c * gate * (1.0 + 0.044715 * square))
    half = 0.5 * (1.0 + t)
    value = gate * half
    slope = half + 0.5 * gate * (1.0 - t * t) * c * (1.0 + 3 * 0.044715 * square)
    return value, slope


class Exchange:
    def __init__(self, p, count, send, recv, local):
        self.count, self.send, self.recv, self.local = count, send, recv, local
        self.me = p.me
        self.Z = p.Z
        self.groups = BLK // 16
        self.wide = 2 * HD * self.groups // count

    def piece(self, d):
        return d % self.groups, pl.ds(pl.multiple_of((d // self.groups) * self.wide, self.wide), self.wide)

    def dev(self, d):
        return (d // self.Z, d % self.Z)

    def copy(self, off, src, dst):
        t = lax.rem(self.me + off, self.count)
        return pltpu.make_async_remote_copy(
            src(t), dst(t), self.send.at[off - 1], self.recv.at[off - 1], device_id=self.dev(t), device_id_type=MESH
        )

    def begin(self, src, dst):
        @pl.loop(1, self.count)
        def _(off):
            self.copy(off, src, dst).start()

        pltpu.make_async_copy(src(self.me), dst(self.me), self.local).start()

    def end(self, src, dst):
        pltpu.make_async_copy(src(self.me), dst(self.me), self.local).wait()

        @pl.loop(1, self.count)
        def _(off):
            self.copy(off, src, dst).wait()


def forward_kernel(grid, units, nseq, sources, kvw, *refs):
    f32, bf16 = jnp.float32, jnp.bfloat16
    n = 6
    start_ref, ends_ref, index_ref, x_ref, dy_ref = refs[:5]
    ins, refs = refs[5 : 5 + n], refs[5 + n :]
    fulls, refs = refs[:n], refs[n:]
    dyx_ref, n2x_ref, refs = *refs[:2], refs[2:]
    n1_ref, q_ref, win_ref, att_ref, mixed_ref, gains_ref, refs = *refs[:6], refs[6:]
    n2, wbuf, small, kv, got, picked, send, recv, local, xsend, xrecv, xlocal, lsem, msend, mrecv = refs
    p = Place(grid)
    count = p.count
    tok, width = x_ref.shape
    batches = tok // BLK
    p.barrier()
    items = [Gather(p, t, ins[t.array], fulls[t.array], send.at[u], recv.at[u], local.at[u]) for u, t in enumerate(units)]
    steps = Steps(staggered(items, [0] + list(range(2, len(items) + 1))))
    advance, through = steps.advance, steps.through

    def load(i, dst, sem):
        return pltpu.make_async_copy(fulls[i], dst, lsem.at[sem])

    def to_mate(k, src, dst):
        return (
            pltpu.make_async_copy(src, dst, lsem.at[3 + k]),
            pltpu.make_async_remote_copy(src, dst, msend.at[k], mrecv.at[k], device_id=p.mate, device_id_type=MESH),
        )

    advance(1)
    shared = [to_mate(0, dy_ref, dyx_ref.at[p.half])]
    start(shared[0])
    x = x_ref[...].astype(f32)
    mixed_ref[...] = x * lax.rsqrt(jnp.mean(x * x, axis=-1, keepdims=True) + EPS)
    through(0)
    load(0, small, 0).start()
    load(0, small, 0).wait()
    gains = small[..., kvw:].reshape(width, 128).astype(f32).T
    gains_ref[...] = gains[:8]
    n1_ref[...] = (mixed_ref[...] * gains[0:1]).astype(bf16)
    ex1 = Exchange(p, count, xsend.at[0], xrecv.at[0], xlocal.at[0])
    ex2 = Exchange(p, count, xsend.at[1], xrecv.at[1], xlocal.at[1])

    kv_value = jnp.dot(n1_ref[...], small[..., :kvw].reshape(width, kvw), preferred_element_type=f32).astype(bf16)
    kv[...] = kv_value.reshape(kv.shape)

    def src1(t):
        g, c = ex1.piece(t)
        return kv.at[:, g, :, c]

    def dst1(t):
        return got.at[ex1.me]

    def src2(t):
        return picked.at[t]

    def dst2(t):
        g, c = ex2.piece(ex2.me)
        return win_ref.at[:, :, g, :, c]

    ex1.begin(src1, dst1)
    advance(6)
    ex1.end(src1, dst1)

    @pl.loop(0, count)
    def _(t):
        for m in range(batches):
            for i in range(sources):
                picked[t, m, i] = got[index_ref[t, m * sources + i], m]

    ex2.begin(src2, dst2)
    through(1)
    load(1, wbuf, 1).start()
    advance(2)
    load(1, wbuf, 1).wait()
    tile = 512
    for j in range(0, width, tile):
        w = wbuf[..., j : j + tile].reshape(width, tile)
        q_ref[:, j : j + tile] = (jnp.dot(n1_ref[...], w, preferred_element_type=f32) * (HD**-0.5)).astype(bf16)
        advance()
    through(2)
    load(2, wbuf, 2).start()
    advance(0)
    ex2.end(src2, dst2)
    load(2, wbuf, 2).wait()
    for m in range(batches):
        rows = pl.ds(m * BLK, BLK)
        for h0 in range(0, H, 2):

            @pl.loop(h0, h0 + 2)
            def _(h):
                cols = pl.ds(pl.multiple_of(h * HD, HD), HD)
                mask = window_mask(start_ref[m], ends_ref, nseq, m, BLK, sources * BLK)
                k = win_ref[m, :, :, :, :HD].reshape(sources * BLK, HD)
                v = win_ref[m, :, :, :, HD:].reshape(sources * BLK, HD)
                prob = softmax_rows(q_ref[rows, cols], k, mask)
                att_ref[rows, cols] = jnp.dot(prob.astype(bf16), v, preferred_element_type=f32).astype(bf16)

            advance()
        for j in range(0, width, tile):
            w = wbuf[..., j : j + tile].reshape(width, tile)
            mixed_ref[rows, j : j + tile] = x_ref[rows, j : j + tile].astype(f32) + jnp.dot(att_ref[rows], w, preferred_element_type=f32)
        mixed = mixed_ref[rows]
        inverse = lax.rsqrt(jnp.mean(mixed * mixed, axis=-1, keepdims=True) + EPS)
        n2[rows] = (mixed * inverse * gains_ref[1:2]).astype(bf16)
        shared.append(to_mate(1 + m, n2.at[rows], n2x_ref.at[p.half, rows]))
        start(shared[-1])
        advance(2)
    steps.finish()
    for copies in shared:
        for c in copies:
            c.wait()


def forward(grid, shards, units, x, dy, start, ends, index, sources, kvw, collective_id):
    a, b, c, z = grid
    count = a * b * c * z
    tok, width = x.shape
    batches = tok // BLK
    bf16 = jnp.bfloat16
    groups = BLK // 16
    wide = 2 * HD * groups // count
    rows = shards[1].shape[0]
    U = len(units)
    any_, vmem, smem = (pl.BlockSpec(memory_space=s) for s in (pl.ANY, pltpu.VMEM, pltpu.SMEM))
    dma = pltpu.SemaphoreType.DMA
    sds = jax.ShapeDtypeStruct
    kinds = {t.array: t.kind for t in units}
    whole = [tuple(grid[:3]) + (z // 2 if kinds[i] == ROWS else z,) + s.shape[-2:] for i, s in enumerate(shards)]
    outs = pl.pallas_call(
        functools.partial(forward_kernel, grid, units, ends.shape[1], sources, kvw),
        out_shape=[sds(w, bf16) for w in whole]
        + [sds((2, tok, width), bf16)] * 2
        + [
            sds((tok, width), bf16),
            sds((tok, width), bf16),
            sds((batches, sources, groups, 16, 2 * HD), bf16),
            sds((tok, width), bf16),
            sds((tok, width), jnp.float32),
            sds((8, width), jnp.float32),
        ],
        in_specs=[smem, smem, smem, vmem, any_] + [any_] * 6,
        out_specs=[any_] * 8 + [vmem] * 6,
        scratch_shapes=[
            pltpu.VMEM((tok, width), bf16),
            pltpu.VMEM(tuple(grid) + (rows, width), bf16),
            pltpu.VMEM(tuple(grid) + (rows, shards[0].shape[1]), bf16),
            pltpu.VMEM((batches, groups, 16, 2 * HD), bf16),
            pltpu.VMEM((count, batches, 16, wide), bf16),
            pltpu.VMEM((count, batches, sources, 16, wide), bf16),
            dma((U, 12)),
            dma((U, 12)),
            dma((U,)),
            dma((2, count - 1)),
            dma((2, count - 1)),
            dma((2,)),
            dma((4 + batches,)),
            dma((1 + batches,)),
            dma((1 + batches,)),
        ],
        compiler_params=pltpu.CompilerParams(collective_id=collective_id, has_side_effects=True, vmem_limit_bytes=VMEM),
        name="forward",
    )(start, ends, index, x, dy, *shards)
    fulls = [o.reshape(-1, s.shape[-1]) for o, s in zip(outs, shards)]
    dy_pair, n2_pair, n1, q, window, att, mixed, gains = outs[6:]
    return fulls, dy_pair, n2_pair, n1, q, window, att, mixed, gains


def backward_kernel(grid, units, nseq, sources, kvw, names, *refs):
    r = types.SimpleNamespace(**dict(zip(names, refs)))
    rest = list(refs[len(names) :])
    p = Place(grid)
    count = p.count
    landings = [rest.pop(0) for _ in units]
    parts = [[rest.pop(0) for _ in u.link_buffers(grid)[1:]] for u in units]
    P_all, T_all, sums, dkv_own, send, recv, local, xsend, xrecv, xlocal, msend, mrecv, sem = rest
    tok, width = r.n1.shape
    batches = tok // BLK
    hidden = r.wg.shape[1]
    grads = [r.g_small, r.g_wq, r.g_wo, r.g_wg, r.g_wu, r.g_wd]
    outs = [r.o_small, r.o_wq, r.o_wo, r.o_wg, r.o_wu, r.o_wd]
    items = {}
    for u, unit in enumerate(units):
        items[unit.array, unit.cols[0]] = Scatter(
            p, unit, grads[unit.array], outs[unit.array], landings[u], parts[u], (send.at[u], recv.at[u], local.at[u])
        )
    rs = Sums({ALL: (P_all, T_all), ROWS: None})
    p.barrier()
    dot = functools.partial(jnp.dot, preferred_element_type=F32)

    def dot_t(a, b):
        return lax.dot_general(a, b, (((1,), (1,)), ((), ())), preferred_element_type=F32)

    def t_dot(a, b):
        return lax.dot_general(a, b, (((0,), (0,)), ((), ())), preferred_element_type=F32)

    def local_copy(src, dst, k):
        return pltpu.make_async_copy(src, dst, sem.at[k])

    def fetch(src, dst, k):
        c = local_copy(src, dst, k)
        c.start()
        c.wait()

    def to_mate(k, src, dst):
        return pltpu.make_async_remote_copy(src, dst, msend.at[k], mrecv.at[k], device_id=p.mate, device_id_type=MESH)

    dn2_swap = to_mate(0, r.dn2_to, r.dn2_got)
    out_swap = to_mate(1, r.out_to, r.out_got)
    tile = 256
    tiles = hidden // tile
    third = tiles // 3
    f32_tok, bf_tok = pltpu.VMEM((tok, width), F32), pltpu.VMEM((tok, width), BF16)
    panel = grid + (width // count,)

    def ffn(n2, n2t, dy, dn2, wg, wu, wd, put_g, put_u, hid, hid_t):
        def weights(i, slot):
            cols = pl.ds(i * tile, tile)
            return [
                local_copy(r.wg.at[:, cols], wg.at[slot], 3 * slot),
                local_copy(r.wu.at[:, cols], wu.at[slot], 3 * slot + 1),
                local_copy(r.wd.at[cols], wd.at[slot], 3 * slot + 2),
            ]

        def results(i, slot):
            cols = pl.ds(i * tile, tile)
            return [
                local_copy(put_g.at[slot], r.g_wg.at[..., cols], 6 + 4 * slot),
                local_copy(put_u.at[slot], r.g_wu.at[..., cols], 7 + 4 * slot),
                local_copy(hid.at[slot], r.hidden.at[:, cols], 8 + 4 * slot),
                local_copy(hid_t.at[slot], r.hidden_t.at[cols], 9 + 4 * slot),
            ]

        start(weights(0, 0))
        first = [local_copy(r.n2, n2, 14), local_copy(r.dy, dy, 15)]
        start(first)
        dn2[...] = jnp.zeros_like(dn2)
        for c in first:
            c.wait()
        for k in range(2):
            n2t[:, k * tok : (k + 1) * tok] = n2[k].T
        def step(i, slot, ahead, behind):
            if ahead is not None:
                start(weights(ahead, 1 - slot))
            for c in weights(i, slot):
                c.wait()
            if behind is not None:
                for c in results(behind, slot):
                    c.wait()
            rows = n2[...].reshape(2 * tok, width)
            gate = dot(rows, wg[slot])
            up = dot(rows, wu[slot])
            value, slope = geglu_parts(gate)
            low = (value * up).astype(BF16)
            hid[slot] = low
            hid_t[slot] = low.T
            dh = dot_t(dy[...].reshape(2 * tok, width), wd[slot])
            dg = (dh * up * slope).astype(BF16)
            du = (dh * value).astype(BF16)
            back = dot_t(dg, wg[slot]) + dot_t(du, wu[slot])
            dn2[...] += back.reshape(dn2.shape)
            put_g[slot] = dot(n2t[...], dg).astype(BF16).reshape(panel + (tile,))
            put_u[slot] = dot(n2t[...], du).astype(BF16).reshape(panel + (tile,))
            start(results(i, slot))

        for i in range(tiles):
            done = i % third == third - 1
            step(i, i % 2, i + 1 if i + 1 < tiles else None, i - 2 if i % third >= 2 else None)
            if done:
                for j in (i - 1, i):
                    for c in results(j, j % 2):
                        c.wait()
                rs.add(items[3, (i + 1 - third) * tile])
                rs.add(items[4, (i + 1 - third) * tile])
            if i >= third - 1:
                rs.tick(1)
        n2[0] = dn2[1 - p.half].astype(BF16)
        fetch(n2.at[0], r.dn2_to, 14)
        dn2_swap.start()
        fetch(dn2.at[p.half], r.dn2_own, 14)

    pair = pltpu.VMEM((2, tok, width), BF16)
    pl.run_scoped(
        ffn,
        pair,
        pltpu.VMEM((width, 2 * tok), BF16),
        pair,
        pltpu.VMEM((2, tok, width), F32),
        pltpu.VMEM((2, width, tile), BF16),
        pltpu.VMEM((2, width, tile), BF16),
        pltpu.VMEM((2, tile, width), BF16),
        pltpu.VMEM((2,) + panel + (tile,), BF16),
        pltpu.VMEM((2,) + panel + (tile,), BF16),
        pltpu.VMEM((2, 2 * tok, tile), BF16),
        pltpu.VMEM((2, tile, 2 * tok), BF16),
    )

    def ffn_rest(dy, hid_t, put_rows, hid, wd, out):
        rows, part = hidden // 2, width // 3
        pulls = [local_copy(r.dy, dy, 0)] + [local_copy(r.hidden_t.at[pl.ds(y * rows, rows)], hid_t.at[y], 1 + y) for y in range(2)]
        start(pulls)
        for c in pulls:
            c.wait()
        for k in range(3):
            cols = pl.ds(k * part, part)
            puts = [local_copy(put_rows.at[y], r.g_wd.at[y, :, :, :, :, cols], 4 + y) for y in range(2)]
            for y in range(2):
                value = dot(hid_t[y], dy[:, :, cols].reshape(2 * tok, part))
                put_rows[y] = value.astype(BF16).reshape(put_rows.shape[1:])
                puts[y].start()
            for c in puts:
                c.wait()
            rs.add(items[5, k * part])
            rs.tick(1)
        some = hidden // 3
        for turn in range(2):
            who = 1 - p.half if turn == 0 else p.half

            def pull(k):
                cols = pl.ds(k * some, some)
                return [
                    local_copy(r.hidden.at[pl.ds(pl.multiple_of(who * tok, tok), tok), cols], hid.at[k % 2], 6 + 2 * (k % 2)),
                    local_copy(r.wd.at[cols], wd.at[k % 2], 7 + 2 * (k % 2)),
                ]

            start(pull(0))
            for k in range(3):
                if k < 2:
                    start(pull(k + 1))
                for c in pull(k):
                    c.wait()
                value = dot(hid[k % 2], wd[k % 2])
                out[...] = value if k == 0 else out[...] + value
            if turn == 0:
                dy[0] = out[...].astype(BF16)
                fetch(dy.at[0], r.out_to, 10)
                out_swap.start()
            else:
                fetch(out, r.out_own, 10)

    def weight_grad(a, b, into, array, k0, scale=None):
        half = width // 2

        def run(at, put):
            at[...] = a.T
            n = half // tile
            for k in range(2):
                puts = [local_copy(put.at[j], into.at[..., pl.ds(k * half + j * tile, tile)], k0 + j) for j in range(n)]
                for j in range(n):
                    c0 = k * half + j * tile
                    value = dot(at[...], b[:, c0 : c0 + tile])
                    value = value if scale is None else value * scale
                    put[j] = value.astype(BF16).reshape(panel + (tile,))
                    puts[j].start()
                for c in puts:
                    c.wait()
                rs.add(items[array, k * half])

        pl.run_scoped(run, pltpu.VMEM((width, tok), BF16), pltpu.VMEM((half // tile,) + panel + (tile,), BF16))

    gains = r.gains

    def norm_back(value, gain, grad):
        inverse = lax.rsqrt(jnp.mean(value * value, axis=-1, keepdims=True) + EPS)
        u = grad * gain
        along = jnp.sum(u * value, axis=-1, keepdims=True) / width
        return inverse * u - value * (inverse * inverse * inverse) * along, jnp.sum(grad * value * inverse, axis=0, keepdims=True)

    def phase_c(dmixed, datt, dq, dgain):
        dgain[...] = jnp.zeros_like(dgain)

        def through_ffn(mixed, dn2, got2, dy, wo):
            pulls = [
                local_copy(r.mixed, mixed, 0),
                local_copy(r.dn2_own, dn2, 1),
                local_copy(r.dy.at[p.half], dy, 2),
                local_copy(r.wo, wo, 3),
            ]
            start(pulls)
            dn2_swap.wait()
            fetch(r.dn2_got, got2, 5)
            for c in pulls:
                c.wait()
            total = jnp.zeros((1, width), F32)
            for i in range(0, tok, 128):
                rows = pl.ds(i, 128)
                d, g = norm_back(mixed[rows], gains[1:2], dn2[rows] + got2[rows].astype(F32))
                total = total + g
                d = dy[rows].astype(F32) + d
                dmixed[rows] = d
                dy[rows] = d.astype(BF16)
            dgain[1:2] = total
            for j in range(0, width, 512):
                datt[:, j : j + 512] = dot_t(dy[...], wo[j : j + 512]).astype(BF16)
            fetch(dy, r.dn2_to, 5)

        pl.run_scoped(
            through_ffn,
            f32_tok,
            f32_tok,
            bf_tok,
            bf_tok,
            pltpu.VMEM((width, width), BF16),
        )

        def through_attention(dkvw, n1, w, small, x):
            later = [local_copy(r.n1, n1, 0), local_copy(r.wq, w, 1), local_copy(r.small, small, 2), local_copy(r.x, x, 3)]
            start(later)

            def heads(q, win, dkv):
                pulls = [local_copy(r.q, q, 4), local_copy(r.window, win, 5)]
                start(pulls)
                for c in pulls:
                    c.wait()
                for m in range(batches):
                    rows = pl.ds(m * BLK, BLK)
                    dkv[...] = jnp.zeros_like(dkv)
                    for h0 in range(0, H, 3):

                        @pl.loop(h0, h0 + 3)
                        def _(h):
                            cols = pl.ds(pl.multiple_of(h * HD, HD), HD)
                            mask = window_mask(r.start[m], r.ends, nseq, m, BLK, sources * BLK)
                            k = win[m, :, :, :, :HD].reshape(sources * BLK, HD)
                            v = win[m, :, :, :, HD:].reshape(sources * BLK, HD)
                            qh, d = q[rows, cols], datt[rows, cols]
                            prob = softmax_rows(qh, k, mask)
                            dp = dot_t(d, v)
                            ds = (prob * (dp - jnp.sum(prob * dp, axis=1, keepdims=True))).astype(BF16)
                            dq[rows, cols] = dot(ds, k).astype(BF16)
                            dkv[:, :HD] += t_dot(ds, qh)
                            dkv[:, HD:] += t_dot(prob.astype(BF16), d)

                        rs.tick(1 if h0 > 0 and m == 0 else 0)
                    dkvw[m] = dkv[...].astype(BF16).reshape(dkvw.shape[1:])

            pl.run_scoped(heads, bf_tok, pltpu.VMEM(r.window.shape, BF16), pltpu.VMEM((sources * BLK, kvw), F32))
            ex1 = Exchange(p, count, xsend.at[0], xrecv.at[0], xlocal.at[0])
            ex2 = Exchange(p, count, xsend.at[1], xrecv.at[1], xlocal.at[1])

            def src1(t):
                g, c = ex1.piece(t)
                return dkvw.at[:, :, g, :, c]

            def dst1(t):
                return r.got.at[ex1.me]

            def src2(t):
                return sums.at[t]

            def dst2(t):
                g, c = ex2.piece(ex2.me)
                return dkv_own.at[:, g, :, c]

            ex1.begin(src1, dst1)
            for c in later:
                c.wait()

            def out_grad(att, dbranch):
                pulls = [local_copy(r.att, att, 4), local_copy(r.dn2_to, dbranch, 5)]
                start(pulls)
                for c in pulls:
                    c.wait()
                weight_grad(att[...], dbranch, r.g_wo, 2, 6)

            pl.run_scoped(out_grad, bf_tok, bf_tok)
            rs.tick()
            weight_grad(n1[...], dq, r.g_wq, 1, 6, HD**-0.5)
            rs.tick()

            def output(mixed, own, theirs, low):
                out_swap.wait()
                for i in range(0, tok, 256):
                    rows = pl.ds(i, 256)
                    pulls = [local_copy(r.mixed.at[rows], mixed, 8), local_copy(r.out_own.at[rows], own, 9), local_copy(r.out_got.at[rows], theirs, 10)]
                    start(pulls)
                    for c in pulls:
                        c.wait()
                    low[...] = (mixed[...] + own[...] + theirs[...].astype(F32)).astype(BF16)
                    fetch(low, r.block_out.at[rows], 11)

            some, some_low = pltpu.VMEM((256, width), F32), pltpu.VMEM((256, width), BF16)
            pl.run_scoped(output, some, some, some_low, some_low)
            rs.tick(0)

            def to_input(dn1, got):
                for j in range(0, width, 512):
                    dn1[:, j : j + 512] = dot_t(dq[...], w[j : j + 512]) * (HD**-0.5)
                ex1.end(src1, dst1)
                fetch(r.got, got, 8)

                @pl.loop(0, count)
                def _(d):
                    for m in range(batches):
                        s = jnp.zeros(sums.shape[2:], F32)
                        for i in range(sources):
                            k = m * sources + i
                            s = s + jnp.where(r.valid[d, k] > 0, got[r.index[d, k], m, i].astype(F32), 0.0)
                        sums[d, m] = s.astype(BF16)

                ex2.begin(src2, dst2)
                rs.tick(1)
                ex2.end(src2, dst2)
                dkv = dkv_own[...].reshape(tok, kvw)
                part = width // grid[0]
                for j in range(grid[0]):
                    dn1[:, j * part : (j + 1) * part] += dot_t(dkv, small[j, ..., :kvw].reshape(part, kvw))
                total = jnp.zeros((1, width), F32)
                for i in range(0, tok, 128):
                    rows = pl.ds(i, 128)
                    d, g = norm_back(x[rows].astype(F32), gains[0:1], dn1[rows])
                    total = total + g
                    x[rows] = (dmixed[rows] + d).astype(BF16)
                dgain[0:1] = total
                store = local_copy(x, r.grad_tokens, 3)
                store.start()
                for j in range(grid[0]):
                    value = t_dot(n1[:, j * part : (j + 1) * part], dkv)
                    small[j, ..., :kvw] = value.astype(BF16).reshape(panel[1:] + (kvw,))
                both = jnp.concatenate([dgain[...], jnp.zeros((120, width), F32)], axis=0)
                small[..., kvw:] = both.T.astype(BF16).reshape(panel + (128,))
                fetch(small, r.g_small, 2)
                rs.add(items[0, 0])
                rs.tick()
                store.wait()

            pl.run_scoped(to_input, f32_tok, pltpu.VMEM(r.got.shape, BF16))

        pl.run_scoped(
            through_attention,
            pltpu.VMEM((batches, sources, BLK // 16, 16, kvw), BF16),
            bf_tok,
            pltpu.VMEM((width, width), BF16),
            pltpu.VMEM(panel + (kvw + 128,), BF16),
            bf_tok,
        )

    def rest_of_it(P_rows, T_rows):
        rs.pools[ROWS] = (P_rows, T_rows)
        pl.run_scoped(
            ffn_rest,
            pair,
            pltpu.VMEM((2, hidden // 2, 2 * tok), BF16),
            pltpu.VMEM((2, 2, 2, p.Z // 2, hidden // 16, width // 3), BF16),
            pltpu.VMEM((2, tok, hidden // 3), BF16),
            pltpu.VMEM((2, hidden // 3, width), BF16),
            f32_tok,
        )
        pl.run_scoped(phase_c, f32_tok, bf_tok, bf_tok, pltpu.VMEM((8, width), F32))
        rs.finish()

    slot_rows = [u for u in units if u.kind == ROWS][0].shape(grid)
    pl.run_scoped(rest_of_it, pltpu.VMEM((3,) + slot_rows, BF16), pltpu.VMEM(slot_rows, BF16))


def backward(grid, fulls, shapes, saved, start, ends, index, valid, units, sources, kvw, collective_id):
    any_, vmem, smem = (pl.BlockSpec(memory_space=s) for s in (pl.ANY, pltpu.VMEM, pltpu.SMEM))
    sds, dma = jax.ShapeDtypeStruct, pltpu.SemaphoreType.DMA
    a, b, c, z = grid
    count = a * b * c * z
    tok, width = saved["n1"].shape
    batches = tok // BLK
    hidden = fulls[3].shape[1]
    U = len(units)
    kinds = {t.array: t.kind for t in units}
    whole = [grid[:3] + (z // 2 if kinds[i] == ROWS else z,) + s[-2:] for i, s in enumerate(shapes)]
    fulls = [fulls[0].reshape(whole[0])] + fulls[1:]
    inputs = dict(start=(start, smem), ends=(ends, smem), index=(index, smem), valid=(valid, smem))
    inputs.update({k: (v, any_) for k, v in zip(ARRAYS, fulls)})
    inputs.update({k: (v, any_) for k, v in saved.items()})
    inputs.update(gains=(saved["gains"], vmem))
    outputs = {"o_" + k: (sds(s, F32), vmem) for k, s in zip(ARRAYS, shapes)}
    low, high = (sds((tok, width), BF16), any_), (sds((tok, width), F32), any_)
    outputs.update(block_out=low, grad_tokens=low, dn2_to=low, dn2_got=low, out_to=low, out_got=low, dn2_own=high, out_own=high)
    wide = kvw * (BLK // 16) // count
    outputs.update(hidden=(sds((2 * tok, hidden), BF16), any_), hidden_t=(sds((hidden, 2 * tok), BF16), any_))
    outputs.update(got=(sds((count, batches, sources, 16, wide), BF16), any_))
    outputs.update({"g_" + k: (sds(w, BF16), any_) for k, w in zip(ARRAYS, whole)})
    names = list(inputs) + list(outputs)
    slot = (a, b, z, width // count, width // 2)
    results = pl.pallas_call(
        functools.partial(backward_kernel, grid, units, ends.shape[1], sources, kvw, names),
        out_shape=[s for s, _ in outputs.values()] + [sds(u.shape(grid), BF16) for u in units],
        in_specs=[s for _, s in inputs.values()],
        out_specs=[s for _, s in outputs.values()] + [any_] * U,
        scratch_shapes=[pltpu.VMEM(s, BF16) for u in units for s in u.link_buffers(grid)[1:]]
        + [
            pltpu.VMEM((5,) + slot, BF16),
            pltpu.VMEM(slot, BF16),
            pltpu.VMEM((count, batches, 16, wide), BF16),
            pltpu.VMEM((batches, BLK // 16, 16, kvw), BF16),
            dma((U, 8)),
            dma((U, 8)),
            dma((U, 2)),
            dma((2, count - 1)),
            dma((2, count - 1)),
            dma((2,)),
            dma((2,)),
            dma((2,)),
            dma((16,)),
        ],
        compiler_params=pltpu.CompilerParams(collective_id=collective_id, has_side_effects=True, vmem_limit_bytes=VMEM),
        name="backward",
    )(*[v for v, _ in inputs.values()])
    found = dict(zip(outputs, results))
    return found["block_out"], found["grad_tokens"], results[: len(ARRAYS)]

def holders_of(perm, block):
    count = perm.shape[1]
    same = perm[:, None, None, :] == block[..., None]
    found = jnp.max(jnp.where(same, jnp.arange(count, dtype=jnp.int32), 0), axis=-1)
    return found.transpose(1, 0, 2).reshape(count, -1)


def fast_body(grid, tokens, w_query, w_keyval, w_out, w_gate, w_up, w_down, gain_attn, gain_ffn, cotangent, block_perm, extra_len):
    batches, _, rows, width = tokens.shape
    tok = batches * rows
    me = lax.axis_index(("dp", "fsdp"))
    count = lax.axis_size(("dp", "fsdp"))
    sources = WIN // BLK + 1
    kvw = w_keyval.shape[1]
    gains = jnp.stack([gain_attn, gain_ffn], axis=1)
    small = jnp.concatenate([w_keyval, jnp.pad(gains, ((0, 0), (0, 126)))], axis=1)
    sub = w_down.shape[0]
    half = w_gate.shape[1] // 2
    shards = [small, w_query, w_out, by_parity(w_gate, sub), by_parity(w_up, sub), w_down]
    units = [Unit(i, ALL, (0, s.shape[0]), (0, s.shape[1])) for i, s in enumerate(shards[:3])]
    for k in (0, 1):
        units += [Unit(i, COLS, (0, w_gate.shape[0]), (k * half // 2, half // 2)) for i in (3, 4)]
        units += [Unit(5, ROWS, (0, sub), (k * width // 2, width // 2))]
    lags = jnp.arange(sources, dtype=jnp.int32)
    index = holders_of(block_perm, jnp.maximum(block_perm[:, :, None] - (sources - 1) + lags, 0))
    start = lax.dynamic_slice_in_dim(block_perm, me, 1, axis=1)[:, 0] * BLK
    ends = jnp.cumsum(extra_len + (WIN - 1), axis=1).astype(jnp.int32)
    x = tokens.reshape(tok, width)
    dy = cotangent.reshape(tok, width)
    fulls, dy_pair, n2_pair, n1b, query, window, att, mixed, gains = forward(grid, shards, units, x, dy, start, ends, index, sources, kvw, 0)
    block = block_perm[:, :, None] + (sources - 1) - lags
    reader = holders_of(block_perm, jnp.minimum(block, count - 1))
    valid = (block < count).astype(jnp.int32).transpose(1, 0, 2).reshape(-1, batches * sources)
    saved = dict(n2=n2_pair, dy=dy_pair, n1=n1b, q=query, window=window, att=att, mixed=mixed, x=x, gains=gains)
    back = [Unit(i, ALL, (0, s.shape[0]), (c, min(width // 2, s.shape[1] - c))) for i, s in enumerate(shards[:3]) for c in range(0, s.shape[1], width // 2)]
    for k in range(3):
        back += [Unit(i, COLS, (0, w_gate.shape[0]), (k * half // 3, half // 3)) for i in (3, 4)]
        back += [Unit(5, ROWS, (0, sub), (k * width // 3, width // 3))]
    block_out, grad_tokens, grads = backward(
        grid, fulls, [s.shape for s in shards], saved, start, ends, reader, valid, back, sources, kvw, 1
    )
    small, dq, do, dg, du, dd = grads
    dg, du = from_parity(dg, sub), from_parity(du, sub)
    return (
        block_out.reshape(tokens.shape),
        grad_tokens.reshape(tokens.shape),
        dq,
        small[:, :kvw],
        do,
        dg,
        du,
        dd,
        small[:, kvw],
        small[:, kvw + 1],
    )


def by_parity(w, sub):
    rows, hidden = w.shape
    return w.reshape(rows, -1, 2, sub).transpose(2, 0, 1, 3).reshape(2, rows, hidden // 2)


def from_parity(w, sub):
    _, rows, part = w.shape
    return w.reshape(2, rows, -1, sub).transpose(1, 2, 0, 3).reshape(rows, 2 * part)


def solution(mesh):
    count = mesh.shape["dp"] * mesh.shape["fsdp"]
    grid = (2, 2, 2, mesh.shape["fsdp"])
    whole_tiles = mesh.shape["dp"] == 8 and 1536 % (16 * count) == 0
    run = functools.partial(fast_body, grid) if whole_tiles else body
    placed = (
        P(None, ("dp", "fsdp"), None, None),
        P(("dp", "fsdp"), None),
        P(("dp", "fsdp"), None),
        P(("dp", "fsdp"), None),
        P(("dp", "fsdp"), None),
        P(("dp", "fsdp"), None),
        P(("dp", "fsdp"), None),
        P(("dp", "fsdp")),
        P(("dp", "fsdp")),
        P(None, ("dp", "fsdp"), None, None),
        P(),
        P(),
    )
    return jax.shard_map(
        run,
        mesh=mesh,
        in_specs=placed,
        out_specs=(
            P(None, ("dp", "fsdp"), None, None),
            P(None, ("dp", "fsdp"), None, None),
            P(("dp", "fsdp"), None),
            P(("dp", "fsdp"), None),
            P(("dp", "fsdp"), None),
            P(("dp", "fsdp"), None),
            P(("dp", "fsdp"), None),
            P(("dp", "fsdp"), None),
            P(("dp", "fsdp")),
            P(("dp", "fsdp")),
        ),
        check_vma=False,
    )
```
